32 devices in a mesh: dp: 16 (over z, y, x), mp: 2 (over core).
Axes of the slice: x: 2, y: 2, z: 4, core: 2. Of those that a mesh axis runs over, the one named last changes fastest.
Arguments:
- inputs: bfloat16 [16, 1024, 1024], P('dp', 'mp'), may hold values from -6 to 6
- memory: bfloat16 [16, 384, 1024], P('dp'), may hold values from -6 to 6
- compressed_memory: bfloat16 [16, 512, 1024], P('dp'), may hold values from -6 to 6
- doc_starts: int32 [16, 4], P('dp'), may hold values from 0 to 991, as said below
- mem_valid: int32 [16], P('dp'), may hold values from 1 to 384
- cmem_valid: int32 [16], P('dp'), may hold values from 1 to 512
- gain_attn: float32 [1024], replicated, may hold values from 0.5 to 1.5
- w_qkv: bfloat16 [3, 1024, 1024], P(None, None, 'mp'), may hold values from -0.1875 to 0.1875
- slopes: float32 [8], P('mp'), may hold values from 0.00026041668 to 0.05
- w_out: bfloat16 [1024, 1024], P('mp'), may hold values from -1.5 to 1.5
- gain_ffn: float32 [1024], replicated, may hold values from 0.5 to 1.5
- w_up: bfloat16 [1024, 4096], P(None, 'mp'), may hold values from -0.1875 to 0.1875
- w_down: bfloat16 [4096, 1024], P('mp'), may hold values from -0.09375 to 0.09375
- w_comp: bfloat16 [3, 1024, 1024], P(None, None, 'mp'), may hold values from -0.109375 to 0.109375
- out_grad: bfloat16 [16, 1024, 1024], P('dp', 'mp'), may hold values from -6 to 6
- comp_grad: bfloat16 [16, 128, 1024], P('dp', None, 'mp'), may hold values from -6 to 6
Outputs:
- output: bfloat16 [16, 1024, 1024], P('dp', 'mp')
- compressed: bfloat16 [16, 128, 1024], P('dp', None, 'mp')
- input_grad: bfloat16 [16, 1024, 1024], P('dp', 'mp')
- gain_attn_grad: float32 [1024], replicated
- w_qkv_grad: float32 [3, 1024, 1024], P(None, 'dp', 'mp')
- slopes_grad: float32 [8], P('mp')
- w_out_grad: float32 [1024, 1024], P('mp', 'dp')
- gain_ffn_grad: float32 [1024], replicated
- w_up_grad: float32 [1024, 4096], P('dp', 'mp')
- w_down_grad: float32 [4096, 1024], P('mp', 'dp')
- w_comp_grad: float32 [3, 1024, 1024], P(None, 'dp', 'mp')
The draws below stay inside these ranges and needn't reach their ends.
Inputs may be any that keep to these rules, and one draw needn't show every extreme that they name: `doc_starts`: each row begins with 0 and rises strictly; the second document of each sequence starts below 512 and the third at or above it.
All inputs are finite; a program needn't handle non-finite values.
Results may differ from the reference program's by a relative error of at most 0.014.
Values may be sent and summed in bfloat16 or wider, within the bound.
No kernel may reach another device: no remote copies, remote signals or barrier semaphores. Data moves between devices by JAX's collectives and lax.ppermute only.
A program may use at most 256 MiB of HBM per device.

```python
import math
import jax
import jax.numpy as jnp
from jax import lax

D = 1024
H = 8
DH = 128
FF = 4096
LEN = 1024
MEM = 384
CMEM = 512
HDIM = 1024
KEYS = 1920
CROWS = 128
SEQS = 16


def draw_doc_starts(key, part):
    key = jax.random.fold_in(key, 11)
    split_keys = jax.random.split(key, 3)
    second = jax.random.randint(split_keys[0], (SEQS, 1), LEN // 16, 5 * LEN // 16)
    third = jax.random.randint(split_keys[1], (SEQS, 1), 10 * LEN // 16, 13 * LEN // 16)
    fourth = jax.random.randint(split_keys[2], (SEQS, 1), 27 * LEN // 32, 31 * LEN // 32)
    return jnp.concatenate([jnp.zeros((SEQS, 1), jnp.int32), second, third, fourth], axis=1).astype(jnp.int32)


def draw_mem_valid(key, part):
    key = jax.random.fold_in(key, 12)
    counts = jax.random.randint(key, (SEQS,), 1, MEM + 1)
    return counts.at[0].set(MEM).at[SEQS - 1].set(1).astype(jnp.int32)


def draw_cmem_valid(key, part):
    key = jax.random.fold_in(key, 13)
    counts = jax.random.randint(key, (SEQS,), 1, CMEM + 1)
    return counts.at[0].set(CMEM).at[SEQS - 1].set(1).astype(jnp.int32)


def shard_levels(own_key, dims, shards, least, largest):
    def one(position, parts):
        draws = jax.random.uniform(jax.random.fold_in(jax.random.fold_in(own_key, 6), position), (parts,), jnp.float32, least / len(shards), largest / len(shards))
        return jnp.repeat(jnp.exp(draws), dims[position] // parts).reshape((-1,) + (1,) * (len(dims) - position - 1))

    loudness = one(*shards[0])
    for cut in shards[1:]:
        loudness = loudness * one(*cut)
    return loudness


def normal_values(own_key, extent, deviation, reach, pieces=(), kind=jnp.bfloat16):
    values = deviation * jax.random.normal(own_key, extent, jnp.float32)
    if pieces:
        values = values * shard_levels(own_key, extent, pieces, -0.22, 0.18)
    return jnp.clip(values, -reach, reach).astype(kind)


def setup_inputs(seed: int = 0) -> dict:
    streams_of = jax.random.split(jax.random.key(seed), 17)
    return {
        "inputs": normal_values(streams_of[0], (SEQS, LEN, D), 1.0, 6.0, ((0, 16), (1, 2))),
        "memory": normal_values(streams_of[1], (SEQS, MEM, D), 1.0, 6.0, ((0, 16),)),
        "compressed_memory": normal_values(streams_of[2], (SEQS, CMEM, D), 1.0, 6.0, ((0, 16),)),
        "doc_starts": draw_doc_starts(jax.random.fold_in(streams_of[16], 71), 0),
        "mem_valid": draw_mem_valid(jax.random.fold_in(streams_of[16], 71), 0),
        "cmem_valid": draw_cmem_valid(jax.random.fold_in(streams_of[16], 71), 0),
        "gain_attn": jnp.clip(1.0 + 0.1 * jax.random.normal(streams_of[6], (D,), jnp.float32), 0.5, 1.5),
        "w_qkv": normal_values(streams_of[7], (3, D, HDIM), D ** -0.5, 0.1875, ((2, 2),)),
        "slopes": jnp.clip(jnp.exp(math.log(0.05) - 5.2574953 * jax.random.uniform(streams_of[8], (H,), jnp.float32) ** shard_levels(streams_of[8], (H,), ((0, 2),), -0.2, 0.2)), 0.00026041668, 0.05),
        "w_out": normal_values(streams_of[9], (HDIM, D), (HDIM // 64) ** -0.5, 1.5, ((0, 2),)),
        "gain_ffn": jnp.clip(1.0 + 0.1 * jax.random.normal(streams_of[10], (D,), jnp.float32), 0.5, 1.5),
        "w_up": normal_values(streams_of[11], (D, FF), D ** -0.5, 0.1875, ((1, 2),)),
        "w_down": normal_values(streams_of[12], (FF, D), FF ** -0.5, 0.09375, ((0, 2),)),
        "w_comp": normal_values(streams_of[13], (3, D, D), (3 * D) ** -0.5, 0.109375, ((2, 2),)),
        "out_grad": normal_values(streams_of[14], (SEQS, LEN, D), 1.0, 6.0, ((0, 16), (1, 2))),
        "comp_grad": normal_values(streams_of[15], (SEQS, CROWS, D), 1.0, 6.0, ((0, 16), (2, 2))),
    }


@jax.custom_vjp
def low(v):
    return lax.optimization_barrier(v.astype(jnp.bfloat16)).astype(jnp.float32)

@jax.custom_vjp
def low_back(v):
    return v

def low_keep(v):
    return (low(v), None)

def low_pass(kept, grad):
    return (grad,)

def back_keep(v):
    return (v, None)

def back_low(kept, grad):
    return (low(grad),)
low.defvjp(low_keep, low_pass)
low_back.defvjp(back_keep, back_low)

def matmul(left, right):
    return jnp.dot(left, right, precision=lax.Precision.HIGHEST)

def layer_norm(rows, gain):
    centre = lax.optimization_barrier(jnp.mean(rows, axis=-1, keepdims=True))
    centred = rows - centre
    spread = lax.optimization_barrier(jnp.mean(centred * centred, axis=-1, keepdims=True))
    return centred * lax.rsqrt(spread + 1e-05) * gain

def gelu_exact(values_in):
    return jax.nn.gelu(values_in, approximate=False)

def visibility(query_pos, starts, mem_len, cmem_len, seq_len, mem_rows, cmem_rows):
    key_tokens = jnp.arange(seq_len, dtype=jnp.int32)
    doc_query = lax.optimization_barrier(jnp.sum((query_pos[:, None] >= starts[None, :]).astype(jnp.int32), axis=1))
    doc_key = lax.optimization_barrier(jnp.sum((key_tokens[:, None] >= starts[None, :]).astype(jnp.int32), axis=1))
    see_tokens = (key_tokens[None, :] <= query_pos[:, None]) & (doc_key[None, :] == doc_query[:, None])
    first_doc = (doc_query == 1)[:, None]
    cmem_index = jnp.arange(cmem_rows, dtype=jnp.int32)
    mem_index = jnp.arange(mem_rows, dtype=jnp.int32)
    see_cmem = first_doc & (cmem_index >= cmem_rows - cmem_len)[None, :]
    see_mem = first_doc & (mem_index >= mem_rows - mem_len)[None, :]
    visible = jnp.concatenate([see_cmem, see_mem, see_tokens], axis=1)
    key_pos = jnp.concatenate([-mem_rows - 3 * (cmem_rows - cmem_index), mem_index - mem_rows, key_tokens])
    distance = (query_pos[:, None] - key_pos[None, :]).astype(jnp.float32)
    return (visible, distance)

def attend_block(start, queries, keys_all, values_all, slopes, starts, mem_len, cmem_len):
    block_rows = min(512, LEN)
    query_pos = start + jnp.arange(block_rows, dtype=jnp.int32)
    visible, distance = visibility(query_pos, starts, mem_len, cmem_len, LEN, MEM, CMEM)
    query_block = lax.dynamic_slice_in_dim(queries, start, block_rows, 0)
    raw = jnp.einsum('qhd,khd->hqk', query_block, keys_all, precision=lax.Precision.HIGHEST) * DH ** (-0.5)
    raw = raw - slopes[:, None, None] * distance[None]
    scores = jnp.where(visible[None], low_back(raw), -1e+30)
    probs = low(jax.nn.softmax(scores, axis=-1))
    return jnp.einsum('hqk,khd->qhd', probs, values_all, precision=lax.Precision.HIGHEST)

def sequence_pass(params, x_rows, mem_rows, cmem_rows, starts, mem_len, cmem_len):
    gain_attn, w_qkv, slopes, w_out, gain_ffn, w_up, w_down, w_comp = params
    normed = low(layer_norm(x_rows, gain_attn))
    context = jnp.concatenate([low(layer_norm(cmem_rows, gain_attn)), low(layer_norm(mem_rows, gain_attn)), normed], 0)
    queries = low(low_back(matmul(normed, w_qkv[0]))).reshape(LEN, H, DH)
    keys_all = low(low_back(matmul(context, w_qkv[1]))).reshape(KEYS, H, DH)
    values_all = low(low_back(matmul(context, w_qkv[2]))).reshape(KEYS, H, DH)
    block_rows = min(512, LEN)
    attend = jax.checkpoint(attend_block)
    block_starts = jnp.arange(LEN // block_rows, dtype=jnp.int32) * block_rows
    attended = lax.map(lambda start: attend(start, queries, keys_all, values_all, slopes, starts, mem_len, cmem_len), block_starts)
    attended = low(low_back(attended.reshape(LEN, H * DH)))
    middle = x_rows + low_back(matmul(attended, w_out))
    normed_ffn = low(layer_norm(middle, gain_ffn))
    pre_act = low_back(matmul(normed_ffn, w_up))
    hidden = low(gelu_exact(pre_act))
    result = middle + low_back(matmul(hidden, w_down))
    compressed = matmul(mem_rows.reshape(MEM // 3, 3 * D), w_comp.reshape(3 * D, D))
    return (result, compressed)

def reference(inputs, memory, compressed_memory, doc_starts, mem_valid, cmem_valid, gain_attn, w_qkv, slopes, w_out, gain_ffn, w_up, w_down, w_comp, out_grad, comp_grad):
    params = (gain_attn.astype(jnp.float32), w_qkv.astype(jnp.float32), slopes.astype(jnp.float32), w_out.astype(jnp.float32), gain_ffn.astype(jnp.float32), w_up.astype(jnp.float32), w_down.astype(jnp.float32), w_comp.astype(jnp.float32))
    mem_float = memory.astype(jnp.float32)
    cmem_float = compressed_memory.astype(jnp.float32)

    def forward(x_all, params_in):
        one_seq = jax.checkpoint(sequence_pass)
        return lax.map(lambda seq_item: one_seq(params_in, *seq_item), (x_all, mem_float, cmem_float, doc_starts, mem_valid, cmem_valid))
    outputs, pullback = jax.vjp(forward, inputs.astype(jnp.float32), params)
    grad_x, grad_params = pullback((out_grad.astype(jnp.float32), comp_grad.astype(jnp.float32)))
    return (outputs[0].astype(jnp.bfloat16), outputs[1].astype(jnp.bfloat16), grad_x.astype(jnp.bfloat16), grad_params[0], grad_params[1], grad_params[2], grad_params[3], grad_params[4], grad_params[5], grad_params[6], grad_params[7])
```

```python
from functools import partial

import jax
import jax.numpy as jnp
from jax import lax
from jax.sharding import PartitionSpec as P


def normalize(rows, gain):
    centre = jnp.mean(rows, axis=-1, keepdims=True)
    centred = rows - centre
    spread = jnp.mean(centred * centred, axis=-1, keepdims=True)
    return centred * lax.rsqrt(spread + 1e-05) * gain


def gelu_exact(values_in):
    return jax.nn.gelu(values_in, approximate=False)


def visibility(query_pos, starts, mem_len, cmem_len, seq_len, mem_rows, cmem_rows):
    key_tokens = jnp.arange(seq_len, dtype=jnp.int32)
    doc_query = jnp.sum((query_pos[:, None] >= starts[None, :]).astype(jnp.int32), axis=1)
    doc_key = jnp.sum((key_tokens[:, None] >= starts[None, :]).astype(jnp.int32), axis=1)
    see_tokens = (key_tokens[None, :] <= query_pos[:, None]) & (
        doc_key[None, :] == doc_query[:, None]
    )
    first_doc = (doc_query == 1)[:, None]
    cmem_index = jnp.arange(cmem_rows, dtype=jnp.int32)
    mem_index = jnp.arange(mem_rows, dtype=jnp.int32)
    see_cmem = first_doc & (cmem_index >= cmem_rows - cmem_len)[None, :]
    see_mem = first_doc & (mem_index >= mem_rows - mem_len)[None, :]
    visible = jnp.concatenate([see_cmem, see_mem, see_tokens], axis=1)
    key_pos = jnp.concatenate(
        [-mem_rows - 3 * (cmem_rows - cmem_index), mem_index - mem_rows, key_tokens]
    )
    distance = (query_pos[:, None] - key_pos[None, :]).astype(jnp.float32)
    return (visible, distance)


def swap_mp(rows):
    return lax.ppermute(rows, "mp", [(0, 1), (1, 0)])


def gather_mp(rows):
    other = swap_mp(rows)
    full = jnp.concatenate([rows, other], axis=0)
    return jnp.roll(full, lax.axis_index("mp") * rows.shape[0], axis=0)


def scatter_mp(rows):
    half = rows.shape[0] // 2
    me = lax.axis_index("mp")
    send = lax.dynamic_slice_in_dim(rows, (1 - me) * half, half, 0)
    keep = lax.dynamic_slice_in_dim(rows, me * half, half, 0)
    got = swap_mp(send.astype(jnp.bfloat16))
    return keep.astype(jnp.float32) + got.astype(jnp.float32)


def scatter_dp(blocks, order):
    n = lax.axis_size("dp")
    bits = n.bit_length() - 1
    me = lax.axis_index("dp")
    rows, cols = blocks.shape
    x = blocks.astype(jnp.bfloat16).reshape((2,) * bits + (rows // n, cols))
    left = list(range(bits - 1, -1, -1))
    for step, bit in enumerate(order):
        axis = left.index(bit)
        left.remove(bit)
        mine = (me >> bit) & 1
        send = lax.dynamic_index_in_dim(x, 1 - mine, axis, keepdims=False)
        keep = lax.dynamic_index_in_dim(x, mine, axis, keepdims=False)
        got = lax.ppermute(send, "dp", [(i, i ^ (1 << bit)) for i in range(n)])
        x = keep.astype(jnp.float32) + got.astype(jnp.float32)
        if step < bits - 1:
            x = x.astype(jnp.bfloat16)
    return x.reshape(rows // n, cols)


def sum_all(vector, axes):
    for axis in axes:
        n = lax.axis_size(axis)
        for bit in range(n.bit_length() - 1):
            vector = vector + lax.ppermute(vector, axis, [(i, i ^ (1 << bit)) for i in range(n)])
    return vector


def order_from(first):
    bits = lax.axis_size("dp").bit_length() - 1
    return [(first + k) % bits for k in range(bits)]


def shards(
    inputs,
    memory,
    compressed_memory,
    doc_starts,
    mem_valid,
    cmem_valid,
    gain_attn,
    w_qkv,
    slopes,
    w_out,
    gain_ffn,
    w_up,
    w_down,
    w_comp,
    out_grad,
    comp_grad,
):
    x_float = inputs[0].astype(jnp.float32)
    starts = doc_starts[0]
    mem_len = mem_valid[0]
    cmem_len = cmem_valid[0]
    mem_float = memory[0].astype(jnp.float32)
    cmem_float = compressed_memory[0].astype(jnp.float32)
    mem_rows = memory.shape[1]
    cmem_rows = compressed_memory.shape[1]
    mem_total = mem_rows + cmem_rows
    width = inputs.shape[2]
    normed_local = normalize(x_float, gain_attn)
    normed = gather_mp(normed_local.astype(jnp.bfloat16))
    seq_len = normed.shape[0]
    context = jnp.concatenate(
        [
            normalize(cmem_float, gain_attn).astype(jnp.bfloat16),
            normalize(mem_float, gain_attn).astype(jnp.bfloat16),
            normed,
        ],
        axis=0,
    )
    keys_len = context.shape[0]
    heads = slopes.shape[0]
    head_dim = w_qkv.shape[2] // heads
    scale = head_dim ** (-0.5)
    queries = (
        jnp.dot(normed, w_qkv[0], preferred_element_type=jnp.float32)
        .astype(jnp.bfloat16)
        .reshape(seq_len, heads, head_dim)
    )
    keys_all = (
        jnp.dot(context, w_qkv[1], preferred_element_type=jnp.float32)
        .astype(jnp.bfloat16)
        .reshape(keys_len, heads, head_dim)
    )
    values_all = (
        jnp.dot(context, w_qkv[2], preferred_element_type=jnp.float32)
        .astype(jnp.bfloat16)
        .reshape(keys_len, heads, head_dim)
    )
    block_rows = min(512, seq_len)
    block_starts = jnp.arange(seq_len // block_rows, dtype=jnp.int32) * block_rows

    def scores_of(start):
        query_pos = start + jnp.arange(block_rows, dtype=jnp.int32)
        visible, distance = visibility(
            query_pos, starts, mem_len, cmem_len, seq_len, mem_rows, cmem_rows
        )
        query_block = lax.dynamic_slice_in_dim(queries, start, block_rows, 0)
        raw = (
            jnp.einsum("qhd,khd->hqk", query_block, keys_all, preferred_element_type=jnp.float32)
            * scale
        )
        raw = raw - slopes[:, None, None] * distance[None]
        return (jnp.where(visible[None], raw, -1e30), query_block, distance)

    def forward_block(start):
        scores, query_block, distance = scores_of(start)
        row_max = jnp.max(scores, axis=-1, keepdims=True)
        exp_terms = jnp.exp(scores - row_max)
        row_total = jnp.sum(exp_terms, axis=-1, keepdims=True)
        weights_low = (exp_terms / row_total).astype(jnp.bfloat16)
        block_out = jnp.einsum(
            "hqk,khd->qhd", weights_low, values_all, preferred_element_type=jnp.float32
        ).astype(jnp.bfloat16)
        return (block_out, (row_max + jnp.log(row_total))[..., 0])

    attended, log_totals = lax.map(forward_block, block_starts)
    attended = attended.reshape(seq_len, heads * head_dim)
    attn_part = jnp.dot(attended, w_out, preferred_element_type=jnp.float32)
    attn_total = scatter_mp(attn_part)
    middle = x_float + attn_total
    normed_ffn_local = normalize(middle, gain_ffn)
    normed_ffn = gather_mp(normed_ffn_local.astype(jnp.bfloat16))
    pre_act = jnp.dot(normed_ffn, w_up, preferred_element_type=jnp.float32)
    hidden = gelu_exact(pre_act).astype(jnp.bfloat16)
    ffn_part = jnp.dot(hidden, w_down, preferred_element_type=jnp.float32)
    ffn_total = scatter_mp(ffn_part)
    result = (middle + ffn_total).astype(jnp.bfloat16)
    mem_groups = memory[0].reshape(mem_rows // 3, 3 * width)
    compressed = jnp.dot(
        mem_groups, w_comp.reshape(3 * width, w_comp.shape[2]), preferred_element_type=jnp.float32
    ).astype(jnp.bfloat16)
    grad_rows = gather_mp(out_grad[0])
    grad_hidden = jnp.einsum("le,fe->lf", grad_rows, w_down, preferred_element_type=jnp.float32)
    _, gelu_back = jax.vjp(gelu_exact, pre_act)
    grad_pre = gelu_back(grad_hidden)[0].astype(jnp.bfloat16)
    grad_down = jnp.einsum("lf,le->ef", hidden, grad_rows, preferred_element_type=jnp.float32)
    grad_up = jnp.einsum("ld,lf->df", normed_ffn, grad_pre, preferred_element_type=jnp.float32)
    grad_up_part, grad_down_part = (
        scatter_dp(grad_up, order_from(0)),
        scatter_dp(grad_down, order_from(1)).T,
    )
    grad_normed_ffn = scatter_mp(
        jnp.einsum("lf,df->ld", grad_pre, w_up, preferred_element_type=jnp.float32)
    )
    _, ffn_norm_back = jax.vjp(normalize, middle, gain_ffn)
    grad_middle_norm, grad_gain_ffn = ffn_norm_back(grad_normed_ffn)
    grad_middle = out_grad[0].astype(jnp.float32) + grad_middle_norm
    grad_attn_rows = gather_mp(grad_middle.astype(jnp.bfloat16))
    grad_out = jnp.einsum("lh,le->eh", attended, grad_attn_rows, preferred_element_type=jnp.float32)
    grad_attended = (
        jnp.einsum("le,he->lh", grad_attn_rows, w_out, preferred_element_type=jnp.float32)
        .astype(jnp.bfloat16)
        .reshape(seq_len, heads, head_dim)
    )

    def backward_block(carry, block_item):
        grad_keys, grad_values, grad_slopes = carry
        start, block_log_total = block_item
        scores, query_block, distance = scores_of(start)
        weights_full = jnp.exp(scores - block_log_total[..., None])
        grad_block = lax.dynamic_slice_in_dim(grad_attended, start, block_rows, 0)
        grad_weights = jnp.einsum(
            "qhd,khd->hqk", grad_block, values_all, preferred_element_type=jnp.float32
        )
        row_inner = jnp.sum(weights_full * grad_weights, axis=-1, keepdims=True)
        grad_scores = (weights_full * (grad_weights - row_inner)).astype(jnp.bfloat16)
        grad_slopes = grad_slopes - jnp.sum(
            grad_scores.astype(jnp.float32) * distance[None], axis=(1, 2)
        )
        grad_query = (
            jnp.einsum("hqk,khd->qhd", grad_scores, keys_all, preferred_element_type=jnp.float32)
            * scale
        )
        grad_keys = (
            grad_keys
            + jnp.einsum(
                "hqk,qhd->khd", grad_scores, query_block, preferred_element_type=jnp.float32
            )
            * scale
        )
        grad_values = grad_values + jnp.einsum(
            "hqk,qhd->khd",
            weights_full.astype(jnp.bfloat16),
            grad_block,
            preferred_element_type=jnp.float32,
        )
        return ((grad_keys, grad_values, grad_slopes), grad_query.astype(jnp.bfloat16))

    zero_keys = jnp.zeros((keys_len, heads, head_dim), jnp.float32)
    carried, grad_queries = lax.scan(
        backward_block,
        (zero_keys, zero_keys, jnp.zeros((heads,), jnp.float32)),
        (block_starts, log_totals),
    )
    grad_keys_low = carried[0].astype(jnp.bfloat16).reshape(keys_len, heads * head_dim)
    grad_values_low = carried[1].astype(jnp.bfloat16).reshape(keys_len, heads * head_dim)
    grad_slopes = carried[2]
    grad_queries = grad_queries.reshape(seq_len, heads * head_dim)
    grad_qkv = (
            jnp.einsum("ld,lh->dh", normed, grad_queries, preferred_element_type=jnp.float32),
            jnp.einsum("ld,lh->dh", context, grad_keys_low, preferred_element_type=jnp.float32),
            jnp.einsum("ld,lh->dh", context, grad_values_low, preferred_element_type=jnp.float32),
        )
    grad_context = jnp.einsum(
        "lh,dh->ld", grad_keys_low, w_qkv[1], preferred_element_type=jnp.float32
    ) + jnp.einsum("lh,dh->ld", grad_values_low, w_qkv[2], preferred_element_type=jnp.float32)
    grad_normed_part = (
        jnp.einsum("lh,dh->ld", grad_queries, w_qkv[0], preferred_element_type=jnp.float32)
        + grad_context[mem_total:]
    )
    grad_normed = scatter_mp(grad_normed_part)
    _, attn_norm_back = jax.vjp(normalize, x_float, gain_attn)
    grad_x_norm, grad_gain_tokens = attn_norm_back(grad_normed)
    grad_inputs = (grad_middle + grad_x_norm).astype(jnp.bfloat16)
    _, cmem_norm_back = jax.vjp(partial(normalize, cmem_float), gain_attn)
    _, mem_norm_back = jax.vjp(partial(normalize, mem_float), gain_attn)
    grad_gain_attn = (
        grad_gain_tokens
        + cmem_norm_back(grad_context[:cmem_rows])[0]
        + mem_norm_back(grad_context[cmem_rows:mem_total])[0]
    )
    groups = mem_groups.reshape(mem_rows // 3, 3, width)
    grad_comp = [
        jnp.einsum("id,ie->de", groups[:, r], comp_grad[0], preferred_element_type=jnp.float32)
        for r in range(3)
    ]
    grad_comp_part = jnp.stack(
        [scatter_dp(part, order_from(r)) for r, part in enumerate(grad_comp)]
    )
    grad_qkv_part = jnp.stack([scatter_dp(part, order_from(r)) for r, part in enumerate(grad_qkv)])
    grad_out_part = scatter_dp(grad_out, order_from(2)).T
    slopes_total = sum_all(grad_slopes, ("dp",))
    gain_attn_total, gain_ffn_total = sum_all(
        jnp.stack([grad_gain_attn, grad_gain_ffn]), ("mp", "dp")
    )
    return (
        result[None],
        compressed[None],
        grad_inputs[None],
        gain_attn_total,
        grad_qkv_part,
        slopes_total,
        grad_out_part,
        gain_ffn_total,
        grad_up_part,
        grad_down_part,
        grad_comp_part,
    )


def solution(mesh):
    placed = (
        P("dp", "mp", None),
        P("dp", None, None),
        P("dp", None, None),
        P("dp", None),
        P("dp"),
        P("dp"),
        P(),
        P(None, None, "mp"),
        P("mp"),
        P("mp", None),
        P(),
        P(None, "mp"),
        P("mp", None),
        P(None, None, "mp"),
        P("dp", "mp", None),
        P("dp", None, "mp"),
    )
    return jax.shard_map(
        shards,
        mesh=mesh,
        in_specs=placed,
        out_specs=(
            P("dp", "mp", None),
            P("dp", None, "mp"),
            P("dp", "mp", None),
            P(),
            P(None, "dp", "mp"),
            P("mp"),
            P("mp", "dp"),
            P(),
            P("dp", "mp"),
            P("mp", "dp"),
            P(None, "dp", "mp"),
        ),
        check_vma=False,
    )
```

```python
from functools import partial

import jax
import jax.numpy as jnp
from jax import lax
from jax.experimental import pallas as pl
from jax.experimental.pallas import tpu as pltpu
from jax.sharding import PartitionSpec as P

F32, BF16 = jnp.float32, jnp.bfloat16
VMEM_LIMIT = 60 * 1024 * 1024
HEAD = 128
TILE = 256
LOG2E = 1.4426950408889634
HIDE = -1e30


def dot(a, b):
    return jnp.dot(a, b, preferred_element_type=F32)


def dot_nt(a, b):
    return lax.dot_general(a, b, (((1,), (1,)), ((), ())), preferred_element_type=F32)


def shape(dims, kind=BF16):
    return jax.ShapeDtypeStruct(dims, kind)


def whole(dims):
    return pl.BlockSpec(dims, lambda *_: (0,) * len(dims))


def call(body, out_shape, in_specs, out_specs, grid=(1,), scratch=(), scalars=1, flops=0, moved=0):
    return pl.pallas_call(
        body,
        grid_spec=pltpu.PrefetchScalarGridSpec(
            num_scalar_prefetch=scalars,
            grid=grid,
            in_specs=in_specs,
            out_specs=out_specs,
            scratch_shapes=scratch,
        ),
        out_shape=out_shape,
        compiler_params=pltpu.CompilerParams(vmem_limit_bytes=VMEM_LIMIT),
        cost_estimate=pl.CostEstimate(flops=flops, bytes_accessed=moved, transcendentals=0),
    )


def put_blocks(me, order, result, send, keep):
    half, rows = send.shape[0], send.shape[1]
    bits = len(order)
    for place in range(2 * half):
        rel = 0
        for k, bit in enumerate(order):
            rel |= ((place >> (bits - 1 - k)) & 1) << bit
        start = pl.multiple_of((me ^ rel) * rows, rows)
        out = send if place >= half else keep
        out[place % half] = result[pl.ds(start, rows), :]


def layer_norm(rows, gain):
    centre = jnp.mean(rows, axis=-1, keepdims=True)
    centred = rows - centre
    spread = jnp.mean(centred * centred, axis=-1, keepdims=True)
    return centred * lax.rsqrt(spread + 1e-05) * gain


def layer_norm_back(rows, gain, grad):
    centre = jnp.mean(rows, axis=-1, keepdims=True)
    centred = rows - centre
    spread = jnp.mean(centred * centred, axis=-1, keepdims=True)
    inverse = lax.rsqrt(spread + 1e-05)
    unit = centred * inverse
    pulled = grad * gain
    return inverse * (
        pulled
        - jnp.mean(pulled, axis=-1, keepdims=True)
        - unit * jnp.mean(pulled * unit, axis=-1, keepdims=True)
    )


def gelu_parts(u):
    bell = jnp.exp2(u * u * (-0.5 * LOG2E))
    t = 1.0 / (1.0 + (0.3275911 * 0.7071067811865476) * jnp.abs(u))
    series = 0.7107068705 + t * (-0.7265760135 + t * 0.5307027145)
    tail = t * (0.127414796 + t * (-0.142248368 + t * series)) * bell
    return jnp.where(u >= 0, 1.0 - tail, tail), u * bell * 0.3989422804014327


def comp_body(orders, me_ref, mem_ref, w_ref, grad_ref, out_ref, *rest):
    outs, (wide, res) = rest[:-2], rest[-2:]
    count = out_ref.shape[0]
    groups = mem_ref.shape[1] // HEAD
    for c in range(groups):
        wide[pl.ds(c * 3 * count, 3 * count), :] = mem_ref[:, c * HEAD : (c + 1) * HEAD].astype(F32)
    total = None
    for r in range(3):
        rows = jnp.concatenate([wide[pl.ds(c * 3 * count + r, count, stride=3), :] for c in range(groups)], axis=1)
        part = dot(rows.astype(BF16), w_ref[r])
        total = part if total is None else total + part
        res[...] = dot(rows.T.astype(BF16), grad_ref[...]).astype(BF16)
        put_blocks(me_ref[0], orders[r], res, outs[2 * r], outs[2 * r + 1])
    out_ref[...] = total.astype(BF16)


def comp_call(me, memory, w_comp, comp_grad, n, orders):
    rows, width = memory.shape
    cols = w_comp.shape[2]
    piece = (n // 2, width // n, cols)
    return call(
        partial(comp_body, orders),
        [shape((rows // 3, cols))] + [shape(piece)] * 6,
        [whole(memory.shape), whole(w_comp.shape), whole(comp_grad.shape)],
        [whole((rows // 3, cols))] + [whole(piece)] * 6,
        scratch=[pltpu.VMEM((rows * width // HEAD, HEAD), F32), pltpu.VMEM((width, cols), BF16)],
        flops=4 * rows * width * cols,
        moved=9 * width * cols * 2,
    )(me, memory, w_comp, comp_grad)


def context_body(_, x_ref, gain_ref, w_ref, nt_ref, k_ref, kt_ref, v_ref, vt_ref):
    normed = layer_norm(x_ref[...].astype(F32), gain_ref[...]).astype(BF16)
    nt_ref[...] = normed.T
    for which, out, flipped in ((1, k_ref, kt_ref), (2, v_ref, vt_ref)):
        low = dot(normed, w_ref[which]).astype(BF16)
        out[...] = low
        flipped[...] = low.T


def context_call(me, rows, gain, w_qkv, tile):
    count, width = rows.shape
    cols = w_qkv.shape[2]
    return call(
        context_body,
        [shape((width, count))] + [shape((count, cols)), shape((cols, count))] * 2,
        [
            pl.BlockSpec((tile, width), lambda i, _: (i, 0)),
            whole(gain.shape),
            whole(w_qkv.shape),
        ],
        [pl.BlockSpec((width, tile), lambda i, _: (0, i))]
        + [
            pl.BlockSpec((tile, cols), lambda i, _: (i, 0)),
            pl.BlockSpec((cols, tile), lambda i, _: (0, i)),
        ]
        * 2,
        grid=(count // tile,),
        flops=4 * count * width * cols,
        moved=3 * width * cols * 2 + count * (2 * width + 4 * cols) * 2,
    )(me, rows, gain, w_qkv)


def tokens_body(tiles, me_ref, own_ref, other_ref, gain_ref, w_ref, x_ref, nt_ref, q_ref, k_ref, kt_ref, v_ref, vt_ref):
    mine = pl.program_id(0) // tiles == me_ref[1]
    low_x = jnp.where(mine, own_ref[...], other_ref[...])
    x_ref[...] = low_x
    normed = layer_norm(low_x.astype(F32), gain_ref[...]).astype(BF16)
    nt_ref[...] = normed.T
    q_ref[...] = dot(normed, w_ref[0]).astype(BF16)
    for which, out, flipped in ((1, k_ref, kt_ref), (2, v_ref, vt_ref)):
        low = dot(normed, w_ref[which]).astype(BF16)
        out[...] = low
        flipped[...] = low.T


def tokens_call(me, own, other, gain, w_qkv, tile):
    half, width = own.shape
    count = 2 * half
    cols = w_qkv.shape[2]
    tiles = half // tile
    side = pl.BlockSpec((tile, width), lambda i, _: (i % tiles, 0))
    tall = pl.BlockSpec((tile, cols), lambda i, _: (i, 0))
    flat = pl.BlockSpec((cols, tile), lambda i, _: (0, i))
    return call(
        partial(tokens_body, tiles),
        [shape((count, width)), shape((width, count)), shape((count, cols))]
        + [shape((count, cols)), shape((cols, count))] * 2,
        [side, side, whole(gain.shape), whole(w_qkv.shape)],
        [
            pl.BlockSpec((tile, width), lambda i, _: (i, 0)),
            pl.BlockSpec((width, tile), lambda i, _: (0, i)),
            tall,
        ]
        + [tall, flat] * 2,
        grid=(count // tile,),
        flops=6 * count * width * cols,
        moved=3 * width * cols * 2 + count * (4 * width + 5 * cols) * 2,
    )(me, own, other, gain, w_qkv)


def flip_body(tiles, me_ref, own_ref, other_ref, x_ref, xt_ref):
    mine = pl.program_id(0) // tiles == me_ref[1]
    low = jnp.where(mine, own_ref[...], other_ref[...])
    x_ref[...] = low
    xt_ref[...] = low.T


def flip_call(me, own, other, tile):
    half, width = own.shape
    tiles = half // tile
    side = pl.BlockSpec((tile, width), lambda i, _: (i % tiles, 0))
    return call(
        partial(flip_body, tiles),
        [shape((2 * half, width)), shape((width, 2 * half))],
        [side, side],
        [
            pl.BlockSpec((tile, width), lambda i, _: (i, 0)),
            pl.BlockSpec((width, tile), lambda i, _: (0, i)),
        ],
        grid=(2 * tiles,),
        moved=12 * half * width,
    )(me, own, other)


def query_limits(places, docs_ref):
    count = docs_ref.shape[1]
    first = jnp.zeros_like(places)
    for d in range(1, count):
        first = jnp.where(places >= docs_ref[0, d], docs_ref[0, d], first)
    return first


def first_key(place, docs_ref):
    first = 0
    for d in range(1, docs_ref.shape[1]):
        first = jnp.where(place >= docs_ref[0, d], docs_ref[0, d], first)
    return first


def attend_loops(q0, docs_ref, valid_ref, cmem, mem, step_keys, step, token_step):
    total = cmem + mem
    any_first = q0 < docs_ref[0, 1]

    @pl.when(any_first)
    def _():
        def one_cmem(i, _):
            start = pl.multiple_of(i * step_keys, step_keys)
            step(start, cmem - valid_ref[1], 3, -mem - 3 * cmem)
            return 0

        lax.fori_loop((cmem - valid_ref[1]) // step_keys, cmem // step_keys, one_cmem, 0)

        def one_mem(i, _):
            start = pl.multiple_of(i * step_keys, step_keys)
            step(start, total - valid_ref[0], 1, -total)
            return 0

        lax.fori_loop((total - valid_ref[0]) // step_keys, total // step_keys, one_mem, 0)

    def one_token(i, _):
        token_step(pl.multiple_of(i * TILE, TILE))
        return 0

    lax.fori_loop(first_key(q0, docs_ref) // TILE, (q0 + TILE) // TILE, one_token, 0)


def forward_body(
    cmem, mem, me_ref, docs_ref, valid_ref, slopes_ref, q_ref, k_ref, vt_ref, kc_ref, vct_ref, w_ref,
    att_ref, part_ref, ot_ref, lse_ref, top_ref, sum_ref, acc_ref,
):
    heads = slopes_ref.shape[0]
    scale = HEAD**-0.5
    power = scale * LOG2E
    q0 = pl.program_id(0) * TILE
    places = q0 + lax.broadcasted_iota(jnp.int32, (1, TILE), 1)
    first = query_limits(places, docs_ref)
    top_ref[...] = jnp.full(top_ref.shape, HIDE, F32)
    sum_ref[...] = jnp.zeros(sum_ref.shape, F32)
    acc_ref[...] = jnp.zeros(acc_ref.shape, F32)

    def block(keys, values, place, visible):
        for h in range(heads):
            cols = slice(h * HEAD, (h + 1) * HEAD)
            scores = dot_nt(keys(cols), q_ref[:, cols])
            scores = scores + place * (slopes_ref[h] / scale)
            scores = jnp.where(visible, scores, HIDE)
            old = top_ref[h : h + 1, :]
            new = jnp.maximum(old, jnp.max(scores, axis=0, keepdims=True))
            probs = jnp.exp2((scores - new) * power)
            fade = jnp.exp2((old - new) * power)
            top_ref[h : h + 1, :] = new
            sum_ref[h : h + 1, :] = sum_ref[h : h + 1, :] * fade + jnp.sum(probs, axis=0, keepdims=True)
            acc_ref[cols, :] = acc_ref[cols, :] * fade + dot(values(cols), probs.astype(BF16))

    def step(start, least, stride, offset):
        index = start + lax.broadcasted_iota(jnp.int32, (HEAD, 1), 0)
        visible = (index >= least) & (places < docs_ref[0, 1])
        block(
            lambda cols: kc_ref[pl.ds(start, HEAD), cols],
            lambda cols: vct_ref[cols, pl.ds(start, HEAD)],
            (index * stride + offset).astype(F32),
            visible,
        )

    def token_step(start):
        index = start + lax.broadcasted_iota(jnp.int32, (TILE, 1), 0)
        visible = (index >= first) & (index <= places)
        block(
            lambda cols: k_ref[pl.ds(start, TILE), cols],
            lambda cols: vt_ref[cols, pl.ds(start, TILE)],
            index.astype(F32),
            visible,
        )

    attend_loops(q0, docs_ref, valid_ref, cmem, mem, HEAD, step, token_step)
    for h in range(heads):
        cols = slice(h * HEAD, (h + 1) * HEAD)
        total = sum_ref[h : h + 1, :]
        out = acc_ref[cols, :] * (1.0 / total)
        ot_ref[cols, :] = out
        att_ref[:, cols] = out.T.astype(BF16)
        lse_ref[h : h + 1, :] = top_ref[h : h + 1, :] * power + jnp.log2(total)
    part_ref[...] = dot(att_ref[...], w_ref[...]).astype(BF16)


def forward_call(me, docs, valid, slopes, q, k, vt, kc, vct, w_out, cmem, mem):
    count, cols = q.shape
    width = w_out.shape[1]
    heads = slopes.shape[0]
    tall = pl.BlockSpec((TILE, cols), lambda i, *_: (i, 0))
    return call(
        partial(forward_body, cmem, mem),
        [shape((count, cols)), shape((count, width)), shape((cols, count), F32), shape((heads, count), F32)],
        [tall, whole(k.shape), whole(vt.shape), whole(kc.shape), whole(vct.shape), whole(w_out.shape)],
        [
            tall,
            pl.BlockSpec((TILE, width), lambda i, *_: (i, 0)),
            pl.BlockSpec((cols, TILE), lambda i, *_: (0, i)),
            pl.BlockSpec((heads, TILE), lambda i, *_: (0, i)),
        ],
        grid=(count // TILE,),
        scratch=[pltpu.VMEM((heads, TILE), F32), pltpu.VMEM((heads, TILE), F32), pltpu.VMEM((cols, TILE), F32)],
        scalars=4,
        flops=count * cols * (count + 2 * width),
        moved=(count * (4 * cols + width) + 4 * cols * width) * 2,
    )(me, docs, valid, slopes, q, k, vt, kc, vct, w_out)


def backward_body(
    cmem, mem, me_ref, docs_ref, valid_ref, slopes_ref, q_ref, g_ref, ot_ref, lse_ref, k_ref, kt_ref, v_ref,
    kc_ref, kct_ref, vc_ref, gq_ref, gk_ref, gv_ref, gkc_ref, gvc_ref, slope_ref,
    gt_ref, delta_ref, accq, acck, accv, acckc, accvc,
):
    heads = slopes_ref.shape[0]
    scale = HEAD**-0.5
    power = scale * LOG2E
    q0 = pl.program_id(0) * TILE
    places = q0 + lax.broadcasted_iota(jnp.int32, (1, TILE), 1)
    first = query_limits(places, docs_ref)
    place_q = places.astype(F32)

    @pl.when(pl.program_id(0) == 0)
    def _():
        for acc in (acck, accv, acckc, accvc, slope_ref):
            acc[...] = jnp.zeros(acc.shape, F32)

    accq[...] = jnp.zeros(accq.shape, F32)
    for h in range(heads):
        cols = slice(h * HEAD, (h + 1) * HEAD)
        flipped = g_ref[:, cols].T
        gt_ref[cols, :] = flipped
        delta_ref[h : h + 1, :] = jnp.sum(flipped.astype(F32) * ot_ref[cols, :], axis=0, keepdims=True)

    def block(keys, keys_t, values, sum_k, sum_v, rows, place, visible):
        far = place_q - place
        for h in range(heads):
            cols = slice(h * HEAD, (h + 1) * HEAD)
            scores = dot_nt(keys[rows, cols], q_ref[:, cols])
            scores = scores * power + place * (slopes_ref[h] * LOG2E)
            scores = jnp.where(visible, scores - lse_ref[h : h + 1, :], HIDE)
            probs = jnp.exp2(scores)
            pulled = dot(values[rows, cols], gt_ref[cols, :])
            grad = probs * (pulled - delta_ref[h : h + 1, :])
            low = grad.astype(BF16)
            slope_ref[h] += jnp.sum((grad * far).reshape(-1, 8, TILE), axis=0)
            sum_v[rows, cols] += dot(probs.astype(BF16), g_ref[:, cols])
            sum_k[rows, cols] += dot(low, q_ref[:, cols])
            accq[cols, :] += dot(keys_t[cols, rows], low)

    def step(start, least, stride, offset):
        index = start + lax.broadcasted_iota(jnp.int32, (HEAD, 1), 0)
        visible = (index >= least) & (places < docs_ref[0, 1])
        place = (index * stride + offset).astype(F32)
        block(kc_ref, kct_ref, vc_ref, acckc, accvc, pl.ds(start, HEAD), place, visible)

    def token_step(start):
        index = start + lax.broadcasted_iota(jnp.int32, (TILE, 1), 0)
        visible = (index >= first) & (index <= places)
        block(k_ref, kt_ref, v_ref, acck, accv, pl.ds(start, TILE), index.astype(F32), visible)

    attend_loops(q0, docs_ref, valid_ref, cmem, mem, HEAD, step, token_step)
    for h in range(heads):
        cols = slice(h * HEAD, (h + 1) * HEAD)
        gq_ref[:, cols] = (accq[cols, :] * scale).T.astype(BF16)

    @pl.when(pl.program_id(0) == pl.num_programs(0) - 1)
    def _():
        gk_ref[...] = (acck[...] * scale).astype(BF16)
        gkc_ref[...] = (acckc[...] * scale).astype(BF16)
        gv_ref[...] = accv[...].astype(BF16)
        gvc_ref[...] = accvc[...].astype(BF16)


def backward_call(me, docs, valid, slopes, q, g, ot, lse, k, kt, v, kc, kct, vc, cmem, mem):
    count, cols = q.shape
    heads = slopes.shape[0]
    tall = pl.BlockSpec((TILE, cols), lambda i, *_: (i, 0))
    flat = pl.BlockSpec((cols, TILE), lambda i, *_: (0, i))
    outs = [(count, cols)] * 2 + [kc.shape] * 2
    return call(
        partial(backward_body, cmem, mem),
        [shape((count, cols))] + [shape(dims) for dims in outs] + [shape((heads, 8, TILE), F32)],
        [tall, tall, flat, pl.BlockSpec((heads, TILE), lambda i, *_: (0, i))]
        + [whole(a.shape) for a in (k, kt, v, kc, kct, vc)],
        [tall] + [whole(dims) for dims in outs] + [whole((heads, 8, TILE))],
        grid=(count // TILE,),
        scratch=[
            pltpu.VMEM((cols, TILE), BF16),
            pltpu.VMEM((heads, TILE), F32),
            pltpu.VMEM((cols, TILE), F32),
        ]
        + [pltpu.VMEM(dims, F32) for dims in outs],
        scalars=4,
        flops=5 * count * cols * count,
        moved=20 * count * cols * 2,
    )(me, docs, valid, slopes, q, g, ot, lse, k, kt, v, kc, kct, vc)


def middle_body(_, x_ref, a_ref, b_ref, gain_ref, mid_ref, n_ref, nt_ref):
    mid = x_ref[...].astype(F32) + (a_ref[...].astype(F32) + b_ref[...].astype(F32))
    mid_ref[...] = mid
    normed = layer_norm(mid, gain_ref[...]).astype(BF16)
    n_ref[...] = normed
    nt_ref[...] = normed.T


def middle_call(me, x, part, other, gain):
    count, width = x.shape
    tall = pl.BlockSpec((TILE, width), lambda i, _: (i, 0))
    return call(
        middle_body,
        [shape((count, width), F32), shape((count, width)), shape((width, count))],
        [tall, tall, tall, whole(gain.shape)],
        [tall, tall, pl.BlockSpec((width, TILE), lambda i, _: (0, i))],
        grid=(count // TILE,),
        moved=14 * count * width,
    )(me, x, part, other, gain)


def ffn_body(orders, me_ref, n_ref, nt_ref, g_ref, gt_ref, up_ref, down_ref, hid_ref, gpre_ref, gain_ref, *rest):
    outs, res = rest[:-1], rest[-1]
    for i in range(n_ref.shape[0] // TILE):
        rows = pl.ds(i * TILE, TILE)
        pre = dot(n_ref[rows, :], up_ref[...])
        back = dot_nt(g_ref[rows, :], down_ref[...])
        cdf, bell = gelu_parts(pre)
        hid_ref[rows, :] = (pre * cdf).astype(BF16)
        gpre_ref[rows, :] = (back * (cdf + bell)).astype(BF16)

    @pl.when(pl.program_id(0) == 0)
    def _():
        gain_ref[...] = jnp.zeros(gain_ref.shape, F32)

    for which, (left, right) in enumerate(((gt_ref, hid_ref), (nt_ref, gpre_ref))):
        for i in range(left.shape[0] // TILE):
            rows = pl.ds(i * TILE, TILE)
            grad = dot(left[rows, :], right[...])
            res[rows, :] = grad.astype(BF16)
            if which == 1:
                dotted = grad * up_ref[rows, :].astype(F32)
                for c in range(0, dotted.shape[1], HEAD):
                    gain_ref[rows, :] += dotted[:, c : c + HEAD]
        put_blocks(me_ref[0], orders[which], res, outs[2 * which], outs[2 * which + 1])


def ffn_call(me, n2, n2t, g, gt, w_up, w_down, start, count, n, orders, step=512):
    rows, width = n2.shape
    begin = start // step
    piece = (n // 2, width // n, count)
    part = pl.BlockSpec((n // 2, width // n, step), lambda j, _: (0, 0, j))
    tall = pl.BlockSpec((rows, step), lambda j, _: (0, j))
    return call(
        partial(ffn_body, orders),
        [shape((rows, count))] * 2 + [shape((width, HEAD), F32)] + [shape(piece)] * 4,
        [whole(a.shape) for a in (n2, n2t, g, gt)]
        + [
            pl.BlockSpec((width, step), lambda j, _: (0, begin + j)),
            pl.BlockSpec((step, width), lambda j, _: (begin + j, 0)),
        ],
        [tall, tall, whole((width, HEAD))] + [part] * 4,
        grid=(count // step,),
        scratch=[pltpu.VMEM((width, step), BF16)],
        flops=8 * rows * width * count,
        moved=8 * rows * width + 12 * width * count,
    )(me, n2, n2t, g, gt, w_up, w_down)


def product_body(flip, pieces, _, *refs):
    lefts, w_ref, out_ref = refs[:pieces], refs[pieces], refs[pieces + 1]
    total = None
    at = 0
    for left in lefts:
        size = left.shape[1]
        part = dot_nt(left[...], w_ref[:, at : at + size]) if flip else dot(left[...], w_ref[at : at + size, :])
        total = part if total is None else total + part
        at += size
    out_ref[...] = total.astype(out_ref.dtype)


def product_call(me, lefts, weight, flip):
    count = lefts[0].shape[0]
    width = weight.shape[0] if flip else weight.shape[1]
    inner = weight.shape[1] if flip else weight.shape[0]
    return call(
        partial(product_body, flip, len(lefts)),
        shape((count, width)),
        [pl.BlockSpec((TILE, a.shape[1]), lambda i, _: (i, 0)) for a in lefts] + [whole(weight.shape)],
        pl.BlockSpec((TILE, width), lambda i, _: (i, 0)),
        grid=(count // TILE,),
        flops=2 * count * width * inner,
        moved=2 * (count * width + count * inner + width * inner),
    )(me, *lefts, weight)


def turn_body(order, me_ref, mid_ref, gain_ref, g_ref, a_ref, b_ref, att_ref, w_ref, gmid_ref, gatt_ref, send, keep, low_t, res):
    i = pl.program_id(0)
    grad = a_ref[...].astype(F32) + b_ref[...].astype(F32)
    total = g_ref[...].astype(F32) + layer_norm_back(mid_ref[...], gain_ref[...], grad)
    gmid_ref[...] = total
    low = total.astype(BF16)
    gatt_ref[...] = dot_nt(low, w_ref[...]).astype(BF16)
    low_t[:, pl.ds(pl.multiple_of(i * TILE, TILE), TILE)] = low.T

    @pl.when(i == pl.num_programs(0) - 1)
    def _():
        for t in range(low_t.shape[0] // TILE):
            rows = pl.ds(t * TILE, TILE)
            res[rows, :] = dot(low_t[rows, :], att_ref[...]).astype(BF16)
        put_blocks(me_ref[0], order, res, send, keep)


def turn_call(me, mid, gain, g, part, other, attended, w_out, n, order):
    count, width = mid.shape
    cols = attended.shape[1]
    tall = pl.BlockSpec((TILE, width), lambda i, _: (i, 0))
    piece = (n // 2, width // n, cols)
    return call(
        partial(turn_body, order),
        [shape((count, width), F32), shape((count, cols)), shape(piece), shape(piece)],
        [tall, whole(gain.shape), tall, tall, tall, whole(attended.shape), whole(w_out.shape)],
        [tall, pl.BlockSpec((TILE, cols), lambda i, _: (i, 0)), whole(piece), whole(piece)],
        grid=(count // TILE,),
        scratch=[pltpu.VMEM((width, count), BF16), pltpu.VMEM((width, cols), BF16)],
        flops=4 * count * width * cols,
        moved=count * width * 14 + 8 * width * cols,
    )(me, mid, gain, g, part, other, attended, w_out)


def qkv_grad_body(orders, me_ref, nt_ref, nct_ref, gq_ref, gk_ref, gkc_ref, gv_ref, gvc_ref, w_ref, gain_ref, *rest):
    outs, res = rest[:-1], rest[-1]
    pairs = ((gq_ref, None), (gk_ref, gkc_ref), (gv_ref, gvc_ref))
    for which, (tokens, context) in enumerate(pairs):
        for t in range(nt_ref.shape[0] // TILE):
            rows = pl.ds(t * TILE, TILE)
            grad = dot(nt_ref[rows, :], tokens[...])
            if context is not None:
                grad = grad + dot(nct_ref[rows, :], context[...])
            res[rows, :] = grad.astype(BF16)
            dotted = grad * w_ref[which, rows, :].astype(F32)
            total = sum(dotted[:, c : c + HEAD] for c in range(0, dotted.shape[1], HEAD))
            gain_ref[rows, :] = total if which == 0 else gain_ref[rows, :] + total
        put_blocks(me_ref[0], orders[which], res, outs[2 * which], outs[2 * which + 1])


def qkv_grad_call(me, nt, nct, gq, gk, gkc, gv, gvc, w_qkv, n, orders):
    width = nt.shape[0]
    cols = gq.shape[1]
    piece = (n // 2, width // n, cols)
    ins = (nt, nct, gq, gk, gkc, gv, gvc, w_qkv)
    return call(
        partial(qkv_grad_body, orders),
        [shape((width, HEAD), F32)] + [shape(piece)] * 6,
        [whole(a.shape) for a in ins],
        [whole((width, HEAD))] + [whole(piece)] * 6,
        scratch=[pltpu.VMEM((width, cols), BF16)],
        flops=2 * width * cols * (3 * nt.shape[1] + 2 * nct.shape[1]),
        moved=20 * width * cols,
    )(me, *ins)


def rows_grad_body(tiles, _, gq_ref, gk_ref, gv_ref, w_ref, send, keep):
    total = dot_nt(gq_ref[...], w_ref[0]) + dot_nt(gk_ref[...], w_ref[1]) + dot_nt(gv_ref[...], w_ref[2])

    @pl.when(pl.program_id(0) < tiles)
    def _():
        send[...] = total.astype(BF16)

    @pl.when(pl.program_id(0) >= tiles)
    def _():
        keep[...] = total.astype(BF16)


def rows_grad_call(me, gq, gk, gv, w_qkv):
    count, cols = gq.shape
    width = w_qkv.shape[1]
    tiles = count // 2 // TILE
    tall = pl.BlockSpec((TILE, cols), lambda i, m: ((i + (1 - m[1]) * tiles) % (2 * tiles), 0))
    return call(
        partial(rows_grad_body, tiles),
        [shape((count // 2, width))] * 2,
        [tall, tall, tall, whole(w_qkv.shape)],
        [
            pl.BlockSpec((TILE, width), lambda i, _: (jnp.minimum(i, tiles - 1), 0)),
            pl.BlockSpec((TILE, width), lambda i, _: (jnp.maximum(i - tiles, 0), 0)),
        ],
        grid=(2 * tiles,),
        flops=6 * count * width * cols,
        moved=2 * (3 * count * cols + 3 * width * cols + count * width),
    )(me, gq, gk, gv, w_qkv)


def last_body(_, x_ref, gain_ref, a_ref, b_ref, gmid_ref, out_ref):
    grad = a_ref[...].astype(F32) + b_ref[...].astype(F32)
    back = layer_norm_back(x_ref[...].astype(F32), gain_ref[...], grad)
    out_ref[...] = (gmid_ref[...] + back).astype(BF16)


def last_call(me, x, gain, part, other, gmid):
    count, width = x.shape
    tall = pl.BlockSpec((TILE, width), lambda i, _: (i, 0))
    tiles = count // TILE
    return call(
        last_body,
        shape((count, width)),
        [tall, whole(gain.shape), tall, tall, pl.BlockSpec((TILE, width), lambda i, m: (i + m[1] * tiles, 0))],
        tall,
        grid=(tiles,),
        moved=12 * count * width,
    )(me, x, gain, part, other, gmid)


def output_body(_, mid_ref, a_ref, b_ref, out_ref):
    out_ref[...] = (mid_ref[...] + (a_ref[...].astype(F32) + b_ref[...].astype(F32))).astype(BF16)


def swap_mp(rows):
    return lax.ppermute(rows, "mp", [(0, 1), (1, 0)])


def scatter_dp(send, keep, order):
    n = lax.axis_size("dp")
    for step, bit in enumerate(order):
        got = lax.ppermute(send, "dp", [(i, i ^ (1 << bit)) for i in range(n)])
        half = keep.shape[0] // 2
        if half == 0:
            return keep[0].astype(F32) + got[0].astype(F32)
        add = lambda a, b: (a.astype(F32) + b.astype(F32)).astype(BF16)
        send, keep = add(keep[half:], got[half:]), add(keep[:half], got[:half])


def sum_dp(vector):
    n = lax.axis_size("dp")
    for bit in range(n.bit_length() - 1):
        vector = vector + lax.ppermute(vector, "dp", [(i, i ^ (1 << bit)) for i in range(n)])
    return vector


def shards(
    inputs, memory, compressed_memory, doc_starts, mem_valid, cmem_valid, gain_attn, w_qkv, slopes, w_out, gain_ffn,
    w_up, w_down, w_comp, out_grad, comp_grad,
):
    n = lax.axis_size("dp")
    bits = n.bit_length() - 1
    along = lambda first: [(first + k) % bits for k in range(bits)]
    orders = [along(0), along(1), along(2)]
    half, width = inputs.shape[1:]
    mem, cmem = memory.shape[1], compressed_memory.shape[1]
    core = lax.axis_index("mp")
    me = jnp.stack([lax.axis_index("dp"), core]).astype(jnp.int32)
    valid = jnp.stack([mem_valid[0], cmem_valid[0]])
    gain1, gain2 = gain_attn[None], gain_ffn[None]

    other_x = swap_mp(inputs[0])
    other_g = swap_mp(out_grad[0])

    compressed, *comp = comp_call(me, memory[0], w_comp, comp_grad[0], n, orders)
    comp_part = [scatter_dp(comp[2 * r], comp[2 * r + 1], orders[r]) for r in range(3)]

    context = jnp.concatenate([compressed_memory[0], memory[0]], axis=0)
    nct, kc, kct, vc, vct = context_call(me, context, gain1, w_qkv, HEAD)
    x, nt, q, k, kt, v, vt = tokens_call(me, inputs[0], other_x, gain1, w_qkv, TILE)
    attended, part, out_t, lse = forward_call(
        me, doc_starts, valid, slopes, q, k, vt, kc, vct, w_out, cmem, mem
    )
    g, gt = flip_call(me, out_grad[0], other_g, TILE)
    mid, n2, n2t = middle_call(me, x, part, swap_mp(part), gain2)

    hidden = w_up.shape[1]
    size = hidden // 2
    pieces = [
        ffn_call(me, n2, n2t, g, gt, w_up, w_down, i * size, size, n, (orders[i], orders[1 + i])) for i in range(2)
    ]
    down_part = [scatter_dp(p[3], p[4], orders[i]) for i, p in enumerate(pieces)]
    up_part = [scatter_dp(p[5], p[6], orders[1 + i]) for i, p in enumerate(pieces)]
    grad_part = product_call(me, [p[1] for p in pieces], w_up, True)
    grad_other = swap_mp(grad_part)
    ffn_part = product_call(me, [p[0] for p in pieces], w_down, False)
    send = lax.dynamic_slice_in_dim(ffn_part, (1 - core) * half, half, 0)
    ffn_keep = lax.dynamic_slice_in_dim(ffn_part, core * half, half, 0)
    mid_keep = lax.dynamic_slice_in_dim(mid, core * half, half, 0)
    result = (mid_keep + (ffn_keep.astype(F32) + swap_mp(send).astype(F32))).astype(BF16)

    gmid, gatt, out_send, out_keep = turn_call(
        me, mid, gain2, g, grad_part, grad_other, attended, w_out, n, orders[0]
    )
    out_part = scatter_dp(out_send, out_keep, orders[0])
    gq, gk, gv, gkc, gvc, slope = backward_call(
        me, doc_starts, valid, slopes, q, gatt, out_t, lse, k, kt, v, kc, kct, vc, cmem, mem
    )
    gain_sum, *qkv = qkv_grad_call(me, nt, nct, gq, gk, gkc, gv, gvc, w_qkv, n, orders)
    qkv_part = [scatter_dp(qkv[2 * r], qkv[2 * r + 1], orders[r]) for r in range(3)]
    rows_send, rows_keep = rows_grad_call(me, gq, gk, gv, w_qkv)
    input_grad = last_call(me, inputs[0], gain1, rows_keep, swap_mp(rows_send), gmid)

    gains = jnp.stack([jnp.sum(gain_sum, axis=1), jnp.sum(pieces[0][2] + pieces[1][2], axis=1)])
    gains = gains + swap_mp(gains)
    slope_sum = jnp.zeros((1, width), F32).at[0, : slopes.shape[0]].set(-jnp.sum(slope, axis=(1, 2)))
    small = sum_dp(jnp.concatenate([gains, slope_sum], axis=0))
    return (
        result[None],
        compressed[None],
        input_grad[None],
        small[0] / gain_attn,
        jnp.stack(qkv_part),
        small[2, : slopes.shape[0]],
        out_part.T,
        small[1] / gain_ffn,
        jnp.concatenate(up_part, axis=1),
        jnp.concatenate(down_part, axis=1).T,
        jnp.stack(comp_part),
    )


def solution(mesh):
    placed = (
        P("dp", "mp", None),
        P("dp", None, None),
        P("dp", None, None),
        P("dp", None),
        P("dp"),
        P("dp"),
        P(),
        P(None, None, "mp"),
        P("mp"),
        P("mp", None),
        P(),
        P(None, "mp"),
        P("mp", None),
        P(None, None, "mp"),
        P("dp", "mp", None),
        P("dp", None, "mp"),
    )
    return jax.shard_map(
        shards,
        mesh=mesh,
        in_specs=placed,
        out_specs=(
            P("dp", "mp", None),
            P("dp", None, "mp"),
            P("dp", "mp", None),
            P(),
            P(None, "dp", "mp"),
            P("mp"),
            P("mp", "dp"),
            P(),
            P("dp", "mp"),
            P("mp", "dp"),
            P(None, "dp", "mp"),
        ),
        check_vma=False,
    )
```

```python
from functools import partial

import jax
import jax.numpy as jnp
from jax import lax
from jax.experimental import pallas as pl
from jax.experimental.pallas import tpu as pltpu
from jax.sharding import PartitionSpec as P

F32, BF16 = jnp.float32, jnp.bfloat16
VMEM_LIMIT = 60 * 1024 * 1024
HEAD = 128
TILE = 256
KEYS = 256
MEM_KEYS = 448
LOG2E = 1.4426950408889634
HIDE = -1e30
COST = pl.CostEstimate(flops=1, bytes_accessed=1, transcendentals=1)


def dot(a, b):
    return jnp.dot(a, b, preferred_element_type=F32)


def dot_nt(a, b):
    return lax.dot_general(a, b, (((1,), (1,)), ((), ())), preferred_element_type=F32)


def shape(dims, kind=BF16):
    return jax.ShapeDtypeStruct(dims, kind)


def whole(dims):
    return pl.BlockSpec(dims, lambda *_: (0,) * len(dims))


def call(body, out_shape, in_specs, out_specs, grid=(1,), scratch=(), scalars=1, after=()):
    ins = scalars + len(in_specs)

    def without(*refs):
        body(*refs[:ins], *refs[ins + len(after) :])

    in_specs = list(in_specs) + [pl.BlockSpec(memory_space=pl.ANY)] * len(after)
    run = pl.pallas_call(
        without,
        grid_spec=pltpu.PrefetchScalarGridSpec(
            num_scalar_prefetch=scalars,
            grid=grid,
            in_specs=in_specs,
            out_specs=out_specs,
            scratch_shapes=scratch,
        ),
        out_shape=out_shape,
        compiler_params=pltpu.CompilerParams(vmem_limit_bytes=VMEM_LIMIT),
        cost_estimate=COST,
    )
    return lambda *args: run(*args, *after)


def put_blocks(me, order, result, send, keep, cols=slice(None), to=slice(None)):
    half, rows = send.shape[0], send.shape[1]
    bits = len(order)
    for place in range(2 * half):
        rel = 0
        for k, bit in enumerate(order):
            rel |= ((place >> (bits - 1 - k)) & 1) << bit
        start = pl.multiple_of((me ^ rel) * rows, rows)
        out = send if place >= half else keep
        out[place % half, :, to] = result[pl.ds(start, rows), cols]


def layer_norm(rows, gain):
    centre = jnp.mean(rows, axis=-1, keepdims=True)
    centred = rows - centre
    spread = jnp.mean(centred * centred, axis=-1, keepdims=True)
    return centred * lax.rsqrt(spread + 1e-05) * gain


def layer_norm_back(rows, gain, grad):
    centre = jnp.mean(rows, axis=-1, keepdims=True)
    centred = rows - centre
    spread = jnp.mean(centred * centred, axis=-1, keepdims=True)
    inverse = lax.rsqrt(spread + 1e-05)
    unit = centred * inverse
    pulled = grad * gain
    return inverse * (
        pulled
        - jnp.mean(pulled, axis=-1, keepdims=True)
        - unit * jnp.mean(pulled * unit, axis=-1, keepdims=True)
    )


def gelu_parts(u):
    bell = jnp.exp2(u * u * (-0.5 * LOG2E))
    t = 1.0 / (1.0 + (0.3275911 * 0.7071067811865476) * jnp.abs(u))
    series = 0.7107068705 + t * (-0.7265760135 + t * 0.5307027145)
    tail = t * (0.127414796 + t * (-0.142248368 + t * series)) * bell
    return jnp.where(u >= 0, 1.0 - tail, tail), u * bell * 0.3989422804014327


def comp_body(_, mem_ref, w_ref, grad_ref, out_ref, wgrad_ref, wide):
    count = out_ref.shape[0]
    groups = mem_ref.shape[1] // HEAD
    for c in range(groups):
        wide[pl.ds(c * 3 * count, 3 * count), :] = mem_ref[:, c * HEAD : (c + 1) * HEAD].astype(F32)
    total = None
    cols = grad_ref.shape[1]
    for r in range(3):
        rows = jnp.concatenate([wide[pl.ds(c * 3 * count + r, count, stride=3), :] for c in range(groups)], axis=1)
        part = dot(rows.astype(BF16), w_ref[r])
        total = part if total is None else total + part
        wgrad_ref[:, r * cols : (r + 1) * cols] = dot(rows.T.astype(BF16), grad_ref[...]).astype(BF16)
    out_ref[...] = total.astype(BF16)


def comp_call(me, memory, w_comp, comp_grad):
    rows, width = memory.shape
    cols = w_comp.shape[2]
    return call(
        comp_body,
        [shape((rows // 3, cols)), shape((width, 3 * cols))],
        [whole(memory.shape), whole(w_comp.shape), whole(comp_grad.shape)],
        [whole((rows // 3, cols)), whole((width, 3 * cols))],
        scratch=[pltpu.VMEM((rows * width // HEAD, HEAD), F32)],
    )(me, memory, w_comp, comp_grad)


def context_body(tiles, _, a_ref, b_ref, gain_ref, w_ref, nt_ref, k_ref, v_ref):
    low_x = jnp.where(pl.program_id(0) < tiles, a_ref[...], b_ref[...])
    normed = layer_norm(low_x.astype(F32), gain_ref[...]).astype(BF16)
    nt_ref[...] = normed.T
    k_ref[...] = dot(normed, w_ref[1]).astype(BF16)
    v_ref[...] = dot(normed, w_ref[2]).astype(BF16)


def context_call(me, cmem, mem, gain, w_qkv, tile, after=()):
    width = mem.shape[1]
    count = cmem.shape[0] + mem.shape[0]
    tiles = cmem.shape[0] // tile
    cols = w_qkv.shape[2]
    return call(
        partial(context_body, tiles),
        [shape((width, count))] + [shape((count, cols))] * 2,
        [
            pl.BlockSpec((tile, width), lambda i, _: (jnp.minimum(i, tiles - 1), 0)),
            pl.BlockSpec((tile, width), lambda i, _: (jnp.maximum(i - tiles, 0), 0)),
            whole(gain.shape),
            whole(w_qkv.shape),
        ],
        [pl.BlockSpec((width, tile), lambda i, _: (0, i))]
        + [pl.BlockSpec((tile, cols), lambda i, _: (i, 0))] * 2,
        grid=(count // tile,),
        after=after,
    )(me, cmem, mem, gain, w_qkv)


def tokens_body(tiles, me_ref, own_ref, other_ref, gain_ref, w_ref, x_ref, nt_ref, q_ref, k_ref, v_ref):
    mine = pl.program_id(0) // tiles == me_ref[1]
    low_x = jnp.where(mine, own_ref[...], other_ref[...])
    x_ref[...] = low_x
    normed = layer_norm(low_x.astype(F32), gain_ref[...]).astype(BF16)
    nt_ref[...] = normed.T
    q_ref[...] = dot(normed, w_ref[0]).astype(BF16)
    k_ref[...] = dot(normed, w_ref[1]).astype(BF16)
    v_ref[...] = dot(normed, w_ref[2]).astype(BF16)


def tokens_call(me, own, other, gain, w_qkv, tile, after=()):
    half, width = own.shape
    count = 2 * half
    cols = w_qkv.shape[2]
    tiles = half // tile
    side = pl.BlockSpec((tile, width), lambda i, _: (i % tiles, 0))
    tall = pl.BlockSpec((tile, cols), lambda i, _: (i, 0))
    return call(
        partial(tokens_body, tiles),
        [shape((count, width)), shape((width, count)), shape((count, cols))]
        + [shape((count, cols))] * 2,
        [side, side, whole(gain.shape), whole(w_qkv.shape)],
        [
            pl.BlockSpec((tile, width), lambda i, _: (i, 0)),
            pl.BlockSpec((width, tile), lambda i, _: (0, i)),
            tall,
        ]
        + [tall] * 2,
        grid=(count // tile,),
        after=after,
    )(me, own, other, gain, w_qkv)


def flip_body(tiles, me_ref, own_ref, other_ref, x_ref, xt_ref):
    mine = pl.program_id(0) // tiles == me_ref[1]
    low = jnp.where(mine, own_ref[...], other_ref[...])
    x_ref[...] = low
    xt_ref[...] = low.T


def flip_call(me, own, other, tile, after=()):
    half, width = own.shape
    tiles = half // tile
    side = pl.BlockSpec((tile, width), lambda i, _: (i % tiles, 0))
    return call(
        partial(flip_body, tiles),
        [shape((2 * half, width)), shape((width, 2 * half))],
        [side, side],
        [
            pl.BlockSpec((tile, width), lambda i, _: (i, 0)),
            pl.BlockSpec((width, tile), lambda i, _: (0, i)),
        ],
        grid=(2 * tiles,),
        after=after,
    )(me, own, other)


def document_start(places, docs_ref):
    first = jnp.zeros_like(places)
    for d in range(1, docs_ref.shape[1]):
        first = jnp.where(places >= docs_ref[0, d], docs_ref[0, d], first)
    return first


def down(start, count):
    return start + lax.broadcasted_iota(jnp.int32, (count, 1), 0)


def memory_bias(start, count, cmem, mem, valid_ref, slope):
    index = down(start, count)
    compressed = index < cmem
    place = jnp.where(compressed, 3 * index - (mem + 3 * cmem), index - (cmem + mem))
    seen = index >= jnp.where(compressed, cmem - valid_ref[1], cmem + mem - valid_ref[0])
    return jnp.where(seen, place.astype(F32) * slope, HIDE)


def cut(of_memory, start, end, size):
    return [(of_memory, at, min(size, end - at)) for at in range(start, end, size)]


def key_blocks(i, tokens, memory):
    blocks = cut(True, 0, memory, MEM_KEYS) if i * TILE < tokens // 2 else []
    return blocks + cut(False, 0, i * TILE, KEYS) + cut(False, i * TILE, (i + 1) * TILE, KEYS)


def hide(scores, of_memory, start, count, i, places, first, docs_ref):
    if of_memory:
        return jnp.where(places < docs_ref[0, 1], scores, HIDE)
    index = down(start, count)
    visible = index >= first
    if start + count > i * TILE:
        visible = visible & (index <= places)
    return jnp.where(visible, scores, HIDE)


def forward_body(
    cmem, mem, me_ref, docs_ref, valid_ref, slopes_ref, q_ref, k_ref, v_ref, kc_ref, vc_ref, w_ref,
    att_ref, part_ref, ot_ref, lse_ref, vt_ref, vct_ref, score_ref, all_ref,
):
    h = pl.program_id(0)
    tokens = q_ref.shape[0]
    scale = HEAD**-0.5
    power = scale * LOG2E
    slope = slopes_ref[h] / scale
    vt_ref[...] = v_ref[...].T
    vct_ref[...] = vc_ref[...].T
    for i in range(tokens // TILE):
        queries = slice(i * TILE, (i + 1) * TILE)
        places = i * TILE + lax.broadcasted_iota(jnp.int32, (1, TILE), 1)
        first = document_start(places, docs_ref)
        blocks = key_blocks(i, tokens, cmem + mem)
        top = jnp.full((8, TILE), HIDE, F32)
        at = 0
        for of_memory, start, count in blocks:
            keys = (kc_ref if of_memory else k_ref)[start : start + count, :]
            if of_memory:
                bias = memory_bias(start, count, cmem, mem, valid_ref, slope)
            else:
                bias = down(start, count).astype(F32) * slope
            scores = hide(dot_nt(keys, q_ref[queries, :]) + bias, of_memory, start, count, i, places, first, docs_ref)
            score_ref[i % 2, at : at + count, :] = scores
            at += count
            top = jnp.maximum(top, jnp.max(scores.reshape(-1, 8, TILE), axis=0))
        top = jnp.max(top, axis=0, keepdims=True)
        total = jnp.zeros((8, TILE), F32)
        out = jnp.zeros((HEAD, TILE), F32)
        at = 0
        for of_memory, start, count in blocks:
            probs = jnp.exp2((score_ref[i % 2, at : at + count, :] - top) * power)
            at += count
            total = total + jnp.sum(probs.reshape(-1, 8, TILE), axis=0)
            out = out + dot((vct_ref if of_memory else vt_ref)[:, start : start + count], probs.astype(BF16))
        total = jnp.sum(total, axis=0, keepdims=True)
        out = out * (1.0 / total)
        ot_ref[:, queries] = out
        low = out.T.astype(BF16)
        att_ref[queries, :] = low
        all_ref[h, queries, :] = low
        lse_ref[0, :, queries] = top * power + jnp.log2(total)

    @pl.when(h == pl.num_programs(0) - 1)
    def _():
        for i in range(tokens // TILE):
            rows = slice(i * TILE, (i + 1) * TILE)
            low = jnp.concatenate([all_ref[g, rows, :] for g in range(all_ref.shape[0])], axis=1)
            part_ref[rows, :] = dot(low, w_ref[...]).astype(BF16)


def forward_call(me, docs, valid, slopes, q, k, v, kc, vc, w_out, cmem, mem, tie=()):
    count, cols = q.shape
    width = w_out.shape[1]
    heads = slopes.shape[0]
    head = pl.BlockSpec((count, HEAD), lambda h, *_: (0, h))
    head_c = pl.BlockSpec((cmem + mem, HEAD), lambda h, *_: (0, h))
    return call(
        partial(forward_body, cmem, mem),
        [shape((count, cols)), shape((count, width)), shape((cols, count), F32), shape((heads, 1, count), F32)],
        [head, head, head, head_c, head_c, whole(w_out.shape)],
        [
            head,
            whole((count, width)),
            pl.BlockSpec((HEAD, count), lambda h, *_: (h, 0)),
            pl.BlockSpec((1, 1, count), lambda h, *_: (h, 0, 0)),
        ],
        grid=(heads,),
        scratch=[
            pltpu.VMEM((HEAD, count), BF16),
            pltpu.VMEM((HEAD, cmem + mem), BF16),
            pltpu.VMEM((2, count + cmem + mem, TILE), F32),
            pltpu.VMEM((heads, count, HEAD), BF16),
        ],
        scalars=4,
    )(me, docs, valid, slopes, q, k, v, kc, vc, w_out)


def backward_body(
    cmem, mem, me_ref, docs_ref, valid_ref, slopes_ref, q_ref, g_ref, ot_ref, lse_ref, k_ref, v_ref, kc_ref, vc_ref,
    gq_ref, gk_ref, gv_ref, gkc_ref, gvc_ref, slope_ref, kt_ref, kct_ref, acck, accv, acckc, accvc,
):
    h = pl.program_id(0)
    tokens = q_ref.shape[0]
    scale = HEAD**-0.5
    power = scale * LOG2E
    slope = slopes_ref[h] * LOG2E
    row = lax.broadcasted_iota(jnp.int32, (8, 1), 0)
    for keys, flipped, memory in ((k_ref, kt_ref, False), (kc_ref, kct_ref, True)):
        flipped[:HEAD, :] = keys[...].T
        index = lax.broadcasted_iota(jnp.int32, (1, keys.shape[0]), 1)
        place = index
        if memory:
            place = jnp.where(index < cmem, 3 * index - (mem + 3 * cmem), index - (cmem + mem))
        high = (place >> 4) << 4
        extra = jnp.where(row == 0, high, jnp.where(row == 1, place - high, jnp.where(row == 2, 1, 0)))
        flipped[HEAD:, :] = jnp.concatenate([extra, jnp.zeros_like(extra)], axis=0).astype(F32).astype(BF16)
    slope_sum = jnp.zeros((1, TILE), F32)
    for i in range(tokens // TILE):
        queries = slice(i * TILE, (i + 1) * TILE)
        places = i * TILE + lax.broadcasted_iota(jnp.int32, (1, TILE), 1)
        first = document_start(places, docs_ref)
        gt = g_ref[queries, :].T
        delta = jnp.sum(gt.astype(F32) * ot_ref[:, queries], axis=0, keepdims=True)
        lse = lse_ref[0, :, queries]
        sum_q = jnp.zeros((HEAD + 16, TILE), F32)
        for of_memory, start, count in key_blocks(i, tokens, cmem + mem):
            rows = slice(start, start + count)
            keys, values = (kc_ref, vc_ref) if of_memory else (k_ref, v_ref)
            if of_memory:
                bias = memory_bias(start, count, cmem, mem, valid_ref, slope)
            else:
                bias = down(start, count).astype(F32) * slope
            scores = dot_nt(keys[rows, :], q_ref[queries, :]) * power + bias
            scores = hide(scores - lse, of_memory, start, count, i, places, first, docs_ref)
            probs = jnp.exp2(scores)
            grad = (probs * (dot(values[rows, :], gt) - delta)).astype(BF16)
            part_v = dot(probs.astype(BF16), g_ref[queries, :])
            part_k = dot(grad, q_ref[queries, :])
            sum_k, sum_v = (acckc, accvc) if of_memory else (acck, accv)
            fresh = i == 0 if of_memory else start >= i * TILE
            sum_v[rows, :] = part_v if fresh else sum_v[rows, :] + part_v
            sum_k[rows, :] = part_k if fresh else sum_k[rows, :] + part_k
            sum_q = sum_q + dot((kct_ref if of_memory else kt_ref)[:, rows], grad)
        gq_ref[queries, :] = (sum_q[:HEAD] * scale).T.astype(BF16)
        far = places.astype(F32) * sum_q[HEAD + 2 : HEAD + 3] - sum_q[HEAD : HEAD + 1] - sum_q[HEAD + 1 : HEAD + 2]
        slope_sum = slope_sum - far
    slope_ref[0] = slope_sum
    gk_ref[...] = (acck[...] * scale).astype(BF16)
    gkc_ref[...] = (acckc[...] * scale).astype(BF16)
    gv_ref[...] = accv[...].astype(BF16)
    gvc_ref[...] = accvc[...].astype(BF16)


def backward_call(me, docs, valid, slopes, q, g, ot, lse, k, v, kc, vc, cmem, mem, after=()):
    count, cols = q.shape
    heads = slopes.shape[0]
    head = pl.BlockSpec((count, HEAD), lambda h, *_: (0, h))
    head_c = pl.BlockSpec((cmem + mem, HEAD), lambda h, *_: (0, h))
    return call(
        partial(backward_body, cmem, mem),
        [shape((count, cols))] * 3 + [shape(kc.shape)] * 2 + [shape((heads, 1, TILE), F32)],
        [
            head,
            head,
            pl.BlockSpec((HEAD, count), lambda h, *_: (h, 0)),
            pl.BlockSpec((1, 1, count), lambda h, *_: (h, 0, 0)),
            head,
            head,
            head_c,
            head_c,
        ],
        [head] * 3 + [head_c] * 2 + [pl.BlockSpec((1, 1, TILE), lambda h, *_: (h, 0, 0))],
        grid=(heads,),
        scratch=[pltpu.VMEM((HEAD + 16, count), BF16), pltpu.VMEM((HEAD + 16, cmem + mem), BF16)]
        + [pltpu.VMEM((count, HEAD), F32)] * 2
        + [pltpu.VMEM((cmem + mem, HEAD), F32)] * 2,
        scalars=4,
        after=after,
    )(me, docs, valid, slopes, q, g, ot, lse, k, v, kc, vc)


def middle_body(_, x_ref, a_ref, b_ref, gain_ref, mid_ref, n_ref, nt_ref):
    mid = x_ref[...].astype(F32) + (a_ref[...].astype(F32) + b_ref[...].astype(F32))
    mid_ref[...] = mid
    normed = layer_norm(mid, gain_ref[...]).astype(BF16)
    n_ref[...] = normed
    nt_ref[...] = normed.T


def middle_call(me, x, part, other, gain):
    count, width = x.shape
    tall = pl.BlockSpec((TILE, width), lambda i, _: (i, 0))
    return call(
        middle_body,
        [shape((count, width), F32), shape((count, width)), shape((width, count))],
        [tall, tall, tall, whole(gain.shape)],
        [tall, tall, pl.BlockSpec((width, TILE), lambda i, _: (0, i))],
        grid=(count // TILE,),
    )(me, x, part, other, gain)


class Copies:
    def __init__(self, sems):
        self.sems, self.count, self.open = sems, 0, []

    def start(self, source, target):
        copy = pltpu.make_async_copy(source, target, self.sems.at[self.count])
        self.count += 1
        copy.start()
        self.open.append(copy)
        return copy

    def finish(self):
        for copy in self.open:
            copy.wait()
        self.open = []


def ship(copies, me, order, result, outs, cols):
    send, keep = outs
    half, rows, width = send.shape
    bits = len(order)
    to = slice(cols.start % width, cols.start % width + cols.stop - cols.start)
    for place in range(2 * half):
        rel = 0
        for k, bit in enumerate(order):
            rel |= ((place >> (bits - 1 - k)) & 1) << bit
        start = pl.multiple_of((me ^ rel) * rows, rows)
        out = send if place >= half else keep
        copies.start(result.at[pl.ds(start, rows), cols], out.at[place % half, :, to])


def ffn_body(orders, second, step, me_ref, *refs):
    if second:
        n_in, nt_in, g_in, gt_in, up_in, down_in, hid_in, gpre_in, *refs = refs
        down_outs, up_outs, refs = refs[:2], refs[2 : 2 * len(orders)], refs[2 * len(orders) :]
        gain_out, out_send, out_keep, *refs = refs
        rows_out, refs = refs[: len(refs) - 15], refs[len(refs) - 15 :]
        n, nt, g, gt, up, down, hid, gpre, res_down, res_up, gain, rows, part, in_sems, out_sems = refs
    else:
        n_in, nt_in, g_in, gt_in, up_in, down_in, *refs = refs
        down_outs, up_outs, refs = refs[:2], refs[2 : 2 * len(orders)], refs[2 * len(orders) :]
        gain_out, hid_out, gpre_out, *refs = refs
        n, nt, g, gt, up, down, hid, gpre, res_down, res_up, gain, in_sems, out_sems = refs
    tokens, width = n.shape
    size = res_down.shape[1]
    base = size if second else 0
    ins, outs = Copies(in_sems), Copies(out_sems)
    mine = slice(base, base + size)
    waits = {}
    for name, source, target in (
        ("n", n_in, n),
        ("up", up_in.at[:, mine], up.at[:, mine]),
        ("g", g_in, g),
        ("down", down_in.at[mine, :], down.at[mine, :]),
        ("gt", gt_in, gt),
        ("nt", nt_in, nt),
    ):
        waits[name] = ins.start(source, target)
    if second:
        for name, source, target in (
            ("gpre", gpre_in, gpre.at[:, :size]),
            ("up2", up_in.at[:, :size], up.at[:, :size]),
            ("hid", hid_in, hid.at[:, :size]),
            ("down2", down_in.at[:size, :], down.at[:size, :]),
        ):
            waits[name] = ins.start(source, target)
    for at in range(base, base + size, step):
        cols = slice(at, at + step)
        local = slice(at - base, at - base + step)
        for i in range(tokens // TILE):
            part_rows = slice(i * TILE, (i + 1) * TILE)
            if at == base and i == 0:
                waits["n"].wait()
                waits["up"].wait()
            pre = dot(n[part_rows, :], up[:, cols])
            if at == base and i == 0:
                waits["g"].wait()
                waits["down"].wait()
            back = dot_nt(g[part_rows, :], down[cols, :])
            cdf, bell = gelu_parts(pre)
            hid[part_rows, cols] = (pre * cdf).astype(BF16)
            gpre[part_rows, cols] = (back * (cdf + bell)).astype(BF16)
        if not second:
            outs.start(hid.at[:, cols], hid_out.at[:, cols])
            outs.start(gpre.at[:, cols], gpre_out.at[:, cols])
        if at == base:
            waits["gt"].wait()
        for i in range(width // TILE):
            part_rows = slice(i * TILE, (i + 1) * TILE)
            res_down[part_rows, local] = dot(gt[part_rows, :], hid[:, cols]).astype(BF16)
        ship(outs, me_ref[0], orders[0], res_down, down_outs, local)
        if at == base:
            waits["nt"].wait()
        for i in range(width // TILE):
            part_rows = slice(i * TILE, (i + 1) * TILE)
            grad = dot(nt[part_rows, :], gpre[:, cols])
            res_up[part_rows, local] = grad.astype(BF16)
            dotted = grad * up[part_rows, cols].astype(F32)
            total = sum(dotted[:, c : c + HEAD] for c in range(0, step, HEAD))
            gain[part_rows, :] = total if at == base else gain[part_rows, :] + total
        which = 2 * ((at - base) * (len(orders) - 1) // size)
        ship(outs, me_ref[0], orders[1 + which // 2], res_up, up_outs[which : which + 2], local)
    outs.start(gain, gain_out)
    if second:
        waits["gpre"].wait()
        waits["up2"].wait()
        for t in range(width // TILE):
            cols = slice(t * TILE, (t + 1) * TILE)
            rows[:, cols] = dot_nt(gpre[...], up[cols, :]).astype(BF16)
        chunk = tokens // len(rows_out)
        for i, target in enumerate(rows_out):
            outs.start(rows.at[i * chunk : (i + 1) * chunk, :], target)
        waits["hid"].wait()
        waits["down2"].wait()
        half = tokens // 2
        for t in range(width // TILE):
            cols = slice(t * TILE, (t + 1) * TILE)
            part[:, cols] = dot(hid[...], down[:, cols]).astype(BF16)
        for core, target in ((1 - me_ref[1], out_send), (me_ref[1], out_keep)):
            outs.start(part.at[pl.ds(pl.multiple_of(core * half, half), half), :], target)
    outs.finish()


def ffn_call(me, n2, n2t, g, gt, w_up, w_down, before, n, orders, step=512, after=()):
    tokens, width = n2.shape
    hidden = w_up.shape[1]
    size = hidden // 2
    second = len(before) > 0
    anywhere = pl.BlockSpec(memory_space=pl.ANY)
    ups = len(orders) - 1
    outs = [shape((n // 2, width // n, size))] * 2 + [shape((n // 2, width // n, size // ups))] * (2 * ups)
    outs += [shape((width, HEAD), F32)]
    scratch = [pltpu.VMEM(a.shape, BF16) for a in (n2, n2t, g, gt, w_up, w_down)]
    scratch += [pltpu.VMEM((tokens, hidden), BF16)] * 2 + [pltpu.VMEM((width, size), BF16)] * 2
    scratch += [pltpu.VMEM((width, HEAD), F32)]
    copies = 2 * n * (size // step) + 1
    if second:
        outs += [shape((tokens // 2, width))] * 2 + [shape((tokens, width))]
        scratch += [pltpu.VMEM((tokens, width), BF16)] * 2
        copies += 3
    else:
        outs += [shape((tokens, size))] * 2
        copies += 2 * (size // step)
    scratch += [pltpu.SemaphoreType.DMA((10,)), pltpu.SemaphoreType.DMA((copies,))]
    ins = 7 + len(before)

    def body(*refs):
        ffn_body(orders, second, step, *refs[:ins], *refs[ins + len(after) :])

    return pl.pallas_call(
        body,
        out_shape=outs,
        in_specs=[pl.BlockSpec(memory_space=pltpu.SMEM)] + [anywhere] * (ins - 1 + len(after)),
        out_specs=[anywhere] * len(outs),
        scratch_shapes=scratch,
        compiler_params=pltpu.CompilerParams(vmem_limit_bytes=VMEM_LIMIT),
        cost_estimate=COST,
    )(me, n2, n2t, g, gt, w_up, w_down, *before, *after)


def turn_body(
    order, me_ref, mid_ref, gain_ref, g_ref, att_ref, w_ref, a_ref, b_ref, gmid_ref, gatt_ref, send, keep, low_t, res
):
    i = pl.program_id(0)
    grad = a_ref[...].astype(F32) + b_ref[...].astype(F32)
    total = g_ref[...].astype(F32) + layer_norm_back(mid_ref[...], gain_ref[...], grad)
    gmid_ref[...] = total
    low = total.astype(BF16)
    gatt_ref[...] = dot_nt(low, w_ref[...]).astype(BF16)
    low_t[:, pl.ds(pl.multiple_of(i * TILE, TILE), TILE)] = low.T

    @pl.when(i == pl.num_programs(0) - 1)
    def _():
        for t in range(low_t.shape[0] // TILE):
            rows = pl.ds(t * TILE, TILE)
            res[rows, :] = dot(low_t[rows, :], att_ref[...]).astype(BF16)
        put_blocks(me_ref[0], order, res, send, keep)


def turn_call(me, mid, gain, g, part, other, attended, w_out, n, order, after=()):
    count, width = mid.shape
    cols = attended.shape[1]
    tall = pl.BlockSpec((TILE, width), lambda i, _: (i, 0))
    piece = (n // 2, width // n, cols)
    return call(
        partial(turn_body, order),
        [shape((count, width), F32), shape((count, cols)), shape(piece), shape(piece)],
        [tall, whole(gain.shape), tall, whole(attended.shape), whole(w_out.shape), tall, tall],
        [tall, pl.BlockSpec((TILE, cols), lambda i, _: (i, 0)), whole(piece), whole(piece)],
        grid=(count // TILE,),
        scratch=[pltpu.VMEM((width, count), BF16), pltpu.VMEM((width, cols), BF16)],
        after=after,
    )(me, mid, gain, g, attended, w_out, part, other)


def across(sums):
    return jnp.sum(sums.T, axis=0, keepdims=True)


def qkv_grad_body(
    orders, me_ref, nt_ref, nct_ref, gq_ref, gk_ref, gkc_ref, gv_ref, gvc_ref, w_ref, up_a, up_b, slope_ref, small_ref,
    *rest,
):
    outs, res, gain_ref = rest[:-2], rest[-2], rest[-1]
    pairs = ((gq_ref, None), (gk_ref, gkc_ref), (gv_ref, gvc_ref))
    for which, (tokens, context) in enumerate(pairs):
        for t in range(nt_ref.shape[0] // TILE):
            rows = pl.ds(t * TILE, TILE)
            grad = dot(nt_ref[rows, :], tokens[...])
            if context is not None:
                grad = grad + dot(nct_ref[rows, :], context[...])
            res[rows, :] = grad.astype(BF16)
            dotted = grad * w_ref[which, rows, :].astype(F32)
            total = sum(dotted[:, c : c + HEAD] for c in range(0, dotted.shape[1], HEAD))
            gain_ref[rows, :] = total if which == 0 else gain_ref[rows, :] + total
        size = res.shape[1]
        if which == 1:
            for flow in range(2):
                from_k = slice(flow * size // 2, (flow + 1) * size // 2)
                put_blocks(me_ref[0], orders[flow], res, outs[2 * flow], outs[2 * flow + 1], from_k, slice(size, size + size // 2))
        else:
            flow = which // 2
            put_blocks(me_ref[0], orders[flow], res, outs[2 * flow], outs[2 * flow + 1], slice(None), slice(0, size))
    small_ref[...] = jnp.zeros(small_ref.shape, F32)
    small_ref[0:1, :] = across(gain_ref[...])
    small_ref[1:2, :] = across(up_a[...] + up_b[...])
    lane = lax.broadcasted_iota(jnp.int32, (1, HEAD), 1)
    slopes = jnp.zeros((1, HEAD), F32)
    for h in range(slope_ref.shape[0]):
        slopes = jnp.where(lane == h, jnp.sum(slope_ref[h], axis=1, keepdims=True), slopes)
    small_ref[2:3, :HEAD] = slopes


def qkv_grad_call(me, nt, nct, gq, gk, gkc, gv, gvc, w_qkv, up_a, up_b, slope, n, orders, after=()):
    width = nt.shape[0]
    cols = gq.shape[1]
    piece = (n // 2, width // n, 3 * cols // 2)
    ins = (nt, nct, gq, gk, gkc, gv, gvc, w_qkv, up_a, up_b, slope)
    return call(
        partial(qkv_grad_body, orders),
        [shape((8, width), F32)] + [shape(piece)] * 4,
        [whole(a.shape) for a in ins],
        [whole((8, width))] + [whole(piece)] * 4,
        scratch=[pltpu.VMEM((width, cols), BF16), pltpu.VMEM((width, HEAD), F32)],
        after=after,
    )(me, *ins)


def rows_grad_body(tiles, _, gq_ref, gk_ref, gv_ref, w_ref, send, keep):
    total = dot_nt(gq_ref[...], w_ref[0]) + dot_nt(gk_ref[...], w_ref[1]) + dot_nt(gv_ref[...], w_ref[2])

    @pl.when(pl.program_id(0) < tiles)
    def _():
        send[...] = total.astype(BF16)

    @pl.when(pl.program_id(0) >= tiles)
    def _():
        keep[...] = total.astype(BF16)


def rows_grad_call(me, gq, gk, gv, w_qkv, after=()):
    count, cols = gq.shape
    width = w_qkv.shape[1]
    tiles = count // 2 // TILE
    tall = pl.BlockSpec((TILE, cols), lambda i, m: ((i + (1 - m[1]) * tiles) % (2 * tiles), 0))
    return call(
        partial(rows_grad_body, tiles),
        [shape((count // 2, width))] * 2,
        [tall, tall, tall, whole(w_qkv.shape)],
        [
            pl.BlockSpec((TILE, width), lambda i, _: (jnp.minimum(i, tiles - 1), 0)),
            pl.BlockSpec((TILE, width), lambda i, _: (jnp.maximum(i - tiles, 0), 0)),
        ],
        grid=(2 * tiles,),
        after=after,
    )(me, gq, gk, gv, w_qkv)


def last_body(_, x_ref, gain_ref, a_ref, b_ref, gmid_ref, out_ref):
    grad = a_ref[...].astype(F32) + b_ref[...].astype(F32)
    back = layer_norm_back(x_ref[...].astype(F32), gain_ref[...], grad)
    out_ref[...] = (gmid_ref[...] + back).astype(BF16)


def last_call(me, x, gain, part, other, gmid, after=()):
    count, width = x.shape
    rows = TILE // 2
    tall = pl.BlockSpec((rows, width), lambda i, _: (i, 0))
    tiles = count // rows
    mine = pl.BlockSpec((rows, width), lambda i, m: (i + m[1] * tiles, 0))
    return call(
        last_body, shape((count, width)), [tall, whole(gain.shape), tall, tall, mine], tall, grid=(tiles,), after=after
    )(me, x, gain, part, other, gmid)


def result_body(_, mid_ref, a_ref, b_ref, out_ref):
    out_ref[...] = (mid_ref[...] + (a_ref[...].astype(F32) + b_ref[...].astype(F32))).astype(BF16)


def result_call(me, mid, part, other, after=()):
    count, width = part.shape
    rows = TILE // 2
    tall = pl.BlockSpec((rows, width), lambda i, _: (i, 0))
    tiles = count // rows
    mine = pl.BlockSpec((rows, width), lambda i, m: (i + m[1] * tiles, 0))
    return call(
        result_body, shape((count, width)), [mine, tall, tall], tall, grid=(tiles,), after=after
    )(me, mid, part, other)


def swap_mp(rows):
    return lax.ppermute(rows, "mp", [(0, 1), (1, 0)])


class Flow:
    def __init__(self, send, keep, order):
        self.send, self.keep, self.order = send, keep, order
        n = lax.axis_size("dp")
        self.got = lax.ppermute(send, "dp", [(i, i ^ (1 << order[0])) for i in range(n)])


def exchange(array, bit):
    return lax.ppermute(array, "dp", [(i, i ^ (1 << bit)) for i in range(lax.axis_size("dp"))])


def add_body(plan, finish, skip, *refs):
    ins, outs = refs[: 2 * sum(plan)], refs[2 * sum(plan) + skip :]
    at = place = 0
    for which, count in enumerate(plan):
        pairs = [(ins[2 * i], ins[2 * i + 1]) for i in range(at, at + count)]
        at += count
        if len(pairs[0][0].shape) == 2:
            outs[-1][...] = pairs[0][0][...] + pairs[0][1][...]
            continue
        if finish is not None:
            finish(which, [keep[0].astype(F32) + got[0].astype(F32) for keep, got in pairs], outs)
            continue
        if len(pairs[0][0].shape) == 3:
            outs[place][...] = pairs[0][0][0].astype(F32) + pairs[0][1][0].astype(F32)
            place += 1
            continue
        col = 0
        place += 2
        for keep, got in pairs:
            to = slice(col, col + keep.shape[3])
            col += keep.shape[3]
            for half, out in ((1, outs[place - 2]), (0, outs[place - 1])):
                out[:, :, to] = (keep[half].astype(F32) + got[half].astype(F32)).astype(BF16)


def advance(groups, after=(), through=(), small=None, finish=None, finals=(), hold=()):
    ins, in_specs, outs, out_specs = [], [], [], []
    last = finish is not None
    steps = 1 if last else max(1, min(group[0].keep.shape[0] for group in groups) // 2)
    for group in groups:
        half = group[0].keep.shape[0] // 2
        size = half // steps
        for flow in group:
            for a in (flow.keep, flow.got):
                _, rows, cols = a.shape
                ins.append(a if half == 0 else a.reshape(2, half, rows, cols))
                in_specs.append(whole(a.shape) if half == 0 else pl.BlockSpec((2, size, rows, cols), lambda i: (0, i, 0, 0)))
        cols = sum(flow.keep.shape[2] for flow in group)
        if half == 0 and not last:
            outs.append(shape((rows, cols), F32))
            out_specs.append(whole((rows, cols)))
        elif not last:
            outs += [shape((half, rows, cols))] * 2
            out_specs += [pl.BlockSpec((size, rows, cols), lambda i: (i, 0, 0))] * 2
    outs += list(finals)
    out_specs += [whole(a.shape) for a in finals]
    plan = [len(group) for group in groups]
    if small is not None:
        ins += list(small)
        in_specs += [whole(small[0].shape)] * 2
        outs.append(shape(small[0].shape, F32))
        out_specs.append(whole(small[0].shape))
        plan.append(1)
    anywhere = pl.BlockSpec(memory_space=pl.ANY)
    results = pl.pallas_call(
        lambda *refs: add_body(plan, finish, len(through) + len(after), *refs[: len(refs) - len(through)]),
        grid=(steps,),
        out_shape=outs + [shape(a.shape, a.dtype) for a in through],
        in_specs=in_specs + [anywhere] * (len(through) + len(after)),
        out_specs=out_specs + [anywhere] * len(through),
        input_output_aliases={len(ins) + i: len(outs) + i for i in range(len(through))},
        compiler_params=pltpu.CompilerParams(vmem_limit_bytes=VMEM_LIMIT),
        cost_estimate=COST,
    )(*ins, *through, *after)
    sums, rest = list(results[: len(outs)]), list(results[len(outs) :])
    tail = [sums.pop()] if small is not None else []
    if not last:
        flat, sums = sums, []
        for i, group in enumerate(groups):
            if group[0].keep.shape[0] == 1:
                sums.append(flat.pop(0))
            elif i in hold:
                sums.append((flat.pop(0), flat.pop(0)))
            else:
                sums.append(Flow(flat.pop(0), flat.pop(0), group[0].order[1:]))
    return sums + tail + rest


def ffn_finish_body(first_ref, keep_ref, got_ref, down_ref, up_ref):
    size = first_ref.shape[1] // 2
    for which, total in enumerate((first_ref[...], keep_ref[0].astype(F32) + got_ref[0].astype(F32))):
        here = slice(which * size, (which + 1) * size)
        down_ref[here, :] = total[:, :size].T
        up_ref[:, here] = total[:, size:]


def ffn_finish_call(first, flow, after):
    block, hidden = first.shape
    ins = (first, flow.keep, flow.got)
    return call(
        lambda _, *refs: ffn_finish_body(*refs),
        [shape((hidden, block), F32), shape((block, hidden), F32)],
        [whole(a.shape) for a in ins],
        [whole((hidden, block)), whole((block, hidden))],
        after=after,
    )(jnp.zeros((1,), jnp.int32), *ins)


def shards(
    inputs, memory, compressed_memory, doc_starts, mem_valid, cmem_valid, gain_attn, w_qkv, slopes, w_out, gain_ffn,
    w_up, w_down, w_comp, out_grad, comp_grad,
):
    n = lax.axis_size("dp")
    bits = n.bit_length() - 1
    rest = list(range(2, bits))
    order_a, order_b = [0, 1] + rest, [1, 0] + rest
    half, width = inputs.shape[1:]
    mem, cmem = memory.shape[1], compressed_memory.shape[1]
    core = lax.axis_index("mp")
    me = jnp.stack([lax.axis_index("dp"), core]).astype(jnp.int32)
    valid = jnp.stack([mem_valid[0], cmem_valid[0]])
    gain1, gain2 = gain_attn[None], gain_ffn[None]

    other_x = swap_mp(inputs[0])
    other_g = swap_mp(out_grad[0])

    compressed, comp = comp_call(me, memory[0], w_comp, comp_grad[0])
    comp_part = lax.psum_scatter(comp, "dp", scatter_dimension=0, tiled=True).astype(F32)

    nct, kc, vc = context_call(me, compressed_memory[0], memory[0], gain1, w_qkv, HEAD, (compressed,))
    x, nt, q, k, v = tokens_call(me, inputs[0], other_x, gain1, w_qkv, TILE, (other_g,))
    attended, part, out_t, lse = forward_call(
        me, doc_starts, valid, slopes, q, k, v, kc, vc, w_out, cmem, mem
    )
    g, gt = flip_call(me, out_grad[0], other_g, TILE, (part,))
    mid, n2, n2t = middle_call(me, x, part, swap_mp(part), gain2)

    down1_s, down1_k, up1_s, up1_k, gain_a, *before = ffn_call(
        me, n2, n2t, g, gt, w_up, w_down, (), n, (order_a, order_b)
    )
    flow_a, flow_b = Flow(down1_s, down1_k, order_a), Flow(up1_s, up1_k, order_b)
    down2_s, down2_k, up2_s, up2_k, gain_b, out_send, out_keep, grad_part = ffn_call(
        me, n2, n2t, g, gt, w_up, w_down, before, n, (order_a, order_b)
    )
    grad_other = swap_mp(grad_part)
    flow_a, flow_b, down2_s, up2_s = advance([[flow_a], [flow_b]], (grad_part,), (down2_s, up2_s))
    flow_c, flow_d = Flow(down2_s, down2_k, order_a), Flow(up2_s, up2_k, order_b)
    gmid, gatt, wout_s, wout_k = turn_call(
        me, mid, gain2, g, grad_part, grad_other, attended, w_out, n, order_a, (flow_a.keep,)
    )
    flow_o = Flow(wout_s, wout_k, order_a)
    gq, gk, gv, gkc, gvc, slope = backward_call(
        me, doc_starts, valid, slopes, q, gatt, out_t, lse, k, v, kc, vc, cmem, mem
    )
    flow_ab, flow_c, flow_d = advance([[flow_a, flow_b], [flow_c], [flow_d]], (gq,))
    small, qx_s, qx_k, qy_s, qy_k = qkv_grad_call(
        me, nt, nct, gq, gk, gkc, gv, gvc, w_qkv, gain_a, gain_b, slope, n, (order_a, order_b),
        (flow_c.keep, comp_part),
    )
    flow_ab, flow_cd, held, qx_s, qy_s, small = advance(
        [[flow_ab], [flow_c, flow_d], [flow_o]], (qx_k,), (qx_s, qy_s, small), hold=(2,)
    )
    flow_x, flow_y = Flow(qx_s, qx_k, order_a), Flow(qy_s, qy_k, order_b)
    gain_rows = jnp.arange(small.shape[0])[:, None] < 2
    small = small + jnp.where(gain_rows, swap_mp(small), 0.0)
    got_small = exchange(small, order_a[0])
    rows_send, rows_keep = rows_grad_call(me, gq, gk, gv, w_qkv, (flow_cd.keep,))
    flow_x, flow_y, flow_cd, ab, small, rows_send, held_send = advance(
        [[flow_x], [flow_y], [flow_cd], [flow_ab]], (rows_keep,), (rows_send, held[0]), (small, got_small)
    )
    flow_o = Flow(held_send, held[1], order_a[1:])
    got_small = exchange(small, order_a[1])
    input_grad = last_call(me, inputs[0], gain1, rows_keep, swap_mp(rows_send), gmid, (flow_x.keep,))
    for bit in order_a[4:]:
        ab, flow_cd = advance([[ab], [flow_cd]])
    flow_x, small, out_send = advance([[flow_x, flow_y, flow_o]], (input_grad,), (out_send,), (small, got_small))
    result = result_call(me, mid, out_keep, swap_mp(out_send))
    got_small = exchange(small, order_a[2])
    down_grad, up_grad = ffn_finish_call(ab, flow_cd, (result,))
    cols, block = w_out.shape[0], width // n
    flow_x, small = advance([[flow_x]], (up_grad,), (), (small, got_small))
    for bit in order_a[3:-1]:
        flow_x, small = advance([[flow_x]], (), (), (small, exchange(small, bit)))
    got_small = exchange(small, order_a[-1])

    def finish_qkv(which, sums, outs):
        outs[0][0] = sums[0][:, :cols]
        outs[0][1, :, : cols // 2] = sums[0][:, cols : cols + cols // 2]
        outs[0][2] = sums[0][:, cols + cols // 2 : 2 * cols + cols // 2]
        outs[0][1, :, cols // 2 :] = sums[0][:, 2 * cols + cols // 2 : 3 * cols]
        outs[1][...] = sums[0][:, 3 * cols :].T

    qkv_grad, wout_grad, small = advance(
        [[flow_x]], (), (), (small, got_small), finish_qkv, [shape((3, block, cols), F32), shape((cols, block), F32)]
    )
    return (
        result[None],
        compressed[None],
        input_grad[None],
        small[0] / gain_attn,
        qkv_grad,
        small[2, : slopes.shape[0]],
        wout_grad,
        small[1] / gain_ffn,
        up_grad,
        down_grad,
        jnp.stack([comp_part[:, r * cols : (r + 1) * cols] for r in range(3)]),
    )


def solution(mesh):
    placed = (
        P("dp", "mp", None),
        P("dp", None, None),
        P("dp", None, None),
        P("dp", None),
        P("dp"),
        P("dp"),
        P(),
        P(None, None, "mp"),
        P("mp"),
        P("mp", None),
        P(),
        P(None, "mp"),
        P("mp", None),
        P(None, None, "mp"),
        P("dp", "mp", None),
        P("dp", None, "mp"),
    )
    return jax.shard_map(
        shards,
        mesh=mesh,
        in_specs=placed,
        out_specs=(
            P("dp", "mp", None),
            P("dp", None, "mp"),
            P("dp", "mp", None),
            P(),
            P(None, "dp", "mp"),
            P("mp"),
            P("mp", "dp"),
            P(),
            P("dp", "mp"),
            P("mp", "dp"),
            P(None, "dp", "mp"),
        ),
        check_vma=False,
    )
```

```python
from functools import partial

import jax
import jax.numpy as jnp
from jax import lax
from jax.experimental import pallas as pl
from jax.experimental.pallas import tpu as pltpu
from jax.sharding import PartitionSpec as P

F32, BF16 = jnp.float32, jnp.bfloat16
VMEM_LIMIT = 60 * 1024 * 1024
HEAD = 128
TILE = 256
KEYS = 256
MEM_KEYS = 448
LOG2E = 1.4426950408889634
HIDE = -1e30
COST = pl.CostEstimate(flops=1, bytes_accessed=1, transcendentals=1)


def dot(a, b):
    return jnp.dot(a, b, preferred_element_type=F32)


def dot_nt(a, b):
    return lax.dot_general(a, b, (((1,), (1,)), ((), ())), preferred_element_type=F32)


def shape(dims, kind=BF16):
    return jax.ShapeDtypeStruct(dims, kind)


def whole(dims):
    return pl.BlockSpec(dims, lambda *_: (0,) * len(dims))


def call(body, out_shape, in_specs, out_specs, grid=(1,), scratch=(), scalars=1, after=()):
    ins = scalars + len(in_specs)

    def without(*refs):
        body(*refs[:ins], *refs[ins + len(after) :])

    in_specs = list(in_specs) + [pl.BlockSpec(memory_space=pl.ANY)] * len(after)
    run = pl.pallas_call(
        without,
        grid_spec=pltpu.PrefetchScalarGridSpec(
            num_scalar_prefetch=scalars,
            grid=grid,
            in_specs=in_specs,
            out_specs=out_specs,
            scratch_shapes=scratch,
        ),
        out_shape=out_shape,
        compiler_params=pltpu.CompilerParams(vmem_limit_bytes=VMEM_LIMIT),
        cost_estimate=COST,
    )
    return lambda *args: run(*args, *after)


def put_blocks(me, order, result, send, keep, cols=slice(None), to=slice(None)):
    half, rows = send.shape[0], send.shape[1]
    bits = len(order)
    for place in range(2 * half):
        rel = 0
        for k, bit in enumerate(order):
            rel |= ((place >> (bits - 1 - k)) & 1) << bit
        start = pl.multiple_of((me ^ rel) * rows, rows)
        out = send if place >= half else keep
        out[place % half, :, to] = result[pl.ds(start, rows), cols]


def layer_norm(rows, gain):
    centre = jnp.mean(rows, axis=-1, keepdims=True)
    centred = rows - centre
    spread = jnp.mean(centred * centred, axis=-1, keepdims=True)
    return centred * lax.rsqrt(spread + 1e-05) * gain


def layer_norm_back(rows, gain, grad):
    centre = jnp.mean(rows, axis=-1, keepdims=True)
    centred = rows - centre
    spread = jnp.mean(centred * centred, axis=-1, keepdims=True)
    inverse = lax.rsqrt(spread + 1e-05)
    unit = centred * inverse
    pulled = grad * gain
    return inverse * (
        pulled
        - jnp.mean(pulled, axis=-1, keepdims=True)
        - unit * jnp.mean(pulled * unit, axis=-1, keepdims=True)
    )


def gelu_parts(u):
    bell = jnp.exp2(u * u * (-0.5 * LOG2E))
    t = 1.0 / (1.0 + (0.3275911 * 0.7071067811865476) * jnp.abs(u))
    series = 0.7107068705 + t * (-0.7265760135 + t * 0.5307027145)
    tail = t * (0.127414796 + t * (-0.142248368 + t * series)) * bell
    return jnp.where(u >= 0, 1.0 - tail, tail), u * bell * 0.3989422804014327


def comp_body(_, mem_ref, w_ref, grad_ref, out_ref, wgrad_ref, wide):
    count = out_ref.shape[0]
    groups = mem_ref.shape[1] // HEAD
    for c in range(groups):
        wide[pl.ds(c * 3 * count, 3 * count), :] = mem_ref[:, c * HEAD : (c + 1) * HEAD].astype(F32)
    total = None
    cols = grad_ref.shape[1]
    for r in range(3):
        rows = jnp.concatenate([wide[pl.ds(c * 3 * count + r, count, stride=3), :] for c in range(groups)], axis=1)
        part = dot(rows.astype(BF16), w_ref[r])
        total = part if total is None else total + part
        wgrad_ref[:, r * cols : (r + 1) * cols] = dot(rows.T.astype(BF16), grad_ref[...]).astype(BF16)
    out_ref[...] = total.astype(BF16)


def comp_call(me, memory, w_comp, comp_grad):
    rows, width = memory.shape
    cols = w_comp.shape[2]
    return call(
        comp_body,
        [shape((rows // 3, cols)), shape((width, 3 * cols))],
        [whole(memory.shape), whole(w_comp.shape), whole(comp_grad.shape)],
        [whole((rows // 3, cols)), whole((width, 3 * cols))],
        scratch=[pltpu.VMEM((rows * width // HEAD, HEAD), F32)],
    )(me, memory, w_comp, comp_grad)


def context_body(tiles, _, a_ref, b_ref, gain_ref, w_ref, nt_ref, k_ref, v_ref):
    low_x = jnp.where(pl.program_id(0) < tiles, a_ref[...], b_ref[...])
    normed = layer_norm(low_x.astype(F32), gain_ref[...]).astype(BF16)
    nt_ref[...] = normed.T
    k_ref[...] = dot(normed, w_ref[1]).astype(BF16)
    v_ref[...] = dot(normed, w_ref[2]).astype(BF16)


def context_call(me, cmem, mem, gain, w_qkv, tile, after=()):
    width = mem.shape[1]
    count = cmem.shape[0] + mem.shape[0]
    tiles = cmem.shape[0] // tile
    cols = w_qkv.shape[2]
    return call(
        partial(context_body, tiles),
        [shape((width, count))] + [shape((count, cols))] * 2,
        [
            pl.BlockSpec((tile, width), lambda i, _: (jnp.minimum(i, tiles - 1), 0)),
            pl.BlockSpec((tile, width), lambda i, _: (jnp.maximum(i - tiles, 0), 0)),
            whole(gain.shape),
            whole(w_qkv.shape),
        ],
        [pl.BlockSpec((width, tile), lambda i, _: (0, i))]
        + [pl.BlockSpec((tile, cols), lambda i, _: (i, 0))] * 2,
        grid=(count // tile,),
        after=after,
    )(me, cmem, mem, gain, w_qkv)


def tokens_body(tiles, me_ref, own_ref, other_ref, gain_ref, w_ref, x_ref, nt_ref, q_ref, k_ref, v_ref):
    mine = pl.program_id(0) // tiles == me_ref[1]
    low_x = jnp.where(mine, own_ref[...], other_ref[...])
    x_ref[...] = low_x
    normed = layer_norm(low_x.astype(F32), gain_ref[...]).astype(BF16)
    nt_ref[...] = normed.T
    q_ref[...] = dot(normed, w_ref[0]).astype(BF16)
    k_ref[...] = dot(normed, w_ref[1]).astype(BF16)
    v_ref[...] = dot(normed, w_ref[2]).astype(BF16)


def tokens_call(me, own, other, gain, w_qkv, tile, after=()):
    half, width = own.shape
    count = 2 * half
    cols = w_qkv.shape[2]
    tiles = half // tile
    side = pl.BlockSpec((tile, width), lambda i, _: (i % tiles, 0))
    tall = pl.BlockSpec((tile, cols), lambda i, _: (i, 0))
    return call(
        partial(tokens_body, tiles),
        [shape((count, width)), shape((width, count)), shape((count, cols))]
        + [shape((count, cols))] * 2,
        [side, side, whole(gain.shape), whole(w_qkv.shape)],
        [
            pl.BlockSpec((tile, width), lambda i, _: (i, 0)),
            pl.BlockSpec((width, tile), lambda i, _: (0, i)),
            tall,
        ]
        + [tall] * 2,
        grid=(count // tile,),
        after=after,
    )(me, own, other, gain, w_qkv)


def flip_body(tiles, me_ref, own_ref, other_ref, x_ref, xt_ref):
    mine = pl.program_id(0) // tiles == me_ref[1]
    low = jnp.where(mine, own_ref[...], other_ref[...])
    x_ref[...] = low
    xt_ref[...] = low.T


def flip_call(me, own, other, tile, after=()):
    half, width = own.shape
    tiles = half // tile
    side = pl.BlockSpec((tile, width), lambda i, _: (i % tiles, 0))
    return call(
        partial(flip_body, tiles),
        [shape((2 * half, width)), shape((width, 2 * half))],
        [side, side],
        [
            pl.BlockSpec((tile, width), lambda i, _: (i, 0)),
            pl.BlockSpec((width, tile), lambda i, _: (0, i)),
        ],
        grid=(2 * tiles,),
        after=after,
    )(me, own, other)


def document_start(places, docs_ref):
    first = jnp.zeros_like(places)
    for d in range(1, docs_ref.shape[1]):
        first = jnp.where(places >= docs_ref[0, d], docs_ref[0, d], first)
    return first


def down(start, count):
    return start + lax.broadcasted_iota(jnp.int32, (count, 1), 0)


def memory_bias(start, count, cmem, mem, valid_ref, slope):
    index = down(start, count)
    compressed = index < cmem
    place = jnp.where(compressed, 3 * index - (mem + 3 * cmem), index - (cmem + mem))
    seen = index >= jnp.where(compressed, cmem - valid_ref[1], cmem + mem - valid_ref[0])
    return jnp.where(seen, place.astype(F32) * slope, HIDE)


def cut(of_memory, start, end, size):
    return [(of_memory, at, min(size, end - at)) for at in range(start, end, size)]


def key_blocks(i, tokens, memory):
    blocks = cut(True, 0, memory, MEM_KEYS) if i * TILE < tokens // 2 else []
    return blocks + cut(False, 0, i * TILE, KEYS) + cut(False, i * TILE, (i + 1) * TILE, KEYS)


def hide(scores, of_memory, start, count, i, places, first, docs_ref):
    if of_memory:
        return jnp.where(places < docs_ref[0, 1], scores, HIDE)
    index = down(start, count)
    visible = index >= first
    if start + count > i * TILE:
        visible = visible & (index <= places)
    return jnp.where(visible, scores, HIDE)


def forward_body(
    cmem, mem, me_ref, docs_ref, valid_ref, slopes_ref, q_ref, k_ref, v_ref, kc_ref, vc_ref, w_ref,
    att_ref, part_ref, ot_ref, lse_ref, vt_ref, vct_ref, score_ref, all_ref,
):
    h = pl.program_id(0)
    tokens = q_ref.shape[0]
    scale = HEAD**-0.5
    power = scale * LOG2E
    slope = slopes_ref[h] / scale
    vt_ref[...] = v_ref[...].T
    vct_ref[...] = vc_ref[...].T
    for i in range(tokens // TILE):
        queries = slice(i * TILE, (i + 1) * TILE)
        places = i * TILE + lax.broadcasted_iota(jnp.int32, (1, TILE), 1)
        first = document_start(places, docs_ref)
        blocks = key_blocks(i, tokens, cmem + mem)
        top = jnp.full((8, TILE), HIDE, F32)
        at = 0
        for of_memory, start, count in blocks:
            keys = (kc_ref if of_memory else k_ref)[start : start + count, :]
            if of_memory:
                bias = memory_bias(start, count, cmem, mem, valid_ref, slope)
            else:
                bias = down(start, count).astype(F32) * slope
            scores = hide(dot_nt(keys, q_ref[queries, :]) + bias, of_memory, start, count, i, places, first, docs_ref)
            score_ref[i % 2, at : at + count, :] = scores
            at += count
            top = jnp.maximum(top, jnp.max(scores.reshape(-1, 8, TILE), axis=0))
        top = jnp.max(top, axis=0, keepdims=True)
        total = jnp.zeros((8, TILE), F32)
        out = jnp.zeros((HEAD, TILE), F32)
        at = 0
        for of_memory, start, count in blocks:
            probs = jnp.exp2((score_ref[i % 2, at : at + count, :] - top) * power)
            at += count
            total = total + jnp.sum(probs.reshape(-1, 8, TILE), axis=0)
            out = out + dot((vct_ref if of_memory else vt_ref)[:, start : start + count], probs.astype(BF16))
        total = jnp.sum(total, axis=0, keepdims=True)
        out = out * (1.0 / total)
        ot_ref[:, queries] = out
        low = out.T.astype(BF16)
        att_ref[queries, :] = low
        all_ref[h, queries, :] = low
        lse_ref[0, :, queries] = top * power + jnp.log2(total)

    @pl.when(h == pl.num_programs(0) - 1)
    def _():
        for i in range(tokens // TILE):
            rows = slice(i * TILE, (i + 1) * TILE)
            low = jnp.concatenate([all_ref[g, rows, :] for g in range(all_ref.shape[0])], axis=1)
            part_ref[rows, :] = dot(low, w_ref[...]).astype(BF16)


def forward_call(me, docs, valid, slopes, q, k, v, kc, vc, w_out, cmem, mem, tie=()):
    count, cols = q.shape
    width = w_out.shape[1]
    heads = slopes.shape[0]
    head = pl.BlockSpec((count, HEAD), lambda h, *_: (0, h))
    head_c = pl.BlockSpec((cmem + mem, HEAD), lambda h, *_: (0, h))
    return call(
        partial(forward_body, cmem, mem),
        [shape((count, cols)), shape((count, width)), shape((cols, count), F32), shape((heads, 1, count), F32)],
        [head, head, head, head_c, head_c, whole(w_out.shape)],
        [
            head,
            whole((count, width)),
            pl.BlockSpec((HEAD, count), lambda h, *_: (h, 0)),
            pl.BlockSpec((1, 1, count), lambda h, *_: (h, 0, 0)),
        ],
        grid=(heads,),
        scratch=[
            pltpu.VMEM((HEAD, count), BF16),
            pltpu.VMEM((HEAD, cmem + mem), BF16),
            pltpu.VMEM((2, count + cmem + mem, TILE), F32),
            pltpu.VMEM((heads, count, HEAD), BF16),
        ],
        scalars=4,
    )(me, docs, valid, slopes, q, k, v, kc, vc, w_out)


def backward_body(
    cmem, mem, me_ref, docs_ref, valid_ref, slopes_ref, q_ref, g_ref, ot_ref, lse_ref, k_ref, v_ref, kc_ref, vc_ref,
    gq_ref, gk_ref, gv_ref, gkc_ref, gvc_ref, slope_ref, kt_ref, kct_ref, acck, accv, acckc, accvc,
):
    h = pl.program_id(0)
    tokens = q_ref.shape[0]
    scale = HEAD**-0.5
    power = scale * LOG2E
    slope = slopes_ref[h] * LOG2E
    row = lax.broadcasted_iota(jnp.int32, (8, 1), 0)
    for keys, flipped, memory in ((k_ref, kt_ref, False), (kc_ref, kct_ref, True)):
        flipped[:HEAD, :] = keys[...].T
        index = lax.broadcasted_iota(jnp.int32, (1, keys.shape[0]), 1)
        place = index
        if memory:
            place = jnp.where(index < cmem, 3 * index - (mem + 3 * cmem), index - (cmem + mem))
        high = (place >> 4) << 4
        extra = jnp.where(row == 0, high, jnp.where(row == 1, place - high, jnp.where(row == 2, 1, 0)))
        flipped[HEAD:, :] = jnp.concatenate([extra, jnp.zeros_like(extra)], axis=0).astype(F32).astype(BF16)
    slope_sum = jnp.zeros((1, TILE), F32)
    for i in range(tokens // TILE):
        queries = slice(i * TILE, (i + 1) * TILE)
        places = i * TILE + lax.broadcasted_iota(jnp.int32, (1, TILE), 1)
        first = document_start(places, docs_ref)
        gt = g_ref[queries, :].T
        delta = jnp.sum(gt.astype(F32) * ot_ref[:, queries], axis=0, keepdims=True)
        lse = lse_ref[0, :, queries]
        sum_q = jnp.zeros((HEAD + 16, TILE), F32)
        for of_memory, start, count in key_blocks(i, tokens, cmem + mem):
            rows = slice(start, start + count)
            keys, values = (kc_ref, vc_ref) if of_memory else (k_ref, v_ref)
            if of_memory:
                bias = memory_bias(start, count, cmem, mem, valid_ref, slope)
            else:
                bias = down(start, count).astype(F32) * slope
            scores = dot_nt(keys[rows, :], q_ref[queries, :]) * power + bias
            scores = hide(scores - lse, of_memory, start, count, i, places, first, docs_ref)
            probs = jnp.exp2(scores)
            grad = (probs * (dot(values[rows, :], gt) - delta)).astype(BF16)
            part_v = dot(probs.astype(BF16), g_ref[queries, :])
            part_k = dot(grad, q_ref[queries, :])
            sum_k, sum_v = (acckc, accvc) if of_memory else (acck, accv)
            fresh = i == 0 if of_memory else start >= i * TILE
            sum_v[rows, :] = part_v if fresh else sum_v[rows, :] + part_v
            sum_k[rows, :] = part_k if fresh else sum_k[rows, :] + part_k
            sum_q = sum_q + dot((kct_ref if of_memory else kt_ref)[:, rows], grad)
        gq_ref[queries, :] = (sum_q[:HEAD] * scale).T.astype(BF16)
        far = places.astype(F32) * sum_q[HEAD + 2 : HEAD + 3] - sum_q[HEAD : HEAD + 1] - sum_q[HEAD + 1 : HEAD + 2]
        slope_sum = slope_sum - far
    slope_ref[0] = slope_sum
    gk_ref[...] = (acck[...] * scale).astype(BF16)
    gkc_ref[...] = (acckc[...] * scale).astype(BF16)
    gv_ref[...] = accv[...].astype(BF16)
    gvc_ref[...] = accvc[...].astype(BF16)


def backward_call(me, docs, valid, slopes, q, g, ot, lse, k, v, kc, vc, cmem, mem, after=()):
    count, cols = q.shape
    heads = slopes.shape[0]
    head = pl.BlockSpec((count, HEAD), lambda h, *_: (0, h))
    head_c = pl.BlockSpec((cmem + mem, HEAD), lambda h, *_: (0, h))
    return call(
        partial(backward_body, cmem, mem),
        [shape((count, cols))] * 3 + [shape(kc.shape)] * 2 + [shape((heads, 1, TILE), F32)],
        [
            head,
            head,
            pl.BlockSpec((HEAD, count), lambda h, *_: (h, 0)),
            pl.BlockSpec((1, 1, count), lambda h, *_: (h, 0, 0)),
            head,
            head,
            head_c,
            head_c,
        ],
        [head] * 3 + [head_c] * 2 + [pl.BlockSpec((1, 1, TILE), lambda h, *_: (h, 0, 0))],
        grid=(heads,),
        scratch=[pltpu.VMEM((HEAD + 16, count), BF16), pltpu.VMEM((HEAD + 16, cmem + mem), BF16)]
        + [pltpu.VMEM((count, HEAD), F32)] * 2
        + [pltpu.VMEM((cmem + mem, HEAD), F32)] * 2,
        scalars=4,
        after=after,
    )(me, docs, valid, slopes, q, g, ot, lse, k, v, kc, vc)


def middle_body(_, x_ref, a_ref, b_ref, gain_ref, mid_ref, n_ref, nt_ref):
    mid = x_ref[...].astype(F32) + (a_ref[...].astype(F32) + b_ref[...].astype(F32))
    mid_ref[...] = mid
    normed = layer_norm(mid, gain_ref[...]).astype(BF16)
    n_ref[...] = normed
    nt_ref[...] = normed.T


def middle_call(me, x, part, other, gain):
    count, width = x.shape
    tall = pl.BlockSpec((TILE, width), lambda i, _: (i, 0))
    return call(
        middle_body,
        [shape((count, width), F32), shape((count, width)), shape((width, count))],
        [tall, tall, tall, whole(gain.shape)],
        [tall, tall, pl.BlockSpec((width, TILE), lambda i, _: (0, i))],
        grid=(count // TILE,),
    )(me, x, part, other, gain)


class Copies:
    def __init__(self, sems):
        self.sems, self.count, self.open = sems, 0, []

    def start(self, source, target):
        copy = pltpu.make_async_copy(source, target, self.sems.at[self.count])
        self.count += 1
        copy.start()
        self.open.append(copy)
        return copy

    def finish(self):
        for copy in self.open:
            copy.wait()
        self.open = []


def ship(copies, me, order, result, outs, cols):
    send, keep = outs
    half, rows, width = send.shape
    bits = len(order)
    to = slice(cols.start % width, cols.start % width + cols.stop - cols.start)
    for place in range(2 * half):
        rel = 0
        for k, bit in enumerate(order):
            rel |= ((place >> (bits - 1 - k)) & 1) << bit
        start = pl.multiple_of((me ^ rel) * rows, rows)
        out = send if place >= half else keep
        copies.start(result.at[pl.ds(start, rows), cols], out.at[place % half, :, to])


def ffn_body(orders, second, step, me_ref, *refs):
    if second:
        n_in, nt_in, g_in, gt_in, up_in, down_in, hid_in, gpre_in, *refs = refs
        down_outs, up_outs, refs = refs[:2], refs[2 : 2 * len(orders)], refs[2 * len(orders) :]
        gain_out, out_send, out_keep, *refs = refs
        rows_out, refs = refs[: len(refs) - 15], refs[len(refs) - 15 :]
        n, nt, g, gt, up, down, hid, gpre, res_down, res_up, gain, rows, part, in_sems, out_sems = refs
    else:
        n_in, nt_in, g_in, gt_in, up_in, down_in, *refs = refs
        down_outs, up_outs, refs = refs[:2], refs[2 : 2 * len(orders)], refs[2 * len(orders) :]
        gain_out, hid_out, gpre_out, *refs = refs
        n, nt, g, gt, up, down, hid, gpre, res_down, res_up, gain, in_sems, out_sems = refs
    tokens, width = n.shape
    size = res_down.shape[1]
    base = size if second else 0
    ins, outs = Copies(in_sems), Copies(out_sems)
    mine = slice(base, base + size)
    waits = {}
    for name, source, target in (
        ("n", n_in, n),
        ("up", up_in.at[:, mine], up.at[:, mine]),
        ("g", g_in, g),
        ("down", down_in.at[mine, :], down.at[mine, :]),
        ("gt", gt_in, gt),
        ("nt", nt_in, nt),
    ):
        waits[name] = ins.start(source, target)
    if second:
        for name, source, target in (
            ("gpre", gpre_in, gpre.at[:, :size]),
            ("up2", up_in.at[:, :size], up.at[:, :size]),
            ("hid", hid_in, hid.at[:, :size]),
            ("down2", down_in.at[:size, :], down.at[:size, :]),
        ):
            waits[name] = ins.start(source, target)
    for at in range(base, base + size, step):
        cols = slice(at, at + step)
        local = slice(at - base, at - base + step)
        for i in range(tokens // TILE):
            part_rows = slice(i * TILE, (i + 1) * TILE)
            if at == base and i == 0:
                waits["n"].wait()
                waits["up"].wait()
            pre = dot(n[part_rows, :], up[:, cols])
            if at == base and i == 0:
                waits["g"].wait()
                waits["down"].wait()
            back = dot_nt(g[part_rows, :], down[cols, :])
            cdf, bell = gelu_parts(pre)
            hid[part_rows, cols] = (pre * cdf).astype(BF16)
            gpre[part_rows, cols] = (back * (cdf + bell)).astype(BF16)
        if not second:
            outs.start(hid.at[:, cols], hid_out.at[:, cols])
            outs.start(gpre.at[:, cols], gpre_out.at[:, cols])
        if at == base:
            waits["gt"].wait()
        for i in range(width // TILE):
            part_rows = slice(i * TILE, (i + 1) * TILE)
            res_down[part_rows, local] = dot(gt[part_rows, :], hid[:, cols]).astype(BF16)
        ship(outs, me_ref[0], orders[0], res_down, down_outs, local)
        if at == base:
            waits["nt"].wait()
        for i in range(width // TILE):
            part_rows = slice(i * TILE, (i + 1) * TILE)
            grad = dot(nt[part_rows, :], gpre[:, cols])
            res_up[part_rows, local] = grad.astype(BF16)
            dotted = grad * up[part_rows, cols].astype(F32)
            total = sum(dotted[:, c : c + HEAD] for c in range(0, step, HEAD))
            gain[part_rows, :] = total if at == base else gain[part_rows, :] + total
        which = 2 * ((at - base) * (len(orders) - 1) // size)
        ship(outs, me_ref[0], orders[1 + which // 2], res_up, up_outs[which : which + 2], local)
    outs.start(gain, gain_out)
    if second:
        waits["gpre"].wait()
        waits["up2"].wait()
        for t in range(width // TILE):
            cols = slice(t * TILE, (t + 1) * TILE)
            rows[:, cols] = dot_nt(gpre[...], up[cols, :]).astype(BF16)
        chunk = tokens // len(rows_out)
        for i, target in enumerate(rows_out):
            outs.start(rows.at[i * chunk : (i + 1) * chunk, :], target)
        waits["hid"].wait()
        waits["down2"].wait()
        half = tokens // 2
        for t in range(width // TILE):
            cols = slice(t * TILE, (t + 1) * TILE)
            part[:, cols] = dot(hid[...], down[:, cols]).astype(BF16)
        for core, target in ((1 - me_ref[1], out_send), (me_ref[1], out_keep)):
            outs.start(part.at[pl.ds(pl.multiple_of(core * half, half), half), :], target)
    outs.finish()


def ffn_call(me, n2, n2t, g, gt, w_up, w_down, before, n, orders, step=512, after=()):
    tokens, width = n2.shape
    hidden = w_up.shape[1]
    size = hidden // 2
    second = len(before) > 0
    anywhere = pl.BlockSpec(memory_space=pl.ANY)
    ups = len(orders) - 1
    outs = [shape((n // 2, width // n, size))] * 2 + [shape((n // 2, width // n, size // ups))] * (2 * ups)
    outs += [shape((width, HEAD), F32)]
    scratch = [pltpu.VMEM(a.shape, BF16) for a in (n2, n2t, g, gt, w_up, w_down)]
    scratch += [pltpu.VMEM((tokens, hidden), BF16)] * 2 + [pltpu.VMEM((width, size), BF16)] * 2
    scratch += [pltpu.VMEM((width, HEAD), F32)]
    copies = 2 * n * (size // step) + 1
    if second:
        outs += [shape((tokens // 2, width))] * 2 + [shape((tokens // 2, width))] * 2
        scratch += [pltpu.VMEM((tokens, width), BF16)] * 2
        copies += 4
    else:
        outs += [shape((tokens, size))] * 2
        copies += 2 * (size // step)
    scratch += [pltpu.SemaphoreType.DMA((10,)), pltpu.SemaphoreType.DMA((copies,))]
    ins = 7 + len(before)

    def body(*refs):
        ffn_body(orders, second, step, *refs[:ins], *refs[ins + len(after) :])

    return pl.pallas_call(
        body,
        out_shape=outs,
        in_specs=[pl.BlockSpec(memory_space=pltpu.SMEM)] + [anywhere] * (ins - 1 + len(after)),
        out_specs=[anywhere] * len(outs),
        scratch_shapes=scratch,
        compiler_params=pltpu.CompilerParams(vmem_limit_bytes=VMEM_LIMIT),
        cost_estimate=COST,
    )(me, n2, n2t, g, gt, w_up, w_down, *before, *after)


def turn_body(
    order, me_ref, mid_ref, gain_ref, g_ref, att_ref, w_ref, a_ref, b_ref, c_ref, d_ref, gmid_ref, gatt_ref, send, keep, low_t, res
):
    i = pl.program_id(0)
    early = i < pl.num_programs(0) // 2
    own, other = jnp.where(early, a_ref[...], b_ref[...]), jnp.where(early, c_ref[...], d_ref[...])
    grad = own.astype(F32) + other.astype(F32)
    total = g_ref[...].astype(F32) + layer_norm_back(mid_ref[...], gain_ref[...], grad)
    gmid_ref[...] = total
    low = total.astype(BF16)
    gatt_ref[...] = dot_nt(low, w_ref[...]).astype(BF16)
    low_t[:, pl.ds(pl.multiple_of(i * TILE, TILE), TILE)] = low.T

    @pl.when(i == pl.num_programs(0) - 1)
    def _():
        for t in range(low_t.shape[0] // TILE):
            rows = pl.ds(t * TILE, TILE)
            res[rows, :] = dot(low_t[rows, :], att_ref[...]).astype(BF16)
        put_blocks(me_ref[0], order, res, send, keep)


def turn_call(me, mid, gain, g, parts, others, attended, w_out, n, order, after=()):
    count, width = mid.shape
    cols = attended.shape[1]
    tall = pl.BlockSpec((TILE, width), lambda i, _: (i, 0))
    tiles = count // 2 // TILE
    early = pl.BlockSpec((TILE, width), lambda i, _: (jnp.minimum(i, tiles - 1), 0))
    late = pl.BlockSpec((TILE, width), lambda i, _: (jnp.maximum(i - tiles, 0), 0))
    piece = (n // 2, width // n, cols)
    return call(
        partial(turn_body, order),
        [shape((count, width), F32), shape((count, cols)), shape(piece), shape(piece)],
        [tall, whole(gain.shape), tall, whole(attended.shape), whole(w_out.shape), early, late, early, late],
        [tall, pl.BlockSpec((TILE, cols), lambda i, _: (i, 0)), whole(piece), whole(piece)],
        grid=(count // TILE,),
        scratch=[pltpu.VMEM((width, count), BF16), pltpu.VMEM((width, cols), BF16)],
        after=after,
    )(me, mid, gain, g, attended, w_out, *parts, *others)


def across(sums):
    return jnp.sum(sums.T, axis=0, keepdims=True)


def qkv_grad_body(
    orders, me_ref, nt_ref, nct_ref, gq_ref, gk_ref, gkc_ref, gv_ref, gvc_ref, w_ref, up_a, up_b, slope_ref, small_ref,
    *rest,
):
    outs, res, gain_ref = rest[:-2], rest[-2], rest[-1]
    pairs = ((gq_ref, None), (gk_ref, gkc_ref), (gv_ref, gvc_ref))
    for which, (tokens, context) in enumerate(pairs):
        for t in range(nt_ref.shape[0] // TILE):
            rows = pl.ds(t * TILE, TILE)
            grad = dot(nt_ref[rows, :], tokens[...])
            if context is not None:
                grad = grad + dot(nct_ref[rows, :], context[...])
            res[rows, :] = grad.astype(BF16)
            dotted = grad * w_ref[which, rows, :].astype(F32)
            total = sum(dotted[:, c : c + HEAD] for c in range(0, dotted.shape[1], HEAD))
            gain_ref[rows, :] = total if which == 0 else gain_ref[rows, :] + total
        size = res.shape[1]
        if which == 1:
            for flow in range(2):
                from_k = slice(flow * size // 2, (flow + 1) * size // 2)
                put_blocks(me_ref[0], orders[flow], res, outs[2 * flow], outs[2 * flow + 1], from_k, slice(size, size + size // 2))
        else:
            flow = which // 2
            put_blocks(me_ref[0], orders[flow], res, outs[2 * flow], outs[2 * flow + 1], slice(None), slice(0, size))
    small_ref[...] = jnp.zeros(small_ref.shape, F32)
    small_ref[0:1, :] = across(gain_ref[...])
    small_ref[1:2, :] = across(up_a[...] + up_b[...])
    lane = lax.broadcasted_iota(jnp.int32, (1, HEAD), 1)
    slopes = jnp.zeros((1, HEAD), F32)
    for h in range(slope_ref.shape[0]):
        slopes = jnp.where(lane == h, jnp.sum(slope_ref[h], axis=1, keepdims=True), slopes)
    small_ref[2:3, :HEAD] = slopes


def qkv_grad_call(me, nt, nct, gq, gk, gkc, gv, gvc, w_qkv, up_a, up_b, slope, n, orders, after=()):
    width = nt.shape[0]
    cols = gq.shape[1]
    piece = (n // 2, width // n, 3 * cols // 2)
    ins = (nt, nct, gq, gk, gkc, gv, gvc, w_qkv, up_a, up_b, slope)
    return call(
        partial(qkv_grad_body, orders),
        [shape((8, width), F32)] + [shape(piece)] * 4,
        [whole(a.shape) for a in ins],
        [whole((8, width))] + [whole(piece)] * 4,
        scratch=[pltpu.VMEM((width, cols), BF16), pltpu.VMEM((width, HEAD), F32)],
        after=after,
    )(me, *ins)


def rows_grad_body(tiles, _, gq_ref, gk_ref, gv_ref, w_ref, send, keep):
    total = dot_nt(gq_ref[...], w_ref[0]) + dot_nt(gk_ref[...], w_ref[1]) + dot_nt(gv_ref[...], w_ref[2])

    @pl.when(pl.program_id(0) < tiles)
    def _():
        send[...] = total.astype(BF16)

    @pl.when(pl.program_id(0) >= tiles)
    def _():
        keep[...] = total.astype(BF16)


def rows_grad_call(me, gq, gk, gv, w_qkv, after=()):
    count, cols = gq.shape
    width = w_qkv.shape[1]
    tiles = count // 2 // TILE
    tall = pl.BlockSpec((TILE, cols), lambda i, m: ((i + (1 - m[1]) * tiles) % (2 * tiles), 0))
    return call(
        partial(rows_grad_body, tiles),
        [shape((count // 2, width))] * 2,
        [tall, tall, tall, whole(w_qkv.shape)],
        [
            pl.BlockSpec((TILE, width), lambda i, _: (jnp.minimum(i, tiles - 1), 0)),
            pl.BlockSpec((TILE, width), lambda i, _: (jnp.maximum(i - tiles, 0), 0)),
        ],
        grid=(2 * tiles,),
        after=after,
    )(me, gq, gk, gv, w_qkv)


def last_body(_, x_ref, gain_ref, a_ref, b_ref, gmid_ref, out_ref):
    grad = a_ref[...].astype(F32) + b_ref[...].astype(F32)
    back = layer_norm_back(x_ref[...].astype(F32), gain_ref[...], grad)
    out_ref[...] = (gmid_ref[...] + back).astype(BF16)


def last_call(me, x, gain, part, other, gmid, after=()):
    count, width = x.shape
    rows = TILE // 2
    tall = pl.BlockSpec((rows, width), lambda i, _: (i, 0))
    tiles = count // rows
    mine = pl.BlockSpec((rows, width), lambda i, m: (i + m[1] * tiles, 0))
    return call(
        last_body, shape((count, width)), [tall, whole(gain.shape), tall, tall, mine], tall, grid=(tiles,), after=after
    )(me, x, gain, part, other, gmid)


def result_body(_, mid_ref, a_ref, b_ref, out_ref):
    out_ref[...] = (mid_ref[...] + (a_ref[...].astype(F32) + b_ref[...].astype(F32))).astype(BF16)


def result_call(me, mid, part, other, after=()):
    count, width = part.shape
    rows = TILE // 2
    tall = pl.BlockSpec((rows, width), lambda i, _: (i, 0))
    tiles = count // rows
    mine = pl.BlockSpec((rows, width), lambda i, m: (i + m[1] * tiles, 0))
    return call(
        result_body, shape((count, width)), [mine, tall, tall], tall, grid=(tiles,), after=after
    )(me, mid, part, other)


def swap_mp(rows):
    return lax.ppermute(rows, "mp", [(0, 1), (1, 0)])


class Flow:
    def __init__(self, send, keep, order):
        self.send, self.keep, self.order = send, keep, order
        n = lax.axis_size("dp")
        self.got = lax.ppermute(send, "dp", [(i, i ^ (1 << order[0])) for i in range(n)])


def exchange(array, bit):
    return lax.ppermute(array, "dp", [(i, i ^ (1 << bit)) for i in range(lax.axis_size("dp"))])


def add_body(plan, finish, skip, *refs):
    ins, outs = refs[: 2 * sum(plan)], refs[2 * sum(plan) + skip :]
    at = place = 0
    for which, count in enumerate(plan):
        pairs = [(ins[2 * i], ins[2 * i + 1]) for i in range(at, at + count)]
        at += count
        if len(pairs[0][0].shape) == 2:
            outs[-1][...] = pairs[0][0][...] + pairs[0][1][...]
            continue
        if finish is not None:
            finish(which, [keep[0].astype(F32) + got[0].astype(F32) for keep, got in pairs], outs)
            continue
        if len(pairs[0][0].shape) == 3:
            outs[place][...] = pairs[0][0][0].astype(F32) + pairs[0][1][0].astype(F32)
            place += 1
            continue
        col = 0
        place += 2
        for keep, got in pairs:
            to = slice(col, col + keep.shape[3])
            col += keep.shape[3]
            for half, out in ((1, outs[place - 2]), (0, outs[place - 1])):
                out[:, :, to] = (keep[half].astype(F32) + got[half].astype(F32)).astype(BF16)


def advance(groups, after=(), through=(), small=None, finish=None, finals=(), hold=()):
    ins, in_specs, outs, out_specs = [], [], [], []
    last = finish is not None
    steps = 1 if last else max(1, min(group[0].keep.shape[0] for group in groups) // 2)
    for group in groups:
        half = group[0].keep.shape[0] // 2
        size = half // steps
        for flow in group:
            for a in (flow.keep, flow.got):
                _, rows, cols = a.shape
                ins.append(a if half == 0 else a.reshape(2, half, rows, cols))
                in_specs.append(whole(a.shape) if half == 0 else pl.BlockSpec((2, size, rows, cols), lambda i: (0, i, 0, 0)))
        cols = sum(flow.keep.shape[2] for flow in group)
        if half == 0 and not last:
            outs.append(shape((rows, cols), F32))
            out_specs.append(whole((rows, cols)))
        elif not last:
            outs += [shape((half, rows, cols))] * 2
            out_specs += [pl.BlockSpec((size, rows, cols), lambda i: (i, 0, 0))] * 2
    outs += list(finals)
    out_specs += [whole(a.shape) for a in finals]
    plan = [len(group) for group in groups]
    if small is not None:
        ins += list(small)
        in_specs += [whole(small[0].shape)] * 2
        outs.append(shape(small[0].shape, F32))
        out_specs.append(whole(small[0].shape))
        plan.append(1)
    anywhere = pl.BlockSpec(memory_space=pl.ANY)
    results = pl.pallas_call(
        lambda *refs: add_body(plan, finish, len(through) + len(after), *refs[: len(refs) - len(through)]),
        grid=(steps,),
        out_shape=outs + [shape(a.shape, a.dtype) for a in through],
        in_specs=in_specs + [anywhere] * (len(through) + len(after)),
        out_specs=out_specs + [anywhere] * len(through),
        input_output_aliases={len(ins) + i: len(outs) + i for i in range(len(through))},
        compiler_params=pltpu.CompilerParams(vmem_limit_bytes=VMEM_LIMIT),
        cost_estimate=COST,
    )(*ins, *through, *after)
    sums, rest = list(results[: len(outs)]), list(results[len(outs) :])
    tail = [sums.pop()] if small is not None else []
    if not last:
        flat, sums = sums, []
        for i, group in enumerate(groups):
            if group[0].keep.shape[0] == 1:
                sums.append(flat.pop(0))
            elif i in hold:
                sums.append((flat.pop(0), flat.pop(0)))
            else:
                sums.append(Flow(flat.pop(0), flat.pop(0), group[0].order[1:]))
    return sums + tail + rest


def finished(flow):
    return advance([[flow]])[0] if isinstance(flow, Flow) else flow


def ffn_finish_body(first_ref, second_ref, comp_ref, down_ref, up_ref, out_ref):
    cols = out_ref.shape[2]
    for r in range(3):
        out_ref[r] = comp_ref[:, r * cols : (r + 1) * cols].astype(F32)
    size = first_ref.shape[1] // 2
    for which, total_ref in enumerate((first_ref, second_ref)):
        here = slice(which * size, (which + 1) * size)
        down_ref[:, here] = total_ref[:, :size]
        up_ref[:, here] = total_ref[:, size:]


def ffn_finish_call(first, second, comp, after):
    block, hidden = first.shape
    ins = (first, second, comp)
    parts = (3, block, comp.shape[1] // 3)
    return call(
        lambda _, *refs: ffn_finish_body(*refs),
        [shape((block, hidden), F32)] * 2 + [shape(parts, F32)],
        [whole(a.shape) for a in ins],
        [whole((block, hidden))] * 2 + [whole(parts)],
        after=after,
    )(jnp.zeros((1,), jnp.int32), *ins)


def shards(
    inputs, memory, compressed_memory, doc_starts, mem_valid, cmem_valid, gain_attn, w_qkv, slopes, w_out, gain_ffn,
    w_up, w_down, w_comp, out_grad, comp_grad,
):
    n = lax.axis_size("dp")
    bits = n.bit_length() - 1
    rest = list(range(2, bits))
    order_a, order_b, order_o = [0, 1] + rest, [1, 0] + rest, [2, 0, 1] + rest[1:]
    half, width = inputs.shape[1:]
    mem, cmem = memory.shape[1], compressed_memory.shape[1]
    core = lax.axis_index("mp")
    me = jnp.stack([lax.axis_index("dp"), core]).astype(jnp.int32)
    valid = jnp.stack([mem_valid[0], cmem_valid[0]])
    gain1, gain2 = gain_attn[None], gain_ffn[None]

    other_x = swap_mp(inputs[0])
    other_g = swap_mp(out_grad[0])

    compressed, comp = comp_call(me, memory[0], w_comp, comp_grad[0])
    comp_part = lax.psum_scatter(comp, "dp", scatter_dimension=0, tiled=True)

    nct, kc, vc = context_call(me, compressed_memory[0], memory[0], gain1, w_qkv, HEAD, (compressed,))
    x, nt, q, k, v = tokens_call(me, inputs[0], other_x, gain1, w_qkv, TILE, (other_g,))
    attended, part, out_t, lse = forward_call(
        me, doc_starts, valid, slopes, q, k, v, kc, vc, w_out, cmem, mem
    )
    g, gt = flip_call(me, out_grad[0], other_g, TILE, (part,))
    mid, n2, n2t = middle_call(me, x, part, swap_mp(part), gain2)

    down1_s, down1_k, up1_s, up1_k, gain_a, *before = ffn_call(
        me, n2, n2t, g, gt, w_up, w_down, (), n, (order_a, order_b)
    )
    flow_a, flow_b = Flow(down1_s, down1_k, order_a), Flow(up1_s, up1_k, order_b)
    down2_s, down2_k, up2_s, up2_k, gain_b, out_send, out_keep, *parts = ffn_call(
        me, n2, n2t, g, gt, w_up, w_down, before, n, (order_a, order_b)
    )
    others = [swap_mp(a) for a in parts]
    flow_a, flow_b, down2_s, up2_s = advance([[flow_a], [flow_b]], (parts[0],), (down2_s, up2_s))
    flow_c, flow_d = Flow(down2_s, down2_k, order_a), Flow(up2_s, up2_k, order_b)
    gmid, gatt, wout_s, wout_k = turn_call(
        me, mid, gain2, g, parts, others, attended, w_out, n, order_o, (flow_a.keep,)
    )
    flow_o = Flow(wout_s, wout_k, order_o)
    gq, gk, gv, gkc, gvc, slope = backward_call(
        me, doc_starts, valid, slopes, q, gatt, out_t, lse, k, v, kc, vc, cmem, mem
    )
    flow_ab, flow_c, flow_d, flow_o = advance([[flow_a, flow_b], [flow_c], [flow_d], [flow_o]], (gq,))
    small, qx_s, qx_k, qy_s, qy_k = qkv_grad_call(
        me, nt, nct, gq, gk, gkc, gv, gvc, w_qkv, gain_a, gain_b, slope, n, (order_a, order_b),
        (flow_c.keep, comp_part),
    )
    flow_ab, flow_cd, held, qx_s, qy_s, small = advance(
        [[flow_ab], [flow_c, flow_d], [flow_o]], (qx_k,), (qx_s, qy_s, small), hold=(2,)
    )
    flow_x, flow_y = Flow(qx_s, qx_k, order_a), Flow(qy_s, qy_k, order_b)
    gain_rows = jnp.arange(small.shape[0])[:, None] < 2
    small = small + jnp.where(gain_rows, swap_mp(small), 0.0)
    got_small = exchange(small, order_a[0])
    rows_send, rows_keep = rows_grad_call(me, gq, gk, gv, w_qkv, (flow_cd.keep,))
    flow_x, flow_y, flow_cd, ab, small, held_send = advance(
        [[flow_x], [flow_y], [flow_cd], [flow_ab]], (rows_keep,), (held[0],), (small, got_small)
    )
    flow_o = Flow(held_send, held[1], order_o[2:])
    got_small = exchange(small, order_a[1])
    flow_x, flow_o, cd, small, rows_send = advance(
        [[flow_x, flow_y], [flow_o], [flow_cd]], (), (rows_send,), (small, got_small)
    )
    got_small = exchange(small, order_a[2])
    while isinstance(cd, Flow):
        ab, cd = finished(ab), finished(cd)
    down_grad, up_grad, comp_grads = ffn_finish_call(ab, cd, comp_part, (flow_x.keep,))
    input_grad = last_call(me, inputs[0], gain1, rows_keep, swap_mp(rows_send), gmid, (up_grad,))
    cols, block = w_out.shape[0], width // n
    flow_x, small, out_send = advance([[flow_x]], (input_grad,), (out_send,), (small, got_small))
    result = result_call(me, mid, out_keep, swap_mp(out_send))
    for bit in order_a[3:-1]:
        flow_x, flow_o, small = advance([[flow_x], [flow_o]], (), (), (small, exchange(small, bit)))
    got_small = exchange(small, order_a[-1])

    def finish_qkv(which, sums, outs):
        total = sums[0]
        if which == 1:
            outs[1][...] = total
            return
        outs[0][0] = total[:, :cols]
        outs[0][1, :, : cols // 2] = total[:, cols : cols + cols // 2]
        outs[0][2] = total[:, cols + cols // 2 : 2 * cols + cols // 2]
        outs[0][1, :, cols // 2 :] = total[:, 2 * cols + cols // 2 :]

    qkv_grad, wout_grad, small = advance(
        [[flow_x], [flow_o]], (result,), (), (small, got_small), finish_qkv,
        [shape((3, block, cols), F32), shape((block, cols), F32)],
    )
    return (
        result[None],
        compressed[None],
        input_grad[None],
        small[0] / gain_attn,
        qkv_grad,
        small[2, : slopes.shape[0]],
        wout_grad.T,
        small[1] / gain_ffn,
        up_grad,
        down_grad.T,
        comp_grads,
    )


def solution(mesh):
    placed = (
        P("dp", "mp", None),
        P("dp", None, None),
        P("dp", None, None),
        P("dp", None),
        P("dp"),
        P("dp"),
        P(),
        P(None, None, "mp"),
        P("mp"),
        P("mp", None),
        P(),
        P(None, "mp"),
        P("mp", None),
        P(None, None, "mp"),
        P("dp", "mp", None),
        P("dp", None, "mp"),
    )
    return jax.shard_map(
        shards,
        mesh=mesh,
        in_specs=placed,
        out_specs=(
            P("dp", "mp", None),
            P("dp", None, "mp"),
            P("dp", "mp", None),
            P(),
            P(None, "dp", "mp"),
            P("mp"),
            P("mp", "dp"),
            P(),
            P("dp", "mp"),
            P("mp", "dp"),
            P(None, "dp", "mp"),
        ),
        check_vma=False,
    )
```

```python
from functools import partial

import jax
import jax.numpy as jnp
from jax import lax
from jax.experimental import pallas as pl
from jax.experimental.pallas import tpu as pltpu
from jax.sharding import PartitionSpec as P

F32, BF16 = jnp.float32, jnp.bfloat16
VMEM_LIMIT = 64 * 1024 * 1024
HEAD = 128
TILE = 256
KEYS = 256
MEM_KEYS = 448
LOG2E = 1.4426950408889634
HIDE = -1e30
COST = pl.CostEstimate(flops=1, bytes_accessed=1, transcendentals=1)


def dot(a, b):
    return jnp.dot(a, b, preferred_element_type=F32)


def dot_nt(a, b):
    return lax.dot_general(a, b, (((1,), (1,)), ((), ())), preferred_element_type=F32)


def shape(dims, kind=BF16):
    return jax.ShapeDtypeStruct(dims, kind)


def whole(dims):
    return pl.BlockSpec(dims, lambda *_: (0,) * len(dims))


def call(body, out_shape, in_specs, out_specs, grid=(1,), scratch=(), scalars=1, after=()):
    ins = scalars + len(in_specs)

    def without(*refs):
        body(*refs[:ins], *refs[ins + len(after) :])

    in_specs = list(in_specs) + [pl.BlockSpec(memory_space=pl.ANY)] * len(after)
    run = pl.pallas_call(
        without,
        grid_spec=pltpu.PrefetchScalarGridSpec(
            num_scalar_prefetch=scalars,
            grid=grid,
            in_specs=in_specs,
            out_specs=out_specs,
            scratch_shapes=scratch,
        ),
        out_shape=out_shape,
        compiler_params=pltpu.CompilerParams(vmem_limit_bytes=VMEM_LIMIT),
        cost_estimate=COST,
    )
    return lambda *args: run(*args, *after)


def put_blocks(me, order, result, send, keep, cols=slice(None), to=slice(None)):
    half, rows = send.shape[0], send.shape[1]
    bits = len(order)
    for place in range(2 * half):
        rel = 0
        for k, bit in enumerate(order):
            rel |= ((place >> (bits - 1 - k)) & 1) << bit
        start = pl.multiple_of((me ^ rel) * rows, rows)
        out = send if place >= half else keep
        out[place % half, :, to] = result[pl.ds(start, rows), cols]


def layer_norm(rows, gain):
    centre = jnp.mean(rows, axis=-1, keepdims=True)
    centred = rows - centre
    spread = jnp.mean(centred * centred, axis=-1, keepdims=True)
    return centred * lax.rsqrt(spread + 1e-05) * gain


def layer_norm_back(rows, gain, grad):
    centre = jnp.mean(rows, axis=-1, keepdims=True)
    centred = rows - centre
    spread = jnp.mean(centred * centred, axis=-1, keepdims=True)
    inverse = lax.rsqrt(spread + 1e-05)
    unit = centred * inverse
    pulled = grad * gain
    return inverse * (
        pulled
        - jnp.mean(pulled, axis=-1, keepdims=True)
        - unit * jnp.mean(pulled * unit, axis=-1, keepdims=True)
    )


def gelu_parts(u):
    bell = jnp.exp2(u * u * (-0.5 * LOG2E))
    t = 1.0 / (1.0 + (0.3275911 * 0.7071067811865476) * jnp.abs(u))
    series = 0.7107068705 + t * (-0.7265760135 + t * 0.5307027145)
    tail = t * (0.127414796 + t * (-0.142248368 + t * series)) * bell
    return jnp.where(u >= 0, 1.0 - tail, tail), u * bell * 0.3989422804014327


def comp_body(_, mem_ref, w_ref, grad_ref, out_ref, wgrad_ref, wide):
    count = out_ref.shape[0]
    groups = mem_ref.shape[1] // HEAD
    for c in range(groups):
        wide[pl.ds(c * 3 * count, 3 * count), :] = mem_ref[:, c * HEAD : (c + 1) * HEAD].astype(F32)
    total = None
    cols = grad_ref.shape[1]
    for r in range(3):
        rows = jnp.concatenate([wide[pl.ds(c * 3 * count + r, count, stride=3), :] for c in range(groups)], axis=1)
        part = dot(rows.astype(BF16), w_ref[r])
        total = part if total is None else total + part
        wgrad_ref[:, r * cols : (r + 1) * cols] = dot(rows.T.astype(BF16), grad_ref[...]).astype(BF16)
    out_ref[...] = total.astype(BF16)


def comp_call(me, memory, w_comp, comp_grad):
    rows, width = memory.shape
    cols = w_comp.shape[2]
    return call(
        comp_body,
        [shape((rows // 3, cols)), shape((width, 3 * cols))],
        [whole(memory.shape), whole(w_comp.shape), whole(comp_grad.shape)],
        [whole((rows // 3, cols)), whole((width, 3 * cols))],
        scratch=[pltpu.VMEM((rows * width // HEAD, HEAD), F32)],
    )(me, memory, w_comp, comp_grad)


def context_body(_, a_ref, b_ref, gain_ref, w_ref, nt_ref, k_ref, v_ref):
    at = 0
    for x_ref in (a_ref, b_ref):
        rows = slice(at, at + x_ref.shape[0])
        at += x_ref.shape[0]
        normed = layer_norm(x_ref[...].astype(F32), gain_ref[...]).astype(BF16)
        nt_ref[:, rows] = normed.T
        k_ref[rows, :] = dot(normed, w_ref[1]).astype(BF16)
        v_ref[rows, :] = dot(normed, w_ref[2]).astype(BF16)


def context_call(me, cmem, mem, gain, w_qkv, after=()):
    width, cols = mem.shape[1], w_qkv.shape[2]
    count = cmem.shape[0] + mem.shape[0]
    ins = (cmem, mem, gain, w_qkv)
    outs = [(width, count), (count, cols), (count, cols)]
    return call(
        context_body,
        [shape(dims) for dims in outs],
        [whole(a.shape) for a in ins],
        [whole(dims) for dims in outs],
        after=after,
    )(me, *ins)


def tokens_body(tiles, me_ref, own_ref, other_ref, gain_ref, w_ref, x_ref, nt_ref, q_ref, k_ref, v_ref):
    mine = pl.program_id(0) // tiles == me_ref[1]
    low_x = jnp.where(mine, own_ref[...], other_ref[...])
    x_ref[...] = low_x
    normed = layer_norm(low_x.astype(F32), gain_ref[...]).astype(BF16)
    nt_ref[...] = normed.T
    q_ref[...] = dot(normed, w_ref[0]).astype(BF16)
    k_ref[...] = dot(normed, w_ref[1]).astype(BF16)
    v_ref[...] = dot(normed, w_ref[2]).astype(BF16)


def tokens_call(me, own, other, gain, w_qkv, tile, after=()):
    half, width = own.shape
    count = 2 * half
    cols = w_qkv.shape[2]
    tiles = half // tile
    side = pl.BlockSpec((tile, width), lambda i, _: (i % tiles, 0))
    tall = pl.BlockSpec((tile, cols), lambda i, _: (i, 0))
    return call(
        partial(tokens_body, tiles),
        [shape((count, width)), shape((width, count)), shape((count, cols))]
        + [shape((count, cols))] * 2,
        [side, side, whole(gain.shape), whole(w_qkv.shape)],
        [
            pl.BlockSpec((tile, width), lambda i, _: (i, 0)),
            pl.BlockSpec((width, tile), lambda i, _: (0, i)),
            tall,
        ]
        + [tall] * 2,
        grid=(count // tile,),
        after=after,
    )(me, own, other, gain, w_qkv)


def flip_body(tiles, me_ref, own_ref, other_ref, x_ref, xt_ref):
    mine = pl.program_id(0) // tiles == me_ref[1]
    low = jnp.where(mine, own_ref[...], other_ref[...])
    x_ref[...] = low
    xt_ref[...] = low.T


def flip_call(me, own, other, tile, after=()):
    half, width = own.shape
    tiles = half // tile
    side = pl.BlockSpec((tile, width), lambda i, _: (i % tiles, 0))
    return call(
        partial(flip_body, tiles),
        [shape((2 * half, width)), shape((width, 2 * half))],
        [side, side],
        [
            pl.BlockSpec((tile, width), lambda i, _: (i, 0)),
            pl.BlockSpec((width, tile), lambda i, _: (0, i)),
        ],
        grid=(2 * tiles,),
        after=after,
    )(me, own, other)


def document_start(places, docs_ref):
    first = jnp.zeros_like(places)
    for d in range(1, docs_ref.shape[1]):
        first = jnp.where(places >= docs_ref[0, d], docs_ref[0, d], first)
    return first


def down(start, count):
    return start + lax.broadcasted_iota(jnp.int32, (count, 1), 0)


def memory_bias(start, count, cmem, mem, valid_ref, slope):
    index = down(start, count)
    compressed = index < cmem
    place = jnp.where(compressed, 3 * index - (mem + 3 * cmem), index - (cmem + mem))
    seen = index >= jnp.where(compressed, cmem - valid_ref[1], cmem + mem - valid_ref[0])
    return jnp.where(seen, place.astype(F32) * slope, HIDE)


def cut(of_memory, start, end, size):
    return [(of_memory, at, min(size, end - at)) for at in range(start, end, size)]


def key_blocks(i, tokens, memory):
    blocks = cut(True, 0, memory, MEM_KEYS) if i * TILE < tokens // 2 else []
    return blocks + cut(False, 0, i * TILE, KEYS) + cut(False, i * TILE, (i + 1) * TILE, KEYS)


def hide(scores, of_memory, start, count, i, places, first, docs_ref):
    if of_memory:
        return jnp.where(places < docs_ref[0, 1], scores, HIDE)
    index = down(start, count)
    visible = index >= first
    if start + count > i * TILE:
        visible = visible & (index <= places)
    return jnp.where(visible, scores, HIDE)


def forward_body(
    cmem, mem, me_ref, docs_ref, valid_ref, slopes_ref, q_ref, k_ref, v_ref, kc_ref, vc_ref, w_ref,
    att_ref, part_ref, ot_ref, lse_ref, vt_ref, vct_ref, score_ref, all_ref,
):
    h = pl.program_id(0)
    tokens = q_ref.shape[0]
    scale = HEAD**-0.5
    power = scale * LOG2E
    slope = slopes_ref[h] / scale
    vt_ref[...] = v_ref[...].T
    vct_ref[...] = vc_ref[...].T
    for i in range(tokens // TILE):
        queries = slice(i * TILE, (i + 1) * TILE)
        places = i * TILE + lax.broadcasted_iota(jnp.int32, (1, TILE), 1)
        first = document_start(places, docs_ref)
        blocks = key_blocks(i, tokens, cmem + mem)
        top = jnp.full((8, TILE), HIDE, F32)
        at = 0
        for of_memory, start, count in blocks:
            keys = (kc_ref if of_memory else k_ref)[start : start + count, :]
            if of_memory:
                bias = memory_bias(start, count, cmem, mem, valid_ref, slope)
            else:
                bias = down(start, count).astype(F32) * slope
            scores = hide(dot_nt(keys, q_ref[queries, :]) + bias, of_memory, start, count, i, places, first, docs_ref)
            score_ref[i % 2, at : at + count, :] = scores
            at += count
            top = jnp.maximum(top, jnp.max(scores.reshape(-1, 8, TILE), axis=0))
        top = jnp.max(top, axis=0, keepdims=True)
        total = jnp.zeros((8, TILE), F32)
        out = jnp.zeros((HEAD, TILE), F32)
        at = 0
        for of_memory, start, count in blocks:
            probs = jnp.exp2((score_ref[i % 2, at : at + count, :] - top) * power)
            at += count
            total = total + jnp.sum(probs.reshape(-1, 8, TILE), axis=0)
            out = out + dot((vct_ref if of_memory else vt_ref)[:, start : start + count], probs.astype(BF16))
        total = jnp.sum(total, axis=0, keepdims=True)
        out = out * (1.0 / total)
        ot_ref[:, queries] = out
        low = out.T.astype(BF16)
        att_ref[queries, :] = low
        all_ref[h, queries, :] = low
        lse_ref[0, :, queries] = top * power + jnp.log2(total)

    @pl.when(h == pl.num_programs(0) - 1)
    def _():
        for i in range(tokens // TILE):
            rows = slice(i * TILE, (i + 1) * TILE)
            low = jnp.concatenate([all_ref[g, rows, :] for g in range(all_ref.shape[0])], axis=1)
            part_ref[rows, :] = dot(low, w_ref[...]).astype(BF16)


def forward_call(me, docs, valid, slopes, q, k, v, kc, vc, w_out, cmem, mem, tie=()):
    count, cols = q.shape
    width = w_out.shape[1]
    heads = slopes.shape[0]
    head = pl.BlockSpec((count, HEAD), lambda h, *_: (0, h))
    head_c = pl.BlockSpec((cmem + mem, HEAD), lambda h, *_: (0, h))
    return call(
        partial(forward_body, cmem, mem),
        [shape((count, cols)), shape((count, width)), shape((cols, count), F32), shape((heads, 1, count), F32)],
        [head, head, head, head_c, head_c, whole(w_out.shape)],
        [
            head,
            whole((count, width)),
            pl.BlockSpec((HEAD, count), lambda h, *_: (h, 0)),
            pl.BlockSpec((1, 1, count), lambda h, *_: (h, 0, 0)),
        ],
        grid=(heads,),
        scratch=[
            pltpu.VMEM((HEAD, count), BF16),
            pltpu.VMEM((HEAD, cmem + mem), BF16),
            pltpu.VMEM((2, count + cmem + mem, TILE), F32),
            pltpu.VMEM((heads, count, HEAD), BF16),
        ],
        scalars=4,
    )(me, docs, valid, slopes, q, k, v, kc, vc, w_out)


def backward_body(
    cmem, mem, me_ref, docs_ref, valid_ref, slopes_ref, q_ref, g_ref, ot_ref, lse_ref, k_ref, v_ref, kc_ref, vc_ref,
    gq_ref, gk_ref, gv_ref, gkc_ref, gvc_ref, slope_ref, kt_ref, kct_ref, acck, accv, acckc, accvc,
):
    h = pl.program_id(0)
    tokens = q_ref.shape[0]
    scale = HEAD**-0.5
    power = scale * LOG2E
    slope = slopes_ref[h] * LOG2E
    row = lax.broadcasted_iota(jnp.int32, (8, 1), 0)
    for keys, flipped, memory in ((k_ref, kt_ref, False), (kc_ref, kct_ref, True)):
        flipped[:HEAD, :] = keys[...].T
        index = lax.broadcasted_iota(jnp.int32, (1, keys.shape[0]), 1)
        place = index
        if memory:
            place = jnp.where(index < cmem, 3 * index - (mem + 3 * cmem), index - (cmem + mem))
        high = (place >> 4) << 4
        extra = jnp.where(row == 0, high, jnp.where(row == 1, place - high, jnp.where(row == 2, 1, 0)))
        flipped[HEAD:, :] = jnp.concatenate([extra, jnp.zeros_like(extra)], axis=0).astype(F32).astype(BF16)
    slope_sum = jnp.zeros((1, TILE), F32)
    for i in range(tokens // TILE):
        queries = slice(i * TILE, (i + 1) * TILE)
        places = i * TILE + lax.broadcasted_iota(jnp.int32, (1, TILE), 1)
        first = document_start(places, docs_ref)
        gt = g_ref[queries, :].T
        delta = jnp.sum(gt.astype(F32) * ot_ref[:, queries], axis=0, keepdims=True)
        lse = lse_ref[0, :, queries]
        sum_q = jnp.zeros((HEAD + 16, TILE), F32)
        for of_memory, start, count in key_blocks(i, tokens, cmem + mem):
            rows = slice(start, start + count)
            keys, values = (kc_ref, vc_ref) if of_memory else (k_ref, v_ref)
            if of_memory:
                bias = memory_bias(start, count, cmem, mem, valid_ref, slope)
            else:
                bias = down(start, count).astype(F32) * slope
            scores = dot_nt(keys[rows, :], q_ref[queries, :]) * power + bias
            scores = hide(scores - lse, of_memory, start, count, i, places, first, docs_ref)
            probs = jnp.exp2(scores)
            grad = (probs * (dot(values[rows, :], gt) - delta)).astype(BF16)
            part_v = dot(probs.astype(BF16), g_ref[queries, :])
            part_k = dot(grad, q_ref[queries, :])
            sum_k, sum_v = (acckc, accvc) if of_memory else (acck, accv)
            fresh = i == 0 if of_memory else start >= i * TILE
            sum_v[rows, :] = part_v if fresh else sum_v[rows, :] + part_v
            sum_k[rows, :] = part_k if fresh else sum_k[rows, :] + part_k
            sum_q = sum_q + dot((kct_ref if of_memory else kt_ref)[:, rows], grad)
        gq_ref[queries, :] = (sum_q[:HEAD] * scale).T.astype(BF16)
        far = places.astype(F32) * sum_q[HEAD + 2 : HEAD + 3] - sum_q[HEAD : HEAD + 1] - sum_q[HEAD + 1 : HEAD + 2]
        slope_sum = slope_sum - far
    slope_ref[0] = slope_sum
    gk_ref[...] = (acck[...] * scale).astype(BF16)
    gkc_ref[...] = (acckc[...] * scale).astype(BF16)
    gv_ref[...] = accv[...].astype(BF16)
    gvc_ref[...] = accvc[...].astype(BF16)


def backward_call(me, docs, valid, slopes, q, g, ot, lse, k, v, kc, vc, cmem, mem, after=()):
    count, cols = q.shape
    heads = slopes.shape[0]
    head = pl.BlockSpec((count, HEAD), lambda h, *_: (0, h))
    head_c = pl.BlockSpec((cmem + mem, HEAD), lambda h, *_: (0, h))
    return call(
        partial(backward_body, cmem, mem),
        [shape((count, cols))] * 3 + [shape(kc.shape)] * 2 + [shape((heads, 1, TILE), F32)],
        [
            head,
            head,
            pl.BlockSpec((HEAD, count), lambda h, *_: (h, 0)),
            pl.BlockSpec((1, 1, count), lambda h, *_: (h, 0, 0)),
            head,
            head,
            head_c,
            head_c,
        ],
        [head] * 3 + [head_c] * 2 + [pl.BlockSpec((1, 1, TILE), lambda h, *_: (h, 0, 0))],
        grid=(heads,),
        scratch=[pltpu.VMEM((HEAD + 16, count), BF16), pltpu.VMEM((HEAD + 16, cmem + mem), BF16)]
        + [pltpu.VMEM((count, HEAD), F32)] * 2
        + [pltpu.VMEM((cmem + mem, HEAD), F32)] * 2,
        scalars=4,
        after=after,
    )(me, docs, valid, slopes, q, g, ot, lse, k, v, kc, vc)


def middle_body(_, x_ref, a_ref, b_ref, gain_ref, mid_ref, n_ref, nt_ref):
    mid = x_ref[...].astype(F32) + (a_ref[...].astype(F32) + b_ref[...].astype(F32))
    mid_ref[...] = mid
    normed = layer_norm(mid, gain_ref[...]).astype(BF16)
    n_ref[...] = normed
    nt_ref[...] = normed.T


def middle_call(me, x, part, other, gain, rows=512):
    count, width = x.shape
    tall = pl.BlockSpec((rows, width), lambda i, _: (i, 0))
    return call(
        middle_body,
        [shape((count, width), F32), shape((count, width)), shape((width, count))],
        [tall, tall, tall, whole(gain.shape)],
        [tall, tall, pl.BlockSpec((width, rows), lambda i, _: (0, i))],
        grid=(count // rows,),
    )(me, x, part, other, gain)


class Copies:
    def __init__(self, sems):
        self.sems, self.count, self.open = sems, 0, []

    def start(self, source, target):
        copy = pltpu.make_async_copy(source, target, self.sems.at[self.count])
        self.count += 1
        copy.start()
        self.open.append(copy)
        return copy

    def finish(self):
        for copy in self.open:
            copy.wait()
        self.open = []


def ship(copies, me, order, result, outs, cols):
    send, keep = outs
    half, rows, width = send.shape
    bits = len(order)
    to = slice(cols.start % width, cols.start % width + cols.stop - cols.start)
    for place in range(2 * half):
        rel = 0
        for k, bit in enumerate(order):
            rel |= ((place >> (bits - 1 - k)) & 1) << bit
        start = pl.multiple_of((me ^ rel) * rows, rows)
        out = send if place >= half else keep
        copies.start(result.at[pl.ds(start, rows), cols], out.at[place % half, :, to])


def ffn_body(orders, second, step, me_ref, *refs):
    if second:
        n_in, nt_in, g_in, gt_in, up_in, down_in, hid_in, gpre_in, *refs = refs
        down_outs, up_outs, refs = refs[:2], refs[2 : 2 * len(orders)], refs[2 * len(orders) :]
        gain_out, out_send, out_keep, *refs = refs
        rows_out, refs = refs[: len(refs) - 15], refs[len(refs) - 15 :]
        n, nt, g, gt, up, down, hid, gpre, res_down, res_up, gain, rows, part, in_sems, out_sems = refs
    else:
        n_in, nt_in, g_in, gt_in, up_in, down_in, *refs = refs
        down_outs, up_outs, refs = refs[:2], refs[2 : 2 * len(orders)], refs[2 * len(orders) :]
        gain_out, hid_out, gpre_out, *refs = refs
        n, nt, g, gt, up, down, hid, gpre, res_down, res_up, gain, in_sems, out_sems = refs
    tokens, width = n.shape
    size = res_down.shape[1]
    base = size if second else 0
    ins, outs = Copies(in_sems), Copies(out_sems)
    mine = slice(base, base + size)
    waits = {}
    for name, source, target in (
        ("n", n_in, n),
        ("up", up_in.at[:, mine], up.at[:, mine]),
        ("g", g_in, g),
        ("down", down_in.at[mine, :], down.at[mine, :]),
        ("gt", gt_in, gt),
        ("nt", nt_in, nt),
    ):
        waits[name] = ins.start(source, target)
    if second:
        for name, source, target in (
            ("gpre", gpre_in, gpre.at[:, :size]),
            ("up2", up_in.at[:, :size], up.at[:, :size]),
            ("hid", hid_in, hid.at[:, :size]),
            ("down2", down_in.at[:size, :], down.at[:size, :]),
        ):
            waits[name] = ins.start(source, target)
    for at in range(base, base + size, step):
        cols = slice(at, at + step)
        local = slice(at - base, at - base + step)
        for i in range(tokens // TILE):
            part_rows = slice(i * TILE, (i + 1) * TILE)
            if at == base and i == 0:
                waits["n"].wait()
                waits["up"].wait()
            pre = dot(n[part_rows, :], up[:, cols])
            if at == base and i == 0:
                waits["g"].wait()
                waits["down"].wait()
            back = dot_nt(g[part_rows, :], down[cols, :])
            cdf, bell = gelu_parts(pre)
            hid[part_rows, cols] = (pre * cdf).astype(BF16)
            gpre[part_rows, cols] = (back * (cdf + bell)).astype(BF16)
        if not second:
            outs.start(hid.at[:, cols], hid_out.at[:, cols])
            outs.start(gpre.at[:, cols], gpre_out.at[:, cols])
        if at == base:
            waits["gt"].wait()
        for i in range(width // TILE):
            part_rows = slice(i * TILE, (i + 1) * TILE)
            res_down[part_rows, local] = dot(gt[part_rows, :], hid[:, cols]).astype(BF16)
        ship(outs, me_ref[0], orders[0], res_down, down_outs, local)
        if at == base:
            waits["nt"].wait()
        for i in range(width // TILE):
            part_rows = slice(i * TILE, (i + 1) * TILE)
            grad = dot(nt[part_rows, :], gpre[:, cols])
            res_up[part_rows, local] = grad.astype(BF16)
            dotted = grad * up[part_rows, cols].astype(F32)
            total = sum(dotted[:, c : c + HEAD] for c in range(0, step, HEAD))
            gain[part_rows, :] = total if at == base else gain[part_rows, :] + total
        which = 2 * ((at - base) * (len(orders) - 1) // size)
        ship(outs, me_ref[0], orders[1 + which // 2], res_up, up_outs[which : which + 2], local)
    outs.start(gain, gain_out)
    if second:
        waits["gpre"].wait()
        waits["up2"].wait()
        for t in range(width // TILE):
            cols = slice(t * TILE, (t + 1) * TILE)
            rows[:, cols] = dot_nt(gpre[...], up[cols, :]).astype(BF16)
        chunk = tokens // len(rows_out)
        for i, target in enumerate(rows_out):
            outs.start(rows.at[i * chunk : (i + 1) * chunk, :], target)
        waits["hid"].wait()
        waits["down2"].wait()
        half = tokens // 2
        for t in range(width // TILE):
            cols = slice(t * TILE, (t + 1) * TILE)
            part[:, cols] = dot(hid[...], down[:, cols]).astype(BF16)
        for core, target in ((1 - me_ref[1], out_send), (me_ref[1], out_keep)):
            outs.start(part.at[pl.ds(pl.multiple_of(core * half, half), half), :], target)
    outs.finish()


def ffn_call(me, n2, n2t, g, gt, w_up, w_down, before, n, orders, step=512, after=()):
    tokens, width = n2.shape
    hidden = w_up.shape[1]
    size = hidden // 2
    second = len(before) > 0
    anywhere = pl.BlockSpec(memory_space=pl.ANY)
    ups = len(orders) - 1
    outs = [shape((n // 2, width // n, size))] * 2 + [shape((n // 2, width // n, size // ups))] * (2 * ups)
    outs += [shape((width, HEAD), F32)]
    scratch = [pltpu.VMEM(a.shape, BF16) for a in (n2, n2t, g, gt, w_up, w_down)]
    scratch += [pltpu.VMEM((tokens, hidden), BF16)] * 2 + [pltpu.VMEM((width, size), BF16)] * 2
    scratch += [pltpu.VMEM((width, HEAD), F32)]
    copies = 2 * n * (size // step) + 1
    if second:
        outs += [shape((tokens // 2, width))] * 2 + [shape((tokens // 2, width))] * 2
        scratch += [pltpu.VMEM((tokens, width), BF16)] * 2
        copies += 4
    else:
        outs += [shape((tokens, size))] * 2
        copies += 2 * (size // step)
    scratch += [pltpu.SemaphoreType.DMA((10,)), pltpu.SemaphoreType.DMA((copies,))]
    ins = 7 + len(before)

    def body(*refs):
        ffn_body(orders, second, step, *refs[:ins], *refs[ins + len(after) :])

    return pl.pallas_call(
        body,
        out_shape=outs,
        in_specs=[pl.BlockSpec(memory_space=pltpu.SMEM)] + [anywhere] * (ins - 1 + len(after)),
        out_specs=[anywhere] * len(outs),
        scratch_shapes=scratch,
        compiler_params=pltpu.CompilerParams(vmem_limit_bytes=VMEM_LIMIT),
        cost_estimate=COST,
    )(me, n2, n2t, g, gt, w_up, w_down, *before, *after)


def turn_body(
    order, me_ref, mid_ref, gain_ref, g_ref, att_ref, w_ref, a_ref, b_ref, c_ref, d_ref, gmid_ref, gatt_ref, send, keep, low_t, res
):
    i = pl.program_id(0)
    early = i < pl.num_programs(0) // 2
    own, other = jnp.where(early, a_ref[...], b_ref[...]), jnp.where(early, c_ref[...], d_ref[...])
    grad = own.astype(F32) + other.astype(F32)
    total = g_ref[...].astype(F32) + layer_norm_back(mid_ref[...], gain_ref[...], grad)
    gmid_ref[...] = total
    low = total.astype(BF16)
    gatt_ref[...] = dot_nt(low, w_ref[...]).astype(BF16)
    low_t[:, pl.ds(pl.multiple_of(i * TILE, TILE), TILE)] = low.T

    @pl.when(i == pl.num_programs(0) - 1)
    def _():
        for t in range(low_t.shape[0] // TILE):
            rows = pl.ds(t * TILE, TILE)
            res[rows, :] = dot(low_t[rows, :], att_ref[...]).astype(BF16)
        put_blocks(me_ref[0], order, res, send, keep)


def turn_call(me, mid, gain, g, parts, others, attended, w_out, n, order, after=()):
    count, width = mid.shape
    cols = attended.shape[1]
    tall = pl.BlockSpec((TILE, width), lambda i, _: (i, 0))
    tiles = count // 2 // TILE
    early = pl.BlockSpec((TILE, width), lambda i, _: (jnp.minimum(i, tiles - 1), 0))
    late = pl.BlockSpec((TILE, width), lambda i, _: (jnp.maximum(i - tiles, 0), 0))
    piece = (n // 2, width // n, cols)
    return call(
        partial(turn_body, order),
        [shape((count, width), F32), shape((count, cols)), shape(piece), shape(piece)],
        [tall, whole(gain.shape), tall, whole(attended.shape), whole(w_out.shape), early, late, early, late],
        [tall, pl.BlockSpec((TILE, cols), lambda i, _: (i, 0)), whole(piece), whole(piece)],
        grid=(count // TILE,),
        scratch=[pltpu.VMEM((width, count), BF16), pltpu.VMEM((width, cols), BF16)],
        after=after,
    )(me, mid, gain, g, attended, w_out, *parts, *others)


def across(sums):
    return jnp.sum(sums.T, axis=0, keepdims=True)


def qkv_grad_body(
    orders, me_ref, nt_ref, nct_ref, gq_ref, gk_ref, gkc_ref, gv_ref, gvc_ref, w_ref, up_a, up_b, slope_ref, small_ref,
    *rest,
):
    outs, res, gain_ref = rest[:-2], rest[-2], rest[-1]
    pairs = ((gq_ref, None), (gk_ref, gkc_ref), (gv_ref, gvc_ref))
    for which, (tokens, context) in enumerate(pairs):
        for t in range(nt_ref.shape[0] // TILE):
            rows = pl.ds(t * TILE, TILE)
            grad = dot(nt_ref[rows, :], tokens[...])
            if context is not None:
                grad = grad + dot(nct_ref[rows, :], context[...])
            res[rows, :] = grad.astype(BF16)
            dotted = grad * w_ref[which, rows, :].astype(F32)
            total = sum(dotted[:, c : c + HEAD] for c in range(0, dotted.shape[1], HEAD))
            gain_ref[rows, :] = total if which == 0 else gain_ref[rows, :] + total
        size = res.shape[1]
        if which == 1:
            for flow in range(2):
                from_k = slice(flow * size // 2, (flow + 1) * size // 2)
                put_blocks(me_ref[0], orders[flow], res, outs[2 * flow], outs[2 * flow + 1], from_k, slice(size, size + size // 2))
        else:
            flow = which // 2
            put_blocks(me_ref[0], orders[flow], res, outs[2 * flow], outs[2 * flow + 1], slice(None), slice(0, size))
    small_ref[...] = jnp.zeros(small_ref.shape, F32)
    small_ref[0:1, :] = across(gain_ref[...])
    small_ref[1:2, :] = across(up_a[...] + up_b[...])
    lane = lax.broadcasted_iota(jnp.int32, (1, HEAD), 1)
    slopes = jnp.zeros((1, HEAD), F32)
    for h in range(slope_ref.shape[0]):
        slopes = jnp.where(lane == h, jnp.sum(slope_ref[h], axis=1, keepdims=True), slopes)
    small_ref[2:3, :HEAD] = slopes


def qkv_grad_call(me, nt, nct, gq, gk, gkc, gv, gvc, w_qkv, up_a, up_b, slope, n, orders, after=()):
    width = nt.shape[0]
    cols = gq.shape[1]
    piece = (n // 2, width // n, 3 * cols // 2)
    ins = (nt, nct, gq, gk, gkc, gv, gvc, w_qkv, up_a, up_b, slope)
    return call(
        partial(qkv_grad_body, orders),
        [shape((8, width), F32)] + [shape(piece)] * 4,
        [whole(a.shape) for a in ins],
        [whole((8, width))] + [whole(piece)] * 4,
        scratch=[pltpu.VMEM((width, cols), BF16), pltpu.VMEM((width, HEAD), F32)],
        after=after,
    )(me, *ins)


def rows_grad_body(tiles, _, gq_ref, gk_ref, gv_ref, w_ref, send, keep):
    total = dot_nt(gq_ref[...], w_ref[0]) + dot_nt(gk_ref[...], w_ref[1]) + dot_nt(gv_ref[...], w_ref[2])

    @pl.when(pl.program_id(0) < tiles)
    def _():
        send[...] = total.astype(BF16)

    @pl.when(pl.program_id(0) >= tiles)
    def _():
        keep[...] = total.astype(BF16)


def rows_grad_call(me, gq, gk, gv, w_qkv, after=(), size=TILE):
    count, cols = gq.shape
    width = w_qkv.shape[1]
    tiles = count // 2 // size
    tall = pl.BlockSpec((size, cols), lambda i, m: ((i + (1 - m[1]) * tiles) % (2 * tiles), 0))
    return call(
        partial(rows_grad_body, tiles),
        [shape((count // 2, width))] * 2,
        [tall, tall, tall, whole(w_qkv.shape)],
        [
            pl.BlockSpec((size, width), lambda i, _: (jnp.minimum(i, tiles - 1), 0)),
            pl.BlockSpec((size, width), lambda i, _: (jnp.maximum(i - tiles, 0), 0)),
        ],
        grid=(2 * tiles,),
        after=after,
    )(me, gq, gk, gv, w_qkv)


def last_body(_, x_ref, gain_ref, a_ref, b_ref, gmid_ref, out_ref):
    grad = a_ref[...].astype(F32) + b_ref[...].astype(F32)
    back = layer_norm_back(x_ref[...].astype(F32), gain_ref[...], grad)
    out_ref[...] = (gmid_ref[...] + back).astype(BF16)


def last_call(me, x, gain, part, other, gmid, after=()):
    count, width = x.shape
    rows = TILE // 2
    tall = pl.BlockSpec((rows, width), lambda i, _: (i, 0))
    tiles = count // rows
    mine = pl.BlockSpec((rows, width), lambda i, m: (i + m[1] * tiles, 0))
    return call(
        last_body, shape((count, width)), [tall, whole(gain.shape), tall, tall, mine], tall, grid=(tiles,), after=after
    )(me, x, gain, part, other, gmid)


def result_body(_, mid_ref, a_ref, b_ref, out_ref):
    out_ref[...] = (mid_ref[...] + (a_ref[...].astype(F32) + b_ref[...].astype(F32))).astype(BF16)


def result_call(me, mid, part, other, after=()):
    count, width = part.shape
    rows = TILE // 2
    tall = pl.BlockSpec((rows, width), lambda i, _: (i, 0))
    tiles = count // rows
    mine = pl.BlockSpec((rows, width), lambda i, m: (i + m[1] * tiles, 0))
    return call(
        result_body, shape((count, width)), [mine, tall, tall], tall, grid=(tiles,), after=after
    )(me, mid, part, other)


def swap_mp(rows):
    return lax.ppermute(rows, "mp", [(0, 1), (1, 0)])


class Flow:
    def __init__(self, send, keep, order):
        self.send, self.keep, self.order = send, keep, order
        n = lax.axis_size("dp")
        self.got = lax.ppermute(send, "dp", [(i, i ^ (1 << order[0])) for i in range(n)])


def exchange(array, bit):
    return lax.ppermute(array, "dp", [(i, i ^ (1 << bit)) for i in range(lax.axis_size("dp"))])


def add_body(plan, finish, skip, *refs):
    ins, outs = refs[: 2 * sum(plan)], refs[2 * sum(plan) + skip :]
    at = place = 0
    for which, count in enumerate(plan):
        pairs = [(ins[2 * i], ins[2 * i + 1]) for i in range(at, at + count)]
        at += count
        if len(pairs[0][0].shape) == 2:
            outs[-1][...] = pairs[0][0][...] + pairs[0][1][...]
            continue
        if finish is not None:
            finish(which, [keep[0].astype(F32) + got[0].astype(F32) for keep, got in pairs], outs)
            continue
        if len(pairs[0][0].shape) == 3:
            outs[place][...] = pairs[0][0][0].astype(F32) + pairs[0][1][0].astype(F32)
            place += 1
            continue
        col = 0
        place += 2
        for keep, got in pairs:
            to = slice(col, col + keep.shape[3])
            col += keep.shape[3]
            for half, out in ((1, outs[place - 2]), (0, outs[place - 1])):
                out[:, :, to] = (keep[half].astype(F32) + got[half].astype(F32)).astype(BF16)


def advance(groups, after=(), through=(), small=None, finish=None, finals=(), hold=()):
    ins, in_specs, outs, out_specs = [], [], [], []
    last = finish is not None
    steps = 1 if last else max(1, min(group[0].keep.shape[0] for group in groups) // 2)
    for group in groups:
        half = group[0].keep.shape[0] // 2
        size = half // steps
        for flow in group:
            for a in (flow.keep, flow.got):
                _, rows, cols = a.shape
                ins.append(a if half == 0 else a.reshape(2, half, rows, cols))
                in_specs.append(whole(a.shape) if half == 0 else pl.BlockSpec((2, size, rows, cols), lambda i: (0, i, 0, 0)))
        cols = sum(flow.keep.shape[2] for flow in group)
        if half == 0 and not last:
            outs.append(shape((rows, cols), F32))
            out_specs.append(whole((rows, cols)))
        elif not last:
            outs += [shape((half, rows, cols))] * 2
            out_specs += [pl.BlockSpec((size, rows, cols), lambda i: (i, 0, 0))] * 2
    outs += list(finals)
    out_specs += [whole(a.shape) for a in finals]
    plan = [len(group) for group in groups]
    if small is not None:
        ins += list(small)
        in_specs += [whole(small[0].shape)] * 2
        outs.append(shape(small[0].shape, F32))
        out_specs.append(whole(small[0].shape))
        plan.append(1)
    anywhere = pl.BlockSpec(memory_space=pl.ANY)
    results = pl.pallas_call(
        lambda *refs: add_body(plan, finish, len(through) + len(after), *refs[: len(refs) - len(through)]),
        grid=(steps,),
        out_shape=outs + [shape(a.shape, a.dtype) for a in through],
        in_specs=in_specs + [anywhere] * (len(through) + len(after)),
        out_specs=out_specs + [anywhere] * len(through),
        input_output_aliases={len(ins) + i: len(outs) + i for i in range(len(through))},
        compiler_params=pltpu.CompilerParams(vmem_limit_bytes=VMEM_LIMIT),
        cost_estimate=COST,
    )(*ins, *through, *after)
    sums, rest = list(results[: len(outs)]), list(results[len(outs) :])
    tail = [sums.pop()] if small is not None else []
    if not last:
        flat, sums = sums, []
        for i, group in enumerate(groups):
            if group[0].keep.shape[0] == 1:
                sums.append(flat.pop(0))
            elif i in hold:
                sums.append((flat.pop(0), flat.pop(0)))
            else:
                sums.append(Flow(flat.pop(0), flat.pop(0), group[0].order[1:]))
    return sums + tail + rest


def finished(flow):
    return advance([[flow]])[0] if isinstance(flow, Flow) else flow


def ffn_finish_body(first_ref, second_ref, comp_ref, down_ref, up_ref, out_ref):
    cols = out_ref.shape[2]
    for r in range(3):
        out_ref[r] = comp_ref[:, r * cols : (r + 1) * cols].astype(F32)
    size = first_ref.shape[1] // 2
    for which, total_ref in enumerate((first_ref, second_ref)):
        here = slice(which * size, (which + 1) * size)
        down_ref[:, here] = total_ref[:, :size]
        up_ref[:, here] = total_ref[:, size:]


def ffn_finish_call(first, second, comp, after):
    block, hidden = first.shape
    ins = (first, second, comp)
    parts = (3, block, comp.shape[1] // 3)
    return call(
        lambda _, *refs: ffn_finish_body(*refs),
        [shape((block, hidden), F32)] * 2 + [shape(parts, F32)],
        [whole(a.shape) for a in ins],
        [whole((block, hidden))] * 2 + [whole(parts)],
        after=after,
    )(jnp.zeros((1,), jnp.int32), *ins)


def shards(
    inputs, memory, compressed_memory, doc_starts, mem_valid, cmem_valid, gain_attn, w_qkv, slopes, w_out, gain_ffn,
    w_up, w_down, w_comp, out_grad, comp_grad,
):
    n = lax.axis_size("dp")
    bits = n.bit_length() - 1
    rest = list(range(2, bits))
    order_a, order_b, order_o = [0, 1] + rest, [1, 0] + rest, [2, 0, 1] + rest[1:]
    half, width = inputs.shape[1:]
    mem, cmem = memory.shape[1], compressed_memory.shape[1]
    core = lax.axis_index("mp")
    me = jnp.stack([lax.axis_index("dp"), core]).astype(jnp.int32)
    valid = jnp.stack([mem_valid[0], cmem_valid[0]])
    gain1, gain2 = gain_attn[None], gain_ffn[None]

    other_x = swap_mp(inputs[0])
    other_g = swap_mp(out_grad[0])

    compressed, comp = comp_call(me, memory[0], w_comp, comp_grad[0])
    comp_part = lax.psum_scatter(comp, "dp", scatter_dimension=0, tiled=True)

    nct, kc, vc = context_call(me, compressed_memory[0], memory[0], gain1, w_qkv, (compressed,))
    x, nt, q, k, v = tokens_call(me, inputs[0], other_x, gain1, w_qkv, TILE, (other_g,))
    attended, part, out_t, lse = forward_call(
        me, doc_starts, valid, slopes, q, k, v, kc, vc, w_out, cmem, mem
    )
    g, gt = flip_call(me, out_grad[0], other_g, 2 * TILE, (part,))
    mid, n2, n2t = middle_call(me, x, part, swap_mp(part), gain2)

    down1_s, down1_k, up1_s, up1_k, gain_a, *before = ffn_call(
        me, n2, n2t, g, gt, w_up, w_down, (), n, (order_a, order_b)
    )
    flow_a, flow_b = Flow(down1_s, down1_k, order_a), Flow(up1_s, up1_k, order_b)
    down2_s, down2_k, up2_s, up2_k, gain_b, out_send, out_keep, *parts = ffn_call(
        me, n2, n2t, g, gt, w_up, w_down, before, n, (order_a, order_b)
    )
    others = [swap_mp(a) for a in parts]
    flow_a, flow_b, down2_s, up2_s = advance([[flow_a], [flow_b]], (parts[0],), (down2_s, up2_s))
    flow_c, flow_d = Flow(down2_s, down2_k, order_a), Flow(up2_s, up2_k, order_b)
    gmid, gatt, wout_s, wout_k = turn_call(
        me, mid, gain2, g, parts, others, attended, w_out, n, order_o, (flow_a.keep,)
    )
    flow_o = Flow(wout_s, wout_k, order_o)
    gq, gk, gv, gkc, gvc, slope = backward_call(
        me, doc_starts, valid, slopes, q, gatt, out_t, lse, k, v, kc, vc, cmem, mem
    )
    flow_ab, flow_c, flow_d, flow_o = advance([[flow_a, flow_b], [flow_c], [flow_d], [flow_o]], (gq,))
    small, qx_s, qx_k, qy_s, qy_k = qkv_grad_call(
        me, nt, nct, gq, gk, gkc, gv, gvc, w_qkv, gain_a, gain_b, slope, n, (order_a, order_b),
        (flow_c.keep, comp_part),
    )
    flow_ab, flow_cd, held, qx_s, qy_s, small = advance(
        [[flow_ab], [flow_c, flow_d], [flow_o]], (qx_k,), (qx_s, qy_s, small), hold=(2,)
    )
    flow_x, flow_y = Flow(qx_s, qx_k, order_a), Flow(qy_s, qy_k, order_b)
    gain_rows = jnp.arange(small.shape[0])[:, None] < 2
    small = small + jnp.where(gain_rows, swap_mp(small), 0.0)
    got_small = exchange(small, order_a[0])
    rows_send, rows_keep = rows_grad_call(me, gq, gk, gv, w_qkv, (flow_cd.keep,))
    flow_x, flow_y, flow_cd, ab, small, held_send = advance(
        [[flow_x], [flow_y], [flow_cd], [flow_ab]], (rows_keep,), (held[0],), (small, got_small)
    )
    flow_o = Flow(held_send, held[1], order_o[2:])
    got_small = exchange(small, order_a[1])
    flow_x, flow_o, cd, small, rows_send = advance(
        [[flow_x, flow_y], [flow_o], [flow_cd]], (), (rows_send,), (small, got_small)
    )
    got_small = exchange(small, order_a[2])
    while isinstance(cd, Flow):
        ab, cd = finished(ab), finished(cd)
    down_grad, up_grad, comp_grads = ffn_finish_call(ab, cd, comp_part, (flow_x.keep,))
    input_grad = last_call(me, inputs[0], gain1, rows_keep, swap_mp(rows_send), gmid, (up_grad,))
    cols, block = w_out.shape[0], width // n
    flow_x, small, out_send = advance([[flow_x]], (input_grad,), (out_send,), (small, got_small))
    result = result_call(me, mid, out_keep, swap_mp(out_send))
    for bit in order_a[3:-1]:
        flow_x, flow_o, small = advance([[flow_x], [flow_o]], (), (), (small, exchange(small, bit)))
    got_small = exchange(small, order_a[-1])

    def finish_qkv(which, sums, outs):
        total = sums[0]
        if which == 1:
            outs[1][...] = total
            return
        outs[0][0] = total[:, :cols]
        outs[0][1, :, : cols // 2] = total[:, cols : cols + cols // 2]
        outs[0][2] = total[:, cols + cols // 2 : 2 * cols + cols // 2]
        outs[0][1, :, cols // 2 :] = total[:, 2 * cols + cols // 2 :]

    qkv_grad, wout_grad, small = advance(
        [[flow_x], [flow_o]], (result,), (), (small, got_small), finish_qkv,
        [shape((3, block, cols), F32), shape((block, cols), F32)],
    )
    return (
        result[None],
        compressed[None],
        input_grad[None],
        small[0] / gain_attn,
        qkv_grad,
        small[2, : slopes.shape[0]],
        wout_grad.T,
        small[1] / gain_ffn,
        up_grad,
        down_grad.T,
        comp_grads,
    )


def solution(mesh):
    placed = (
        P("dp", "mp", None),
        P("dp", None, None),
        P("dp", None, None),
        P("dp", None),
        P("dp"),
        P("dp"),
        P(),
        P(None, None, "mp"),
        P("mp"),
        P("mp", None),
        P(),
        P(None, "mp"),
        P("mp", None),
        P(None, None, "mp"),
        P("dp", "mp", None),
        P("dp", None, "mp"),
    )
    return jax.shard_map(
        shards,
        mesh=mesh,
        in_specs=placed,
        out_specs=(
            P("dp", "mp", None),
            P("dp", None, "mp"),
            P("dp", "mp", None),
            P(),
            P(None, "dp", "mp"),
            P("mp"),
            P("mp", "dp"),
            P(),
            P("dp", "mp"),
            P("mp", "dp"),
            P(None, "dp", "mp"),
        ),
        check_vma=False,
    )
```

```python
from functools import partial

import jax
import jax.numpy as jnp
from jax import lax
from jax.experimental import pallas as pl
from jax.experimental.pallas import tpu as pltpu
from jax.sharding import PartitionSpec as P

F32, BF16 = jnp.float32, jnp.bfloat16
VMEM_LIMIT = 64 * 1024 * 1024
HEAD = 128
TILE = 256
KEYS = 256
MEM_KEYS = 448
LOG2E = 1.4426950408889634
HIDE = -1e30
COST = pl.CostEstimate(flops=1, bytes_accessed=1, transcendentals=1)


def dot(a, b):
    return jnp.dot(a, b, preferred_element_type=F32)


def dot_nt(a, b):
    return lax.dot_general(a, b, (((1,), (1,)), ((), ())), preferred_element_type=F32)


def shape(dims, kind=BF16):
    return jax.ShapeDtypeStruct(dims, kind)


def whole(dims):
    return pl.BlockSpec(dims, lambda *_: (0,) * len(dims))


def call(body, out_shape, in_specs, out_specs, grid=(1,), scratch=(), scalars=1, after=()):
    ins = scalars + len(in_specs)

    def without(*refs):
        body(*refs[:ins], *refs[ins + len(after) :])

    in_specs = list(in_specs) + [pl.BlockSpec(memory_space=pl.ANY)] * len(after)
    run = pl.pallas_call(
        without,
        grid_spec=pltpu.PrefetchScalarGridSpec(
            num_scalar_prefetch=scalars,
            grid=grid,
            in_specs=in_specs,
            out_specs=out_specs,
            scratch_shapes=scratch,
        ),
        out_shape=out_shape,
        compiler_params=pltpu.CompilerParams(vmem_limit_bytes=VMEM_LIMIT),
        cost_estimate=COST,
    )
    return lambda *args: run(*args, *after)


def put_blocks(me, order, result, send, keep, cols=slice(None), to=slice(None)):
    half, rows = send.shape[0], send.shape[1]
    bits = len(order)
    for place in range(2 * half):
        rel = 0
        for k, bit in enumerate(order):
            rel |= ((place >> (bits - 1 - k)) & 1) << bit
        start = pl.multiple_of((me ^ rel) * rows, rows)
        out = send if place >= half else keep
        out[place % half, :, to] = result[pl.ds(start, rows), cols]


def layer_norm(rows, gain):
    centre = jnp.mean(rows, axis=-1, keepdims=True)
    centred = rows - centre
    spread = jnp.mean(centred * centred, axis=-1, keepdims=True)
    return centred * lax.rsqrt(spread + 1e-05) * gain


def layer_norm_back(rows, gain, grad):
    centre = jnp.mean(rows, axis=-1, keepdims=True)
    centred = rows - centre
    spread = jnp.mean(centred * centred, axis=-1, keepdims=True)
    inverse = lax.rsqrt(spread + 1e-05)
    unit = centred * inverse
    pulled = grad * gain
    return inverse * (
        pulled
        - jnp.mean(pulled, axis=-1, keepdims=True)
        - unit * jnp.mean(pulled * unit, axis=-1, keepdims=True)
    )


def gelu_parts(u):
    bell = jnp.exp2(u * u * (-0.5 * LOG2E))
    t = 1.0 / (1.0 + (0.3275911 * 0.7071067811865476) * jnp.abs(u))
    series = 0.7107068705 + t * (-0.7265760135 + t * 0.5307027145)
    tail = t * (0.127414796 + t * (-0.142248368 + t * series)) * bell
    return jnp.where(u >= 0, 1.0 - tail, tail), u * bell * 0.3989422804014327


def comp_body(_, mem_ref, w_ref, grad_ref, out_ref, wgrad_ref, wide):
    count = out_ref.shape[0]
    groups = mem_ref.shape[1] // HEAD
    for c in range(groups):
        wide[pl.ds(c * 3 * count, 3 * count), :] = mem_ref[:, c * HEAD : (c + 1) * HEAD].astype(F32)
    total = None
    cols = grad_ref.shape[1]
    for r in range(3):
        rows = jnp.concatenate([wide[pl.ds(c * 3 * count + r, count, stride=3), :] for c in range(groups)], axis=1)
        part = dot(rows.astype(BF16), w_ref[r])
        total = part if total is None else total + part
        wgrad_ref[:, r * cols : (r + 1) * cols] = dot(rows.T.astype(BF16), grad_ref[...]).astype(BF16)
    out_ref[...] = total.astype(BF16)


def comp_call(me, memory, w_comp, comp_grad):
    rows, width = memory.shape
    cols = w_comp.shape[2]
    return call(
        comp_body,
        [shape((rows // 3, cols)), shape((width, 3 * cols))],
        [whole(memory.shape), whole(w_comp.shape), whole(comp_grad.shape)],
        [whole((rows // 3, cols)), whole((width, 3 * cols))],
        scratch=[pltpu.VMEM((rows * width // HEAD, HEAD), F32)],
    )(me, memory, w_comp, comp_grad)


def context_body(_, a_ref, b_ref, gain_ref, w_ref, nt_ref, k_ref, v_ref):
    at = 0
    for x_ref in (a_ref, b_ref):
        rows = slice(at, at + x_ref.shape[0])
        at += x_ref.shape[0]
        normed = layer_norm(x_ref[...].astype(F32), gain_ref[...]).astype(BF16)
        nt_ref[:, rows] = normed.T
        k_ref[rows, :] = dot(normed, w_ref[1]).astype(BF16)
        v_ref[rows, :] = dot(normed, w_ref[2]).astype(BF16)


def context_call(me, cmem, mem, gain, w_qkv, after=()):
    width, cols = mem.shape[1], w_qkv.shape[2]
    count = cmem.shape[0] + mem.shape[0]
    ins = (cmem, mem, gain, w_qkv)
    outs = [(width, count), (count, cols), (count, cols)]
    return call(
        context_body,
        [shape(dims) for dims in outs],
        [whole(a.shape) for a in ins],
        [whole(dims) for dims in outs],
        after=after,
    )(me, *ins)


def tokens_body(tiles, me_ref, own_ref, other_ref, gain_ref, w_ref, x_ref, nt_ref, q_ref, k_ref, v_ref):
    mine = pl.program_id(0) // tiles == me_ref[1]
    low_x = jnp.where(mine, own_ref[...], other_ref[...])
    x_ref[...] = low_x
    normed = layer_norm(low_x.astype(F32), gain_ref[...]).astype(BF16)
    nt_ref[...] = normed.T
    q_ref[...] = dot(normed, w_ref[0]).astype(BF16)
    k_ref[...] = dot(normed, w_ref[1]).astype(BF16)
    v_ref[...] = dot(normed, w_ref[2]).astype(BF16)


def tokens_call(me, own, other, gain, w_qkv, tile, after=()):
    half, width = own.shape
    count = 2 * half
    cols = w_qkv.shape[2]
    tiles = half // tile
    side = pl.BlockSpec((tile, width), lambda i, _: (i % tiles, 0))
    tall = pl.BlockSpec((tile, cols), lambda i, _: (i, 0))
    return call(
        partial(tokens_body, tiles),
        [shape((count, width)), shape((width, count)), shape((count, cols))]
        + [shape((count, cols))] * 2,
        [side, side, whole(gain.shape), whole(w_qkv.shape)],
        [
            pl.BlockSpec((tile, width), lambda i, _: (i, 0)),
            pl.BlockSpec((width, tile), lambda i, _: (0, i)),
            tall,
        ]
        + [tall] * 2,
        grid=(count // tile,),
        after=after,
    )(me, own, other, gain, w_qkv)


def flip_body(tiles, me_ref, own_ref, other_ref, x_ref, xt_ref):
    mine = pl.program_id(0) // tiles == me_ref[1]
    low = jnp.where(mine, own_ref[...], other_ref[...])
    x_ref[...] = low
    xt_ref[...] = low.T


def flip_call(me, own, other, tile, after=()):
    half, width = own.shape
    tiles = half // tile
    side = pl.BlockSpec((tile, width), lambda i, _: (i % tiles, 0))
    return call(
        partial(flip_body, tiles),
        [shape((2 * half, width)), shape((width, 2 * half))],
        [side, side],
        [
            pl.BlockSpec((tile, width), lambda i, _: (i, 0)),
            pl.BlockSpec((width, tile), lambda i, _: (0, i)),
        ],
        grid=(2 * tiles,),
        after=after,
    )(me, own, other)


def document_start(places, docs_ref):
    first = jnp.zeros_like(places)
    for d in range(1, docs_ref.shape[1]):
        first = jnp.where(places >= docs_ref[0, d], docs_ref[0, d], first)
    return first


def down(start, count):
    return start + lax.broadcasted_iota(jnp.int32, (count, 1), 0)


def memory_bias(start, count, cmem, mem, valid_ref, slope):
    index = down(start, count)
    compressed = index < cmem
    place = jnp.where(compressed, 3 * index - (mem + 3 * cmem), index - (cmem + mem))
    seen = index >= jnp.where(compressed, cmem - valid_ref[1], cmem + mem - valid_ref[0])
    return jnp.where(seen, place.astype(F32) * slope, HIDE)


def cut(of_memory, start, end, size):
    return [(of_memory, at, min(size, end - at)) for at in range(start, end, size)]


def key_blocks(i, tokens, memory, size, memory_size):
    blocks = cut(True, 0, memory, memory_size) if i * TILE < tokens // 2 else []
    return blocks + cut(False, 0, i * TILE, size) + cut(False, i * TILE, (i + 1) * TILE, size)


def hide(scores, of_memory, start, count, i, places, first, docs_ref):
    if of_memory:
        return jnp.where(places < docs_ref[0, 1], scores, HIDE)
    index = down(start, count)
    visible = index >= first
    if start + count > i * TILE:
        visible = visible & (index <= places)
    return jnp.where(visible, scores, HIDE)


def forward_body(
    cmem, mem, me_ref, docs_ref, valid_ref, slopes_ref, q_ref, k_ref, v_ref, kc_ref, vc_ref, w_ref,
    att_ref, part_ref, ot_ref, lse_ref, vt_ref, vct_ref, score_ref, all_ref,
):
    h = pl.program_id(0)
    tokens = q_ref.shape[0]
    scale = HEAD**-0.5
    power = scale * LOG2E
    slope = slopes_ref[h] / scale
    vt_ref[...] = v_ref[...].T
    vct_ref[...] = vc_ref[...].T
    for i in range(tokens // TILE):
        queries = slice(i * TILE, (i + 1) * TILE)
        places = i * TILE + lax.broadcasted_iota(jnp.int32, (1, TILE), 1)
        first = document_start(places, docs_ref)
        blocks = key_blocks(i, tokens, cmem + mem, KEYS, MEM_KEYS)
        top = jnp.full((8, TILE), HIDE, F32)
        at = 0
        for of_memory, start, count in blocks:
            keys = (kc_ref if of_memory else k_ref)[start : start + count, :]
            if of_memory:
                bias = memory_bias(start, count, cmem, mem, valid_ref, slope)
            else:
                bias = down(start, count).astype(F32) * slope
            scores = hide(dot_nt(keys, q_ref[queries, :]) + bias, of_memory, start, count, i, places, first, docs_ref)
            score_ref[i % 2, at : at + count, :] = scores
            at += count
            top = jnp.maximum(top, jnp.max(scores.reshape(-1, 8, TILE), axis=0))
        top = jnp.max(top, axis=0, keepdims=True)
        total = jnp.zeros((8, TILE), F32)
        out = jnp.zeros((HEAD, TILE), F32)
        at = 0
        for of_memory, start, count in blocks:
            probs = jnp.exp2((score_ref[i % 2, at : at + count, :] - top) * power)
            at += count
            total = total + jnp.sum(probs.reshape(-1, 8, TILE), axis=0)
            out = out + dot((vct_ref if of_memory else vt_ref)[:, start : start + count], probs.astype(BF16))
        total = jnp.sum(total, axis=0, keepdims=True)
        out = out * (1.0 / total)
        ot_ref[:, queries] = out
        low = out.T.astype(BF16)
        att_ref[queries, :] = low
        all_ref[h, queries, :] = low
        lse_ref[0, :, queries] = top * power + jnp.log2(total)

    @pl.when(h == pl.num_programs(0) - 1)
    def _():
        for i in range(tokens // TILE):
            rows = slice(i * TILE, (i + 1) * TILE)
            low = jnp.concatenate([all_ref[g, rows, :] for g in range(all_ref.shape[0])], axis=1)
            part_ref[rows, :] = dot(low, w_ref[...]).astype(BF16)


def forward_call(me, docs, valid, slopes, q, k, v, kc, vc, w_out, cmem, mem, tie=()):
    count, cols = q.shape
    width = w_out.shape[1]
    heads = slopes.shape[0]
    head = pl.BlockSpec((count, HEAD), lambda h, *_: (0, h))
    head_c = pl.BlockSpec((cmem + mem, HEAD), lambda h, *_: (0, h))
    return call(
        partial(forward_body, cmem, mem),
        [shape((count, cols)), shape((count, width)), shape((cols, count), F32), shape((heads, 1, count), F32)],
        [head, head, head, head_c, head_c, whole(w_out.shape)],
        [
            head,
            whole((count, width)),
            pl.BlockSpec((HEAD, count), lambda h, *_: (h, 0)),
            pl.BlockSpec((1, 1, count), lambda h, *_: (h, 0, 0)),
        ],
        grid=(heads,),
        scratch=[
            pltpu.VMEM((HEAD, count), BF16),
            pltpu.VMEM((HEAD, cmem + mem), BF16),
            pltpu.VMEM((2, count + cmem + mem, TILE), F32),
            pltpu.VMEM((heads, count, HEAD), BF16),
        ],
        scalars=4,
    )(me, docs, valid, slopes, q, k, v, kc, vc, w_out)


def backward_body(
    cmem, mem, me_ref, docs_ref, valid_ref, slopes_ref, q_ref, g_ref, ot_ref, lse_ref, k_ref, v_ref, kc_ref, vc_ref,
    gq_ref, gk_ref, gv_ref, gkc_ref, gvc_ref, slope_ref, kt_ref, kct_ref, acck, accv, acckc, accvc,
):
    h = pl.program_id(0)
    tokens = q_ref.shape[0]
    scale = HEAD**-0.5
    power = scale * LOG2E
    slope = slopes_ref[h] * LOG2E
    row = lax.broadcasted_iota(jnp.int32, (8, 1), 0)
    for keys, flipped, memory in ((k_ref, kt_ref, False), (kc_ref, kct_ref, True)):
        flipped[:HEAD, :] = keys[...].T
        index = lax.broadcasted_iota(jnp.int32, (1, keys.shape[0]), 1)
        place = index
        if memory:
            place = jnp.where(index < cmem, 3 * index - (mem + 3 * cmem), index - (cmem + mem))
        high = (place >> 4) << 4
        extra = jnp.where(row == 0, high, jnp.where(row == 1, place - high, jnp.where(row == 2, 1, 0)))
        flipped[HEAD:, :] = jnp.concatenate([extra, jnp.zeros_like(extra)], axis=0).astype(F32).astype(BF16)
    slope_sum = jnp.zeros((1, TILE), F32)
    for i in range(tokens // TILE):
        queries = slice(i * TILE, (i + 1) * TILE)
        places = i * TILE + lax.broadcasted_iota(jnp.int32, (1, TILE), 1)
        first = document_start(places, docs_ref)
        gt = g_ref[queries, :].T
        delta = jnp.sum(gt.astype(F32) * ot_ref[:, queries], axis=0, keepdims=True)
        lse = lse_ref[0, :, queries]
        sum_q = jnp.zeros((HEAD + 16, TILE), F32)
        for of_memory, start, count in key_blocks(i, tokens, cmem + mem, 2 * KEYS, 2 * MEM_KEYS):
            rows = slice(start, start + count)
            keys, values = (kc_ref, vc_ref) if of_memory else (k_ref, v_ref)
            if of_memory:
                bias = memory_bias(start, count, cmem, mem, valid_ref, slope)
            else:
                bias = down(start, count).astype(F32) * slope
            scores = dot_nt(keys[rows, :], q_ref[queries, :]) * power + bias
            scores = hide(scores - lse, of_memory, start, count, i, places, first, docs_ref)
            probs = jnp.exp2(scores)
            grad = (probs * (dot(values[rows, :], gt) - delta)).astype(BF16)
            part_v = dot(probs.astype(BF16), g_ref[queries, :])
            part_k = dot(grad, q_ref[queries, :])
            sum_k, sum_v = (acckc, accvc) if of_memory else (acck, accv)
            fresh = i == 0 if of_memory else start >= i * TILE
            sum_v[rows, :] = part_v if fresh else sum_v[rows, :] + part_v
            sum_k[rows, :] = part_k if fresh else sum_k[rows, :] + part_k
            sum_q = sum_q + dot((kct_ref if of_memory else kt_ref)[:, rows], grad)
        gq_ref[queries, :] = (sum_q[:HEAD] * scale).T.astype(BF16)
        far = places.astype(F32) * sum_q[HEAD + 2 : HEAD + 3] - sum_q[HEAD : HEAD + 1] - sum_q[HEAD + 1 : HEAD + 2]
        slope_sum = slope_sum - far
    slope_ref[0] = slope_sum
    gk_ref[...] = (acck[...] * scale).astype(BF16)
    gkc_ref[...] = (acckc[...] * scale).astype(BF16)
    gv_ref[...] = accv[...].astype(BF16)
    gvc_ref[...] = accvc[...].astype(BF16)


def backward_call(me, docs, valid, slopes, q, g, ot, lse, k, v, kc, vc, cmem, mem, after=()):
    count, cols = q.shape
    heads = slopes.shape[0]
    head = pl.BlockSpec((count, HEAD), lambda h, *_: (0, h))
    head_c = pl.BlockSpec((cmem + mem, HEAD), lambda h, *_: (0, h))
    return call(
        partial(backward_body, cmem, mem),
        [shape((count, cols))] * 3 + [shape(kc.shape)] * 2 + [shape((heads, 1, TILE), F32)],
        [
            head,
            head,
            pl.BlockSpec((HEAD, count), lambda h, *_: (h, 0)),
            pl.BlockSpec((1, 1, count), lambda h, *_: (h, 0, 0)),
            head,
            head,
            head_c,
            head_c,
        ],
        [head] * 3 + [head_c] * 2 + [pl.BlockSpec((1, 1, TILE), lambda h, *_: (h, 0, 0))],
        grid=(heads,),
        scratch=[pltpu.VMEM((HEAD + 16, count), BF16), pltpu.VMEM((HEAD + 16, cmem + mem), BF16)]
        + [pltpu.VMEM((count, HEAD), F32)] * 2
        + [pltpu.VMEM((cmem + mem, HEAD), F32)] * 2,
        scalars=4,
        after=after,
    )(me, docs, valid, slopes, q, g, ot, lse, k, v, kc, vc)


def middle_body(_, x_ref, a_ref, b_ref, gain_ref, mid_ref, n_ref, nt_ref):
    mid = x_ref[...].astype(F32) + (a_ref[...].astype(F32) + b_ref[...].astype(F32))
    mid_ref[...] = mid
    normed = layer_norm(mid, gain_ref[...]).astype(BF16)
    n_ref[...] = normed
    nt_ref[...] = normed.T


def middle_call(me, x, part, other, gain, rows=512):
    count, width = x.shape
    tall = pl.BlockSpec((rows, width), lambda i, _: (i, 0))
    return call(
        middle_body,
        [shape((count, width), F32), shape((count, width)), shape((width, count))],
        [tall, tall, tall, whole(gain.shape)],
        [tall, tall, pl.BlockSpec((width, rows), lambda i, _: (0, i))],
        grid=(count // rows,),
    )(me, x, part, other, gain)


class Copies:
    def __init__(self, sems):
        self.sems, self.count, self.open = sems, 0, []

    def start(self, source, target):
        copy = pltpu.make_async_copy(source, target, self.sems.at[self.count])
        self.count += 1
        copy.start()
        self.open.append(copy)
        return copy

    def finish(self):
        for copy in self.open:
            copy.wait()
        self.open = []


def ship(copies, me, order, result, outs, cols):
    send, keep = outs
    half, rows, width = send.shape
    bits = len(order)
    to = slice(cols.start % width, cols.start % width + cols.stop - cols.start)
    for place in range(2 * half):
        rel = 0
        for k, bit in enumerate(order):
            rel |= ((place >> (bits - 1 - k)) & 1) << bit
        start = pl.multiple_of((me ^ rel) * rows, rows)
        out = send if place >= half else keep
        copies.start(result.at[pl.ds(start, rows), cols], out.at[place % half, :, to])


def ffn_body(orders, second, step, me_ref, *refs):
    if second:
        n_in, nt_in, g_in, gt_in, up_in, down_in, hid_in, gpre_in, *refs = refs
        down_outs, up_outs, refs = refs[:2], refs[2 : 2 * len(orders)], refs[2 * len(orders) :]
        gain_out, out_send, out_keep, *refs = refs
        rows_out, refs = refs[: len(refs) - 15], refs[len(refs) - 15 :]
        n, nt, g, gt, up, down, hid, gpre, res_down, res_up, gain, rows, part, in_sems, out_sems = refs
    else:
        n_in, nt_in, g_in, gt_in, up_in, down_in, *refs = refs
        down_outs, up_outs, refs = refs[:2], refs[2 : 2 * len(orders)], refs[2 * len(orders) :]
        gain_out, hid_out, gpre_out, *refs = refs
        n, nt, g, gt, up, down, hid, gpre, res_down, res_up, gain, in_sems, out_sems = refs
    tokens, width = n.shape
    size = res_down.shape[1]
    base = size if second else 0
    ins, outs = Copies(in_sems), Copies(out_sems)
    mine = slice(base, base + size)
    waits = {}
    for name, source, target in (
        ("n", n_in, n),
        ("up", up_in.at[:, mine], up.at[:, mine]),
        ("g", g_in, g),
        ("down", down_in.at[mine, :], down.at[mine, :]),
        ("gt", gt_in, gt),
        ("nt", nt_in, nt),
    ):
        waits[name] = ins.start(source, target)
    if second:
        for name, source, target in (
            ("gpre", gpre_in, gpre.at[:, :size]),
            ("up2", up_in.at[:, :size], up.at[:, :size]),
            ("hid", hid_in, hid.at[:, :size]),
            ("down2", down_in.at[:size, :], down.at[:size, :]),
        ):
            waits[name] = ins.start(source, target)
    for at in range(base, base + size, step):
        cols = slice(at, at + step)
        local = slice(at - base, at - base + step)
        for i in range(tokens // TILE):
            part_rows = slice(i * TILE, (i + 1) * TILE)
            if at == base and i == 0:
                waits["n"].wait()
                waits["up"].wait()
            pre = dot(n[part_rows, :], up[:, cols])
            if at == base and i == 0:
                waits["g"].wait()
                waits["down"].wait()
            back = dot_nt(g[part_rows, :], down[cols, :])
            cdf, bell = gelu_parts(pre)
            hid[part_rows, cols] = (pre * cdf).astype(BF16)
            gpre[part_rows, cols] = (back * (cdf + bell)).astype(BF16)
        if not second:
            outs.start(hid.at[:, cols], hid_out.at[:, cols])
            outs.start(gpre.at[:, cols], gpre_out.at[:, cols])
        if at == base:
            waits["gt"].wait()
        for i in range(width // TILE):
            part_rows = slice(i * TILE, (i + 1) * TILE)
            res_down[part_rows, local] = dot(gt[part_rows, :], hid[:, cols]).astype(BF16)
        ship(outs, me_ref[0], orders[0], res_down, down_outs, local)
        if at == base:
            waits["nt"].wait()
        for i in range(width // TILE):
            part_rows = slice(i * TILE, (i + 1) * TILE)
            grad = dot(nt[part_rows, :], gpre[:, cols])
            res_up[part_rows, local] = grad.astype(BF16)
            dotted = grad * up[part_rows, cols].astype(F32)
            total = sum(dotted[:, c : c + HEAD] for c in range(0, step, HEAD))
            gain[part_rows, :] = total if at == base else gain[part_rows, :] + total
        which = 2 * ((at - base) * (len(orders) - 1) // size)
        ship(outs, me_ref[0], orders[1 + which // 2], res_up, up_outs[which : which + 2], local)
    outs.start(gain, gain_out)
    if second:
        waits["gpre"].wait()
        waits["up2"].wait()
        for t in range(width // TILE):
            cols = slice(t * TILE, (t + 1) * TILE)
            rows[:, cols] = dot_nt(gpre[...], up[cols, :]).astype(BF16)
        chunk = tokens // len(rows_out)
        for i, target in enumerate(rows_out):
            outs.start(rows.at[i * chunk : (i + 1) * chunk, :], target)
        waits["hid"].wait()
        waits["down2"].wait()
        half = tokens // 2
        for t in range(width // TILE):
            cols = slice(t * TILE, (t + 1) * TILE)
            part[:, cols] = dot(hid[...], down[:, cols]).astype(BF16)
        for core, target in ((1 - me_ref[1], out_send), (me_ref[1], out_keep)):
            outs.start(part.at[pl.ds(pl.multiple_of(core * half, half), half), :], target)
    outs.finish()


def ffn_call(me, n2, n2t, g, gt, w_up, w_down, before, n, orders, step=1024, after=()):
    tokens, width = n2.shape
    hidden = w_up.shape[1]
    size = hidden // 2
    second = len(before) > 0
    anywhere = pl.BlockSpec(memory_space=pl.ANY)
    ups = len(orders) - 1
    outs = [shape((n // 2, width // n, size))] * 2 + [shape((n // 2, width // n, size // ups))] * (2 * ups)
    outs += [shape((width, HEAD), F32)]
    scratch = [pltpu.VMEM(a.shape, BF16) for a in (n2, n2t, g, gt, w_up, w_down)]
    scratch += [pltpu.VMEM((tokens, hidden), BF16)] * 2 + [pltpu.VMEM((width, size), BF16)] * 2
    scratch += [pltpu.VMEM((width, HEAD), F32)]
    copies = 2 * n * (size // step) + 1
    if second:
        outs += [shape((tokens // 2, width))] * 2 + [shape((tokens // 2, width))] * 2
        scratch += [pltpu.VMEM((tokens, width), BF16)] * 2
        copies += 4
    else:
        outs += [shape((tokens, size))] * 2
        copies += 2 * (size // step)
    scratch += [pltpu.SemaphoreType.DMA((10,)), pltpu.SemaphoreType.DMA((copies,))]
    ins = 7 + len(before)

    def body(*refs):
        ffn_body(orders, second, step, *refs[:ins], *refs[ins + len(after) :])

    return pl.pallas_call(
        body,
        out_shape=outs,
        in_specs=[pl.BlockSpec(memory_space=pltpu.SMEM)] + [anywhere] * (ins - 1 + len(after)),
        out_specs=[anywhere] * len(outs),
        scratch_shapes=scratch,
        compiler_params=pltpu.CompilerParams(vmem_limit_bytes=VMEM_LIMIT),
        cost_estimate=COST,
    )(me, n2, n2t, g, gt, w_up, w_down, *before, *after)


def turn_body(
    order, me_ref, mid_ref, gain_ref, g_ref, att_ref, w_ref, a_ref, b_ref, c_ref, d_ref, gmid_ref, gatt_ref, send, keep, low_t, res
):
    i = pl.program_id(0)
    early = i < pl.num_programs(0) // 2
    own, other = jnp.where(early, a_ref[...], b_ref[...]), jnp.where(early, c_ref[...], d_ref[...])
    grad = own.astype(F32) + other.astype(F32)
    total = g_ref[...].astype(F32) + layer_norm_back(mid_ref[...], gain_ref[...], grad)
    gmid_ref[...] = total
    low = total.astype(BF16)
    gatt_ref[...] = dot_nt(low, w_ref[...]).astype(BF16)
    low_t[:, pl.ds(pl.multiple_of(i * TILE, TILE), TILE)] = low.T

    @pl.when(i == pl.num_programs(0) - 1)
    def _():
        for t in range(low_t.shape[0] // TILE):
            rows = pl.ds(t * TILE, TILE)
            res[rows, :] = dot(low_t[rows, :], att_ref[...]).astype(BF16)
        put_blocks(me_ref[0], order, res, send, keep)


def turn_call(me, mid, gain, g, parts, others, attended, w_out, n, order, after=()):
    count, width = mid.shape
    cols = attended.shape[1]
    tall = pl.BlockSpec((TILE, width), lambda i, _: (i, 0))
    tiles = count // 2 // TILE
    early = pl.BlockSpec((TILE, width), lambda i, _: (jnp.minimum(i, tiles - 1), 0))
    late = pl.BlockSpec((TILE, width), lambda i, _: (jnp.maximum(i - tiles, 0), 0))
    piece = (n // 2, width // n, cols)
    return call(
        partial(turn_body, order),
        [shape((count, width), F32), shape((count, cols)), shape(piece), shape(piece)],
        [tall, whole(gain.shape), tall, whole(attended.shape), whole(w_out.shape), early, late, early, late],
        [tall, pl.BlockSpec((TILE, cols), lambda i, _: (i, 0)), whole(piece), whole(piece)],
        grid=(count // TILE,),
        scratch=[pltpu.VMEM((width, count), BF16), pltpu.VMEM((width, cols), BF16)],
        after=after,
    )(me, mid, gain, g, attended, w_out, *parts, *others)


def across(sums):
    return jnp.sum(sums.T, axis=0, keepdims=True)


def qkv_grad_body(
    orders, me_ref, nt_ref, nct_ref, gq_ref, gk_ref, gkc_ref, gv_ref, gvc_ref, w_ref, up_a, up_b, slope_ref, small_ref,
    *rest,
):
    outs, res, gain_ref = rest[:-2], rest[-2], rest[-1]
    pairs = ((gq_ref, None), (gk_ref, gkc_ref), (gv_ref, gvc_ref))
    for which, (tokens, context) in enumerate(pairs):
        for t in range(nt_ref.shape[0] // TILE):
            rows = pl.ds(t * TILE, TILE)
            grad = dot(nt_ref[rows, :], tokens[...])
            if context is not None:
                grad = grad + dot(nct_ref[rows, :], context[...])
            res[rows, :] = grad.astype(BF16)
            dotted = grad * w_ref[which, rows, :].astype(F32)
            total = sum(dotted[:, c : c + HEAD] for c in range(0, dotted.shape[1], HEAD))
            gain_ref[rows, :] = total if which == 0 else gain_ref[rows, :] + total
        size = res.shape[1]
        if which == 1:
            for flow in range(2):
                from_k = slice(flow * size // 2, (flow + 1) * size // 2)
                put_blocks(me_ref[0], orders[flow], res, outs[2 * flow], outs[2 * flow + 1], from_k, slice(size, size + size // 2))
        else:
            flow = which // 2
            put_blocks(me_ref[0], orders[flow], res, outs[2 * flow], outs[2 * flow + 1], slice(None), slice(0, size))
    small_ref[...] = jnp.zeros(small_ref.shape, F32)
    small_ref[0:1, :] = across(gain_ref[...])
    small_ref[1:2, :] = across(up_a[...] + up_b[...])
    lane = lax.broadcasted_iota(jnp.int32, (1, HEAD), 1)
    slopes = jnp.zeros((1, HEAD), F32)
    for h in range(slope_ref.shape[0]):
        slopes = jnp.where(lane == h, jnp.sum(slope_ref[h], axis=1, keepdims=True), slopes)
    small_ref[2:3, :HEAD] = slopes


def qkv_grad_call(me, nt, nct, gq, gk, gkc, gv, gvc, w_qkv, up_a, up_b, slope, n, orders, after=()):
    width = nt.shape[0]
    cols = gq.shape[1]
    piece = (n // 2, width // n, 3 * cols // 2)
    ins = (nt, nct, gq, gk, gkc, gv, gvc, w_qkv, up_a, up_b, slope)
    return call(
        partial(qkv_grad_body, orders),
        [shape((8, width), F32)] + [shape(piece)] * 4,
        [whole(a.shape) for a in ins],
        [whole((8, width))] + [whole(piece)] * 4,
        scratch=[pltpu.VMEM((width, cols), BF16), pltpu.VMEM((width, HEAD), F32)],
        after=after,
    )(me, *ins)


def rows_grad_body(tiles, _, gq_ref, gk_ref, gv_ref, w_ref, send, keep):
    total = dot_nt(gq_ref[...], w_ref[0]) + dot_nt(gk_ref[...], w_ref[1]) + dot_nt(gv_ref[...], w_ref[2])

    @pl.when(pl.program_id(0) < tiles)
    def _():
        send[...] = total.astype(BF16)

    @pl.when(pl.program_id(0) >= tiles)
    def _():
        keep[...] = total.astype(BF16)


def rows_grad_call(me, gq, gk, gv, w_qkv, after=(), size=TILE):
    count, cols = gq.shape
    width = w_qkv.shape[1]
    tiles = count // 2 // size
    tall = pl.BlockSpec((size, cols), lambda i, m: ((i + (1 - m[1]) * tiles) % (2 * tiles), 0))
    return call(
        partial(rows_grad_body, tiles),
        [shape((count // 2, width))] * 2,
        [tall, tall, tall, whole(w_qkv.shape)],
        [
            pl.BlockSpec((size, width), lambda i, _: (jnp.minimum(i, tiles - 1), 0)),
            pl.BlockSpec((size, width), lambda i, _: (jnp.maximum(i - tiles, 0), 0)),
        ],
        grid=(2 * tiles,),
        after=after,
    )(me, gq, gk, gv, w_qkv)


def last_body(_, x_ref, gain_ref, a_ref, b_ref, gmid_ref, out_ref):
    grad = a_ref[...].astype(F32) + b_ref[...].astype(F32)
    back = layer_norm_back(x_ref[...].astype(F32), gain_ref[...], grad)
    out_ref[...] = (gmid_ref[...] + back).astype(BF16)


def last_call(me, x, gain, part, other, gmid, after=()):
    count, width = x.shape
    rows = TILE
    tall = pl.BlockSpec((rows, width), lambda i, _: (i, 0))
    tiles = count // rows
    mine = pl.BlockSpec((rows, width), lambda i, m: (i + m[1] * tiles, 0))
    return call(
        last_body, shape((count, width)), [tall, whole(gain.shape), tall, tall, mine], tall, grid=(tiles,), after=after
    )(me, x, gain, part, other, gmid)


def result_body(_, mid_ref, a_ref, b_ref, out_ref):
    out_ref[...] = (mid_ref[...] + (a_ref[...].astype(F32) + b_ref[...].astype(F32))).astype(BF16)


def result_call(me, mid, part, other, after=()):
    count, width = part.shape
    rows = TILE
    tall = pl.BlockSpec((rows, width), lambda i, _: (i, 0))
    tiles = count // rows
    mine = pl.BlockSpec((rows, width), lambda i, m: (i + m[1] * tiles, 0))
    return call(
        result_body, shape((count, width)), [mine, tall, tall], tall, grid=(tiles,), after=after
    )(me, mid, part, other)


def swap_mp(rows):
    return lax.ppermute(rows, "mp", [(0, 1), (1, 0)])


class Flow:
    def __init__(self, send, keep, order):
        self.send, self.keep, self.order = send, keep, order
        n = lax.axis_size("dp")
        self.got = lax.ppermute(send, "dp", [(i, i ^ (1 << order[0])) for i in range(n)])


def exchange(array, bit):
    return lax.ppermute(array, "dp", [(i, i ^ (1 << bit)) for i in range(lax.axis_size("dp"))])


def add_body(plan, finish, skip, *refs):
    ins, outs = refs[: 2 * sum(plan)], refs[2 * sum(plan) + skip :]
    at = place = 0
    for which, count in enumerate(plan):
        pairs = [(ins[2 * i], ins[2 * i + 1]) for i in range(at, at + count)]
        at += count
        if len(pairs[0][0].shape) == 2:
            outs[-1][...] = pairs[0][0][...] + pairs[0][1][...]
            continue
        if finish is not None:
            finish(which, [keep[0].astype(F32) + got[0].astype(F32) for keep, got in pairs], outs)
            continue
        if len(pairs[0][0].shape) == 3:
            outs[place][...] = pairs[0][0][0].astype(F32) + pairs[0][1][0].astype(F32)
            place += 1
            continue
        col = 0
        place += 2
        for keep, got in pairs:
            to = slice(col, col + keep.shape[3])
            col += keep.shape[3]
            for half, out in ((1, outs[place - 2]), (0, outs[place - 1])):
                out[:, :, to] = (keep[half].astype(F32) + got[half].astype(F32)).astype(BF16)


def advance(groups, after=(), through=(), small=None, finish=None, finals=(), hold=()):
    ins, in_specs, outs, out_specs = [], [], [], []
    last = finish is not None
    steps = 1 if last else max(1, min(group[0].keep.shape[0] for group in groups) // 2)
    for group in groups:
        half = group[0].keep.shape[0] // 2
        size = half // steps
        for flow in group:
            for a in (flow.keep, flow.got):
                _, rows, cols = a.shape
                ins.append(a if half == 0 else a.reshape(2, half, rows, cols))
                in_specs.append(whole(a.shape) if half == 0 else pl.BlockSpec((2, size, rows, cols), lambda i: (0, i, 0, 0)))
        cols = sum(flow.keep.shape[2] for flow in group)
        if half == 0 and not last:
            outs.append(shape((rows, cols), F32))
            out_specs.append(whole((rows, cols)))
        elif not last:
            outs += [shape((half, rows, cols))] * 2
            out_specs += [pl.BlockSpec((size, rows, cols), lambda i: (i, 0, 0))] * 2
    outs += list(finals)
    out_specs += [whole(a.shape) for a in finals]
    plan = [len(group) for group in groups]
    if small is not None:
        ins += list(small)
        in_specs += [whole(small[0].shape)] * 2
        outs.append(shape(small[0].shape, F32))
        out_specs.append(whole(small[0].shape))
        plan.append(1)
    anywhere = pl.BlockSpec(memory_space=pl.ANY)
    results = pl.pallas_call(
        lambda *refs: add_body(plan, finish, len(through) + len(after), *refs[: len(refs) - len(through)]),
        grid=(steps,),
        out_shape=outs + [shape(a.shape, a.dtype) for a in through],
        in_specs=in_specs + [anywhere] * (len(through) + len(after)),
        out_specs=out_specs + [anywhere] * len(through),
        input_output_aliases={len(ins) + i: len(outs) + i for i in range(len(through))},
        compiler_params=pltpu.CompilerParams(vmem_limit_bytes=VMEM_LIMIT),
        cost_estimate=COST,
    )(*ins, *through, *after)
    sums, rest = list(results[: len(outs)]), list(results[len(outs) :])
    tail = [sums.pop()] if small is not None else []
    if not last:
        flat, sums = sums, []
        for i, group in enumerate(groups):
            if group[0].keep.shape[0] == 1:
                sums.append(flat.pop(0))
            elif i in hold:
                sums.append((flat.pop(0), flat.pop(0)))
            else:
                sums.append(Flow(flat.pop(0), flat.pop(0), group[0].order[1:]))
    return sums + tail + rest


def finished(flow):
    return advance([[flow]])[0] if isinstance(flow, Flow) else flow


def ffn_finish_body(first_ref, second_ref, comp_ref, down_ref, up_ref, out_ref):
    cols = out_ref.shape[2]
    for r in range(3):
        out_ref[r] = comp_ref[:, r * cols : (r + 1) * cols].astype(F32)
    size = first_ref.shape[1] // 2
    for which, total_ref in enumerate((first_ref, second_ref)):
        here = slice(which * size, (which + 1) * size)
        down_ref[:, here] = total_ref[:, :size]
        up_ref[:, here] = total_ref[:, size:]


def ffn_finish_call(first, second, comp, after):
    block, hidden = first.shape
    ins = (first, second, comp)
    parts = (3, block, comp.shape[1] // 3)
    return call(
        lambda _, *refs: ffn_finish_body(*refs),
        [shape((block, hidden), F32)] * 2 + [shape(parts, F32)],
        [whole(a.shape) for a in ins],
        [whole((block, hidden))] * 2 + [whole(parts)],
        after=after,
    )(jnp.zeros((1,), jnp.int32), *ins)


def shards(
    inputs, memory, compressed_memory, doc_starts, mem_valid, cmem_valid, gain_attn, w_qkv, slopes, w_out, gain_ffn,
    w_up, w_down, w_comp, out_grad, comp_grad,
):
    n = lax.axis_size("dp")
    bits = n.bit_length() - 1
    rest = list(range(2, bits))
    order_a, order_b, order_o = [0, 1] + rest, [1, 0] + rest, [2, 0, 1] + rest[1:]
    half, width = inputs.shape[1:]
    mem, cmem = memory.shape[1], compressed_memory.shape[1]
    core = lax.axis_index("mp")
    me = jnp.stack([lax.axis_index("dp"), core]).astype(jnp.int32)
    valid = jnp.stack([mem_valid[0], cmem_valid[0]])
    gain1, gain2 = gain_attn[None], gain_ffn[None]

    other_x = swap_mp(inputs[0])
    other_g = swap_mp(out_grad[0])

    compressed, comp = comp_call(me, memory[0], w_comp, comp_grad[0])
    comp_part = lax.psum_scatter(comp, "dp", scatter_dimension=0, tiled=True)

    nct, kc, vc = context_call(me, compressed_memory[0], memory[0], gain1, w_qkv, (compressed,))
    x, nt, q, k, v = tokens_call(me, inputs[0], other_x, gain1, w_qkv, TILE, (other_g,))
    attended, part, out_t, lse = forward_call(
        me, doc_starts, valid, slopes, q, k, v, kc, vc, w_out, cmem, mem
    )
    g, gt = flip_call(me, out_grad[0], other_g, 2 * TILE, (part,))
    mid, n2, n2t = middle_call(me, x, part, swap_mp(part), gain2)

    down1_s, down1_k, up1_s, up1_k, gain_a, *before = ffn_call(
        me, n2, n2t, g, gt, w_up, w_down, (), n, (order_a, order_b)
    )
    flow_a, flow_b = Flow(down1_s, down1_k, order_a), Flow(up1_s, up1_k, order_b)
    down2_s, down2_k, up2_s, up2_k, gain_b, out_send, out_keep, *parts = ffn_call(
        me, n2, n2t, g, gt, w_up, w_down, before, n, (order_a, order_b)
    )
    others = [swap_mp(a) for a in parts]
    flow_a, flow_b, down2_s, up2_s = advance([[flow_a], [flow_b]], (parts[0],), (down2_s, up2_s))
    flow_c, flow_d = Flow(down2_s, down2_k, order_a), Flow(up2_s, up2_k, order_b)
    gmid, gatt, wout_s, wout_k = turn_call(
        me, mid, gain2, g, parts, others, attended, w_out, n, order_o, (flow_a.keep,)
    )
    flow_o = Flow(wout_s, wout_k, order_o)
    gq, gk, gv, gkc, gvc, slope = backward_call(
        me, doc_starts, valid, slopes, q, gatt, out_t, lse, k, v, kc, vc, cmem, mem
    )
    flow_ab, flow_c, flow_d, flow_o = advance([[flow_a, flow_b], [flow_c], [flow_d], [flow_o]], (gq,))
    small, qx_s, qx_k, qy_s, qy_k = qkv_grad_call(
        me, nt, nct, gq, gk, gkc, gv, gvc, w_qkv, gain_a, gain_b, slope, n, (order_a, order_b),
        (flow_c.keep, comp_part),
    )
    flow_ab, flow_cd, held, qx_s, qy_s, small = advance(
        [[flow_ab], [flow_c, flow_d], [flow_o]], (qx_k,), (qx_s, qy_s, small), hold=(2,)
    )
    flow_x, flow_y = Flow(qx_s, qx_k, order_a), Flow(qy_s, qy_k, order_b)
    gain_rows = jnp.arange(small.shape[0])[:, None] < 2
    small = small + jnp.where(gain_rows, swap_mp(small), 0.0)
    got_small = exchange(small, order_a[0])
    rows_send, rows_keep = rows_grad_call(me, gq, gk, gv, w_qkv, (flow_cd.keep,))
    flow_x, flow_y, flow_cd, ab, small, held_send = advance(
        [[flow_x], [flow_y], [flow_cd], [flow_ab]], (rows_keep,), (held[0],), (small, got_small)
    )
    flow_o = Flow(held_send, held[1], order_o[2:])
    got_small = exchange(small, order_a[1])
    flow_x, flow_o, cd, small, rows_send = advance(
        [[flow_x, flow_y], [flow_o], [flow_cd]], (), (rows_send,), (small, got_small)
    )
    got_small = exchange(small, order_a[2])
    while isinstance(cd, Flow):
        ab, cd = finished(ab), finished(cd)
    down_grad, up_grad, comp_grads = ffn_finish_call(ab, cd, comp_part, (flow_x.keep,))
    input_grad = last_call(me, inputs[0], gain1, rows_keep, swap_mp(rows_send), gmid, (up_grad,))
    cols, block = w_out.shape[0], width // n
    flow_x, small, out_send = advance([[flow_x]], (input_grad,), (out_send,), (small, got_small))
    result = result_call(me, mid, out_keep, swap_mp(out_send))
    for bit in order_a[3:-1]:
        flow_x, flow_o, small = advance([[flow_x], [flow_o]], (), (), (small, exchange(small, bit)))
    got_small = exchange(small, order_a[-1])

    def finish_qkv(which, sums, outs):
        total = sums[0]
        if which == 1:
            outs[1][...] = total
            return
        outs[0][0] = total[:, :cols]
        outs[0][1, :, : cols // 2] = total[:, cols : cols + cols // 2]
        outs[0][2] = total[:, cols + cols // 2 : 2 * cols + cols // 2]
        outs[0][1, :, cols // 2 :] = total[:, 2 * cols + cols // 2 :]

    qkv_grad, wout_grad, small = advance(
        [[flow_x], [flow_o]], (result,), (), (small, got_small), finish_qkv,
        [shape((3, block, cols), F32), shape((block, cols), F32)],
    )
    return (
        result[None],
        compressed[None],
        input_grad[None],
        small[0] / gain_attn,
        qkv_grad,
        small[2, : slopes.shape[0]],
        wout_grad.T,
        small[1] / gain_ffn,
        up_grad,
        down_grad.T,
        comp_grads,
    )


def solution(mesh):
    placed = (
        P("dp", "mp", None),
        P("dp", None, None),
        P("dp", None, None),
        P("dp", None),
        P("dp"),
        P("dp"),
        P(),
        P(None, None, "mp"),
        P("mp"),
        P("mp", None),
        P(),
        P(None, "mp"),
        P("mp", None),
        P(None, None, "mp"),
        P("dp", "mp", None),
        P("dp", None, "mp"),
    )
    return jax.shard_map(
        shards,
        mesh=mesh,
        in_specs=placed,
        out_specs=(
            P("dp", "mp", None),
            P("dp", None, "mp"),
            P("dp", "mp", None),
            P(),
            P(None, "dp", "mp"),
            P("mp"),
            P("mp", "dp"),
            P(),
            P("dp", "mp"),
            P("mp", "dp"),
            P(None, "dp", "mp"),
        ),
        check_vma=False,
    )
```
